512 devices in a mesh: ctx: 64 (over z_hi, y, x, core), tp: 8 (over z_lo).
Axes of the slice: x: 4, y: 4, z: 16 (z_hi: 2, z_lo: 8; z = z_hi * 8 + z_lo), core: 2. Of those that a mesh axis runs over, the one named last changes fastest.
Arguments:
- tokens_in: bfloat16 [16384, 4096], P('ctx'), may hold values from -6 to 6
- pre_gain: bfloat16 [4096], replicated, may hold values from 0.099609375 to 1.8984375
- w_in: bfloat16 [4096, 3, 2048], P('ctx', None, 'tp'), may hold values from -0.09375 to 0.09375
- w_out: bfloat16 [2048, 4096], P('ctx', 'tp'), may hold values from -0.5 to 0.5
- long_filter: bfloat16 [16384, 2048], P('ctx', 'tp'), may hold values from -0.046875 to 0.046875
- w_unembed: bfloat16 [4096, 512], P('tp'), may hold values from -0.1875 to 0.1875
- target_ids: int32 [16384], P('ctx'), may hold values from 0 to 511
- score_mask: int32 [16384], P('ctx'), may hold values 0 or 1
Outputs:
- token_logprob: float32 [16384], P('ctx')
The draws below stay inside these ranges and needn't reach their ends.
All inputs are finite; a program needn't handle non-finite values. No bound on the sum of `score_mask` on one device may be relied on, other than what follows from the above.
Results may differ from the reference program's by a relative error of at most 0.0045.
Values may be sent and summed in bfloat16 or wider, within the bound.
No kernel may reach another device: no remote copies, remote signals or barrier semaphores. Data moves between devices by JAX's collectives and lax.ppermute only.
A program may use at most 64 MiB of HBM per device.

```python
import math
import jax
import jax.numpy as jnp
import numpy as np
from jax import lax

D = 4096
CH = 2048
VOCAB = 512
TOKENS = 16384


def shared_plan(key):
    key = jax.random.fold_in(key, 101)
    sign_key, col_key, off_key = jax.random.split(key, 3)
    signs = jnp.where(jax.random.bernoulli(sign_key, 0.5, (D,)), 1.0, -1.0).astype(jnp.float32)
    first_col = jax.random.randint(col_key, (), 0, VOCAB)
    second_col = (first_col + 1 + jax.random.randint(off_key, (), 0, VOCAB - 1)) % VOCAB
    return (signs, first_col, second_col)


def draw_tokens_in(key, part):
    signs, first_col, second_col = shared_plan(key)
    key = jax.random.fold_in(key, 3)
    noise_key, pick_key, extra_key, level_key = jax.random.split(key, 4)
    background = jnp.clip(jax.random.normal(noise_key, (TOKENS, D), jnp.float32), -6.0, 6.0)
    row_index = jnp.arange(TOKENS)[:, None]
    extra_rows = jax.random.randint(extra_key, (1, 3), 0, TOKENS)
    chosen = (jax.random.randint(pick_key, (TOKENS, 1), 0, 32) == 0) | jnp.any(row_index == extra_rows, axis=1, keepdims=True)
    levels = jnp.array([0.6, 1.0, 1.4], jnp.float32)
    level = levels[jax.random.randint(level_key, (TOKENS, 1), 0, 3)]
    amplitude = level * (35.0 / math.sqrt(D))
    rows = jnp.where(chosen, 0.5 * background + amplitude * signs[None, :], background)
    return jnp.clip(rows, -6.0, 6.0).astype(jnp.bfloat16)


def draw_w_unembed(key, part):
    signs, first_col, second_col = shared_plan(key)
    key = jax.random.fold_in(key, 5)
    spread = 2.0 / math.sqrt(D)
    background = jnp.clip(jax.random.normal(key, (D, VOCAB), jnp.float32), -6.0, 6.0)
    column = jnp.arange(VOCAB)[None, :]
    planted = 6.0 / math.sqrt(D) * signs[:, None]
    weights = jnp.where(column == first_col, planted, jnp.where(column == second_col, 0.99 * planted, spread * background))
    return weights.astype(jnp.bfloat16)


def plant(result, stream_key, least, top_value):
    place = [jax.random.randint(jax.random.fold_in(stream_key, axis), (), 0, length) for axis, length in enumerate(result.shape)]
    main_axis = result.shape.index(max(result.shape))
    neighbour = place[:main_axis] + [(place[main_axis] + 1) % result.shape[main_axis]] + place[main_axis + 1:]
    return result.at[tuple(place)].set(least).at[tuple(neighbour)].set(top_value)


def steps_of(stream_key, extent, cuts, least, top_value):
    level = 1.0
    for dim, shards_of in cuts:
        draws = jax.random.uniform(jax.random.fold_in(jax.random.fold_in(stream_key, 6), dim), (shards_of,), jnp.float32, least / len(cuts), top_value / len(cuts))
        level = level * jnp.repeat(jnp.exp(draws), extent[dim] // shards_of).reshape((-1,) + (1,) * (len(extent) - 1 - dim))
    return level


def rank_bounds(amount, lean):
    weights = [(1 << 20) // math.isqrt(rank ** lean) + 1 for rank in range(1, amount + 1)]
    width = 1 + sum(weights) // (1 << 30)
    return np.cumsum(np.array([max(1, weight // width) for weight in weights]))


def ranked_ids(rng, dims, count, skew):
    table = rank_bounds(count, skew)
    lot = jax.random.randint(jax.random.fold_in(rng, 1), dims, 0, int(table[count - 1]))
    grade = jnp.searchsorted(jnp.asarray(table, jnp.int32), lot, side="right")
    return jax.random.permutation(jax.random.fold_in(rng, 2), count)[grade].astype(jnp.int32)


def noise(own_key, shape, scale, limit, cuts=(), dtype=jnp.bfloat16):
    gain = steps_of(own_key, shape, cuts, -0.22, 0.18) if cuts else 1.0
    result = jax.random.normal(own_key, shape, jnp.float32) * scale * gain
    return jnp.minimum(jnp.maximum(result, -limit), limit).astype(dtype)


def setup_inputs(seed: int = 0) -> dict:
    keys = jax.random.split(jax.random.key(seed), 9)
    tokens_in = draw_tokens_in(jax.random.fold_in(keys[8], 71), 0)
    pre_gain = jnp.clip(1.0 + 0.18 * jax.random.normal(keys[1], (D,), jnp.float32), 0.099609375, 1.8984375).astype(jnp.bfloat16)
    w_in = noise(keys[2], (D, 3, CH), D ** -0.5, 0.09375, ((0, 64), (2, 8)))
    w_out = noise(keys[3], (CH, D), (CH // 16) ** -0.5, 0.5, ((0, 64), (1, 8)))
    long_filter = noise(keys[4], (TOKENS, CH), TOKENS ** -0.5, 0.046875, ((0, 64), (1, 8)))
    w_unembed = draw_w_unembed(jax.random.fold_in(keys[8], 71), 0)
    target_ids = plant(ranked_ids(keys[6], (TOKENS,), VOCAB, 2), jax.random.fold_in(keys[6], 3), 0, VOCAB - 1).astype(jnp.int32)
    score_mask = plant((jax.random.randint(keys[7], (TOKENS,), 0, 4) < 3).astype(jnp.int32), jax.random.fold_in(keys[7], 1), 0, 1)
    return {"tokens_in": tokens_in, "pre_gain": pre_gain, "w_in": w_in, "w_out": w_out, "long_filter": long_filter, "w_unembed": w_unembed, "target_ids": target_ids, "score_mask": score_mask}


NORM_EPS = 1e-05

def reference(tokens_in, pre_gain, w_in, w_out, long_filter, w_unembed, target_ids, score_mask):
    stream = tokens_in.astype(jnp.float32)
    scale = lax.rsqrt(lax.optimization_barrier(jnp.mean(stream * stream, axis=1, keepdims=True)) + NORM_EPS)
    normed = (stream * scale * pre_gain.astype(jnp.float32)).astype(jnp.bfloat16)
    flat_in = w_in.reshape(D, 3 * CH)
    proj = jnp.dot(normed, flat_in, preferred_element_type=jnp.float32).astype(jnp.bfloat16)
    proj = proj.reshape(-1, 3, CH)
    gate_out = proj[:, 0].astype(jnp.float32)
    gated = (proj[:, 1].astype(jnp.float32) * proj[:, 2].astype(jnp.float32)).astype(jnp.bfloat16)
    length = gated.shape[0]
    signal_spec = jnp.fft.rfft(gated.astype(jnp.float32), n=2 * length, axis=0)
    filter_spec = jnp.fft.rfft(long_filter.astype(jnp.float32), n=2 * length, axis=0)
    conv = jnp.fft.irfft(signal_spec * filter_spec, n=2 * length, axis=0)[:length]
    conv = conv.astype(jnp.float32).astype(jnp.bfloat16)
    mixed = (gate_out * conv.astype(jnp.float32)).astype(jnp.bfloat16)
    out = jnp.dot(mixed, w_out, preferred_element_type=jnp.float32).astype(jnp.bfloat16)
    resid = (stream + out.astype(jnp.float32)).astype(jnp.bfloat16)
    logits = jnp.dot(resid, w_unembed, preferred_element_type=jnp.float32)
    row_top = lax.optimization_barrier(jnp.max(logits, axis=1))
    log_total = row_top + jnp.log(lax.optimization_barrier(jnp.sum(jnp.exp(logits - row_top[:, None]), axis=1)))
    picked = jnp.take_along_axis(logits, target_ids.astype(jnp.int32)[:, None], axis=1)[:, 0]
    return (picked - log_total) * score_mask.astype(jnp.float32)
```

```python
import math

import jax
import jax.numpy as jnp
import numpy as np
from jax import lax
from jax.sharding import PartitionSpec as P

NORM_EPS = 1e-05
F32 = jnp.float32
BF16 = jnp.bfloat16

COORDS = [(z, y, x, c) for z in range(2) for y in range(4) for x in range(4) for c in range(2)]


def ctx_id(z, y, x, c):
    return ((z * 4 + y) * 4 + x) * 2 + c


def ctx_perm(move):
    return [(ctx_id(*at), ctx_id(*move(*at))) for at in COORDS]


PERM_CORE = ctx_perm(lambda z, y, x, c: (z, y, x, 1 - c))
PERM_Z = ctx_perm(lambda z, y, x, c: (1 - z, y, x, c))
PERM_Z_UP = [(i, i + 32) for i in range(32)]
GROUPS_X = [[ctx_id(z, y, x, c) for x in range(4)] for z in range(2) for y in range(4) for c in range(2)]
GROUPS_Y = [[ctx_id(z, y, x, c) for y in range(4)] for z in range(2) for x in range(4) for c in range(2)]
GROUPS_PLANE = [
    [ctx_id(z, y, x, c) for y in range(4) for x in range(4) for c in range(2)] for z in range(2)
]
GROUPS_CORE = [
    [ctx_id(z, y, x, c) for y in range(4) for x in range(4)] for z in range(2) for c in range(2)
]
GROUPS_TP = [[0, 1, 2, 3], [4, 5, 6, 7]]


def weight_routes(flip):
    pairs = []
    for i in range(64):
        for q in range(8):
            plane, core, chip, half = i // 8, (i % 8) // 4, (i % 4) * 4 + q // 2, q % 2
            z = half ^ flip
            pairs.append((i * 8 + q, (z * 32 + chip * 2 + core) * 8 + plane))
    return pairs


ROUTE_SAME, ROUTE_FLIP = weight_routes(0), weight_routes(1)


def tables():
    index = np.arange(128)
    inner = 2.0 * math.pi * (np.outer(index, index) % 128) / 128
    outer = 2.0 * math.pi * np.outer(index, index) / 16384
    return (np.cos(inner), np.sin(inner), np.cos(outer), np.sin(outer))


COS, SIN, COS_TW, SIN_TW = tables()


def mm(left, right):
    return jnp.dot(left, right, preferred_element_type=F32)


def spectrum(cube):
    rows, chans, _ = cube.shape
    flat = cube.reshape(rows, chans * 128)
    first = mm(jnp.asarray(np.concatenate([COS[:, :rows], SIN[:, :rows]]), BF16), flat)
    real = first[:128].reshape(128, chans, 128)
    imag = -first[128:].reshape(128, chans, 128)
    cos_tw, sin_tw = (jnp.asarray(t, F32)[:, None, :] for t in (COS_TW, SIN_TW))
    real_t = (real * cos_tw + imag * sin_tw).astype(BF16).reshape(128 * chans, 128)
    imag_t = (imag * cos_tw - real * sin_tw).astype(BF16).reshape(128 * chans, 128)
    both = jnp.asarray(np.concatenate([COS, SIN], axis=1), BF16)
    from_real, from_imag = mm(real_t, both), mm(imag_t, both)
    real_x = from_real[:, :128] + from_imag[:, 128:]
    imag_x = from_imag[:, :128] - from_real[:, 128:]
    return (real_x.reshape(128, chans, 128), imag_x.reshape(128, chans, 128))


def inverse(real_y, imag_y):
    chans = real_y.shape[1]
    both = jnp.asarray(np.concatenate([COS, SIN], axis=1), BF16)
    from_real = mm(real_y.astype(BF16).reshape(128 * chans, 128), both)
    from_imag = mm(imag_y.astype(BF16).reshape(128 * chans, 128), both)
    real_z = (from_real[:, :128] - from_imag[:, 128:]).reshape(128, chans, 128)
    imag_z = (from_imag[:, :128] + from_real[:, 128:]).reshape(128, chans, 128)
    cos_tw, sin_tw = (jnp.asarray(t, F32)[:, None, :] for t in (COS_TW, SIN_TW))
    real_w = (real_z * cos_tw - imag_z * sin_tw).astype(BF16).reshape(128, chans * 128)
    imag_w = (imag_z * cos_tw + real_z * sin_tw).astype(BF16).reshape(128, chans * 128)
    last = jnp.asarray(np.concatenate([COS[:64], -SIN[:64]], axis=1) / 16384.0, BF16)
    return mm(last, jnp.concatenate([real_w, imag_w])).reshape(64, chans, 128)


def by_position(own, other, place):
    return jnp.where(place == 0, jnp.stack([own, other]), jnp.stack([other, own]))


def per_device(tokens_in, pre_gain, w_in, w_out, long_filter, w_unembed, target_ids, score_mask):
    ctx, tp = lax.axis_index("ctx"), lax.axis_index("tp")
    core, z = ctx % 2, ctx // 32

    halves = w_in.reshape(64, 3, 2, 128)
    keep = lax.dynamic_index_in_dim(halves, core, 2, False).reshape(64, 384)
    give = lax.dynamic_index_in_dim(halves, 1 - core, 2, False).reshape(64, 384)
    got = lax.ppermute(give, "ctx", PERM_CORE)
    own = by_position(keep, got, core).reshape(128, 384)
    other = lax.ppermute(own, "ctx", PERM_Z)
    block = by_position(own, other, z).reshape(1, 256, 384)
    block = lax.all_to_all(
        jnp.broadcast_to(block, (4, 256, 384)), "ctx", 0, 0, axis_index_groups=GROUPS_X, tiled=True
    )
    block = lax.all_to_all(
        jnp.broadcast_to(block[None], (4, 4, 256, 384)), "ctx", 0, 0, axis_index_groups=GROUPS_Y, tiled=True
    )
    weights = block.reshape(4096, 384)

    stream = tokens_in.astype(F32)
    scale = lax.rsqrt(jnp.mean(stream * stream, axis=1, keepdims=True) + NORM_EPS)
    normed = (stream * scale * pre_gain.astype(F32)).astype(BF16)
    normed = normed.reshape(256, 2, 16, 128).transpose(0, 2, 1, 3).reshape(256, 4096)
    normed = by_position(normed, lax.ppermute(normed, "ctx", PERM_CORE), core).reshape(512, 4096)

    chans = long_filter.reshape(2, 128, 2, 16, 8).transpose(3, 2, 0, 4, 1).reshape(32, 2, 8, 128)
    chans = lax.all_to_all(chans, "ctx", 0, 0, axis_index_groups=GROUPS_PLANE, tiled=True)
    chans = chans.reshape(64, 8, 128)
    chans = by_position(chans, lax.ppermute(chans, "ctx", PERM_Z), z)
    low_real, low_imag = spectrum(chans[0])
    high_real, high_imag = spectrum(chans[1])
    sign = jnp.asarray(1.0 - 2.0 * (np.arange(128) % 2), F32)[:, None, None]
    all_real, all_imag = sign * low_real + high_real, sign * low_imag + high_imag

    partial = mm(w_out, w_unembed).astype(BF16).reshape(8, 16, 128)
    partial = lax.all_to_all(partial, "tp", 0, 0, tiled=True)
    piece = jnp.sum(partial.astype(F32), axis=0).astype(BF16)
    same = lax.ppermute(piece, ("ctx", "tp"), ROUTE_SAME)
    flip = lax.ppermute(piece, ("ctx", "tp"), ROUTE_FLIP)
    rows8 = by_position(same, flip, z).reshape(1, 8, 512)

    proj = mm(normed, weights).astype(BF16)
    gate = proj[:, :128]
    gated = (proj[:, 128:256].astype(F32) * proj[:, 256:].astype(F32)).astype(BF16)
    gate = gate.reshape(2, 256, 128)
    gate_keep = lax.dynamic_index_in_dim(gate, core, 0, False)
    gate_got = lax.ppermute(lax.dynamic_index_in_dim(gate, 1 - core, 0, False), "ctx", PERM_CORE)
    gate_all = by_position(gate_keep, gate_got, core).reshape(2, 2, 128, 16, 8).transpose(3, 0, 1, 4, 2)

    signal = gated.reshape(4, 128, 16, 8).transpose(2, 0, 3, 1)
    signal = lax.all_to_all(signal, "ctx", 0, 0, axis_index_groups=GROUPS_CORE, tiled=True)
    signal = signal.reshape(64, 8, 128)
    before = lax.ppermute(signal, "ctx", PERM_Z_UP)
    w_mix = lax.all_to_all(
        jnp.broadcast_to(rows8, (32, 8, 512)), "ctx", 0, 0, axis_index_groups=GROUPS_PLANE, tiled=True
    ).reshape(256, 512)
    own_real, own_imag = spectrum(signal)
    old_real, old_imag = spectrum(before)
    real_y = own_real * low_real - own_imag * low_imag + old_real * all_real - old_imag * all_imag
    imag_y = own_real * low_imag + own_imag * low_real + old_real * all_imag + old_imag * all_real
    conv = inverse(real_y, imag_y).astype(BF16)

    conv = conv.reshape(32, 2, 8, 128)
    conv = lax.all_to_all(conv, "ctx", 0, 0, axis_index_groups=GROUPS_PLANE, tiled=True)
    conv = conv.reshape(16, 2, 2, 8, 128)
    mixed = (gate_all.astype(F32) * conv.astype(F32)).astype(BF16)
    mixed = mixed.transpose(2, 4, 0, 1, 3).reshape(256, 256)

    width = w_unembed.shape[0]
    stream_slice = lax.dynamic_slice_in_dim(tokens_in, tp * width, width, 1)
    logits = mm(stream_slice, w_unembed) + mm(mixed, w_mix)
    logits = logits.astype(BF16).reshape(4, 64, 512)
    logits = lax.all_to_all(logits, "tp", 0, 0, axis_index_groups=GROUPS_TP, tiled=True)
    logits = jnp.sum(logits.astype(F32), axis=0).astype(BF16)
    far = lax.ppermute(logits, "tp", [(i, i ^ 4) for i in range(8)])
    logits = logits.astype(F32) + far.astype(F32)

    row_top = jnp.max(logits, axis=1, keepdims=True)
    log_total = row_top[:, 0] + jnp.log(jnp.sum(jnp.exp(logits - row_top), axis=1))
    ids = lax.dynamic_slice_in_dim(target_ids, (tp % 4) * 64, 64, 0)
    vocab_index = lax.broadcasted_iota(jnp.int32, (64, 512), 1)
    picked = jnp.sum(jnp.where(vocab_index == ids[:, None], logits, 0.0), axis=1)
    scores = jnp.broadcast_to((picked - log_total)[None, None, :], (4, 8, 64))
    scores = lax.all_to_all(scores, "tp", 0, 0, axis_index_groups=GROUPS_TP, tiled=True)
    return scores[:, 0].reshape(256) * score_mask.astype(F32)


def solution(mesh):
    return jax.shard_map(
        per_device,
        mesh=mesh,
        in_specs=(
            P("ctx", None),
            P(),
            P("ctx", None, "tp"),
            P("ctx", "tp"),
            P("ctx", "tp"),
            P("tp", None),
            P("ctx"),
            P("ctx"),
        ),
        out_specs=P("ctx"),
        check_vma=False,
    )
```

```python
import math

import jax
import jax.numpy as jnp
import numpy as np
from jax import lax
from jax.experimental import pallas as pl
from jax.experimental.pallas import tpu as pltpu
from jax.sharding import PartitionSpec as P

NORM_EPS = 1e-05
F32 = jnp.float32
BF16 = jnp.bfloat16

COORDS = [(z, y, x, c) for z in range(2) for y in range(4) for x in range(4) for c in range(2)]


def ctx_id(z, y, x, c):
    return ((z * 4 + y) * 4 + x) * 2 + c


def ctx_perm(move):
    return [(ctx_id(*at), ctx_id(*move(*at))) for at in COORDS]


PERM_CORE = ctx_perm(lambda z, y, x, c: (z, y, x, 1 - c))
PERM_Z = ctx_perm(lambda z, y, x, c: (1 - z, y, x, c))
PERM_Z_UP = [(i, i + 32) for i in range(32)]
PERM_X = [ctx_perm(lambda z, y, x, c, k=k: (z, y, (x + k) % 4, c)) for k in range(4)]
PERM_Y = [ctx_perm(lambda z, y, x, c, k=k: (z, (y + k) % 4, x, c)) for k in range(4)]
GROUPS_X = [[ctx_id(z, y, x, c) for x in range(4)] for z in range(2) for y in range(4) for c in range(2)]
GROUPS_Y = [[ctx_id(z, y, x, c) for y in range(4)] for z in range(2) for x in range(4) for c in range(2)]
GROUPS_PLANE = [
    [ctx_id(z, y, x, c) for y in range(4) for x in range(4) for c in range(2)] for z in range(2)
]
GROUPS_CORE = [
    [ctx_id(z, y, x, c) for z in range(2) for y in range(4) for x in range(4)] for c in range(2)
]
GROUPS_TP = [[0, 1, 2, 3], [4, 5, 6, 7]]


def weight_routes(flip):
    pairs = []
    for i in range(64):
        for q in range(8):
            plane, core, chip, half = i // 8, (i % 8) // 4, (i % 4) * 4 + q // 2, q % 2
            z = half ^ flip
            pairs.append((i * 8 + q, (z * 32 + chip * 2 + core) * 8 + plane))
    return pairs


ROUTE_SAME, ROUTE_FLIP = weight_routes(0), weight_routes(1)


def tables():
    index = np.arange(128)
    inner = 2.0 * math.pi * (np.outer(index, index) % 128) / 128
    outer = 2.0 * math.pi * np.outer(index, index) / 16384
    cos, sin = np.cos(inner), np.sin(inner)
    first = np.concatenate([cos[:, :64], -sin[:, :64]], axis=0)
    second = np.block([[cos, -sin], [sin, cos]])
    back = np.block([[cos, sin], [-sin, cos]])
    last = np.concatenate([cos[:64], -sin[:64]], axis=1) / 16384.0
    return (first, second, back, last, np.cos(outer), np.sin(outer))


FIRST, SECOND, BACK, LAST, COS_TW, SIN_TW = tables()


def mm(left, right):
    return jnp.dot(left, right, preferred_element_type=F32)


def whole(count):
    return [pl.BlockSpec(memory_space=pltpu.VMEM)] * count


SCALARS = pl.BlockSpec(memory_space=pltpu.SMEM)


def spectrum(rows, scratch, first, second, cos_tw, sin_tw):
    scratch[...] = rows
    cube = jnp.concatenate([scratch[pl.ds(c, 64, stride=8), :] for c in range(8)], axis=1)
    step = mm(first, cube.astype(BF16))
    parts = []
    for c in range(8):
        real, imag = step[:128, c * 128 : c * 128 + 128], step[128:, c * 128 : c * 128 + 128]
        parts.append(
            jnp.concatenate(
                [(real * cos_tw + imag * sin_tw).astype(BF16), (imag * cos_tw - real * sin_tw).astype(BF16)],
                axis=1,
            )
        )
    return mm(jnp.concatenate(parts, axis=0), second)


def filter_kernel(z_ref, own_ref, got_ref, first, second, cos_tw, sin_tw, low_ref, all_ref, scratch):
    upper = z_ref[0] == 1
    own, got = own_ref[...].astype(F32), got_ref[...].astype(F32)
    args = (scratch, first[...], second[...], cos_tw[...], sin_tw[...])
    low = spectrum(jnp.where(upper, got, own), *args)
    high = spectrum(own, *args)
    odd = lax.broadcasted_iota(jnp.int32, (1024, 256), 0) & 1
    low_ref[...] = low
    all_ref[...] = jnp.where(odd == 1, -low, low) + high


def conv_kernel(
    z_ref, sig_ref, low_ref, all_ref, piece_ref, first, second, back, last, cos_tw_ref, sin_tw_ref, out_ref, scratch
):
    z = z_ref[0]
    cos_tw, sin_tw = cos_tw_ref[...], sin_tw_ref[...]
    args = (scratch, first[...], second[...], cos_tw, sin_tw)
    own = spectrum(sig_ref[z].astype(F32), *args)
    old = spectrum(sig_ref[0].astype(F32) * z.astype(F32), *args)
    low, every = low_ref[...], all_ref[...]
    own_r, own_i, old_r, old_i = own[:, :128], own[:, 128:], old[:, :128], old[:, 128:]
    low_r, low_i, all_r, all_i = low[:, :128], low[:, 128:], every[:, :128], every[:, 128:]
    real = own_r * low_r - own_i * low_i + old_r * all_r - old_i * all_i
    imag = own_r * low_i + own_i * low_r + old_r * all_i + old_i * all_r
    half = mm(jnp.concatenate([real.astype(BF16), imag.astype(BF16)], axis=1), back[...])
    parts = []
    for c in range(8):
        real, imag = half[c * 128 : c * 128 + 128, :128], half[c * 128 : c * 128 + 128, 128:]
        parts.append(
            jnp.concatenate(
                [(real * cos_tw - imag * sin_tw).astype(BF16), (imag * cos_tw + real * sin_tw).astype(BF16)],
                axis=0,
            )
        )
    result = mm(last[...], jnp.concatenate(parts, axis=1))
    for c in range(8):
        scratch[pl.ds(c, 64, stride=8), :] = result[:, c * 128 : c * 128 + 128]
    piece = piece_ref[...]
    for d in range(32):
        out_ref[d, :16] = scratch[d * 16 : d * 16 + 16].astype(BF16)
        out_ref[d, 16:] = piece


def proj_kernel(at_ref, own_ref, other_ref, low_ref, b0, b1, b2, b3, sig_ref, gate_ref):
    y_at, x_at, core = at_ref[0], at_ref[1], at_ref[2]

    def block(ref, lead, row):
        return jnp.concatenate([ref[lead, row + 128 * g : row + 128 * g + 128, :] for g in range(3)], axis=1)

    for part, tokens in enumerate((own_ref, other_ref)):
        total = jnp.zeros((256, 384), F32)
        for y in range(4):
            for x in (0, 2):
                left = tokens[:, (y * 4 + x) * 128 : (y * 4 + x) * 128 + 256]
                right = jnp.concatenate([block(low_ref, y, x * 384), block(low_ref, y, x * 384 + 384)], axis=0)
                total += mm(left, right)
        for step, ref in enumerate((b0, b1, b2, b3)):
            x = lax.rem(x_at + 4 - step, 4)
            for k in (0, 2):
                starts = [2048 + (lax.rem(y_at + 4 - j, 4) * 4 + x) * 128 for j in (k, k + 1)]
                left = jnp.concatenate([tokens[:, pl.ds(pl.multiple_of(s, 128), 128)] for s in starts], axis=1)
                right = jnp.concatenate([block(ref, k, 0), block(ref, k + 1, 0)], axis=0)
                total += mm(left, right)
        proj = total.astype(BF16).astype(F32)
        gated = proj[:, 128:256] * proj[:, 256:]
        place = core if part == 0 else 1 - core
        first, second = gated[:128].T, gated[128:].T
        for p in range(16):
            rows = jnp.concatenate([first[p * 8 : p * 8 + 8], second[p * 8 : p * 8 + 8]], axis=0).astype(BF16)
            sig_ref[0, p, pl.ds(pl.multiple_of(place * 16, 16), 16), :] = rows
            sig_ref[1, p, pl.ds(pl.multiple_of(place * 16, 16), 16), :] = rows
        gate_ref[place, 0] = proj[:128, :128].T.astype(BF16)
        gate_ref[place, 1] = proj[128:, :128].T.astype(BF16)


def mix_kernel(core_ref, got_ref, keep_ref, other_ref, base_ref, out_ref):
    core = core_ref[0]
    keep, other = keep_ref[...].astype(F32), other_ref[...].astype(F32)
    conv = got_ref[:, :16, :].astype(F32)
    for rb in range(2):
        total = base_ref[rb * 128 : rb * 128 + 128, :]
        for c in range(2):
            cube = jnp.concatenate([conv[p * 2 + c, rb * 8 : rb * 8 + 8] for p in range(16)], axis=0)
            gate = jnp.where(core == c, keep[rb], other[rb])
            mixed = (gate * cube).T.astype(BF16)
            weights = []
            for p in range(16):
                piece = got_ref[p * 2 + c, 16:, :].astype(F32)
                weights.append(jnp.concatenate([piece[v * 8 : v * 8 + 8] for v in range(4)], axis=1))
            total += mm(mixed, jnp.concatenate(weights, axis=0).astype(BF16))
        out_ref[rb * 128 : rb * 128 + 128, :] = total.astype(BF16)


def call(kernel, outs, specs, scratch, flops, args):
    return pl.pallas_call(
        kernel,
        out_shape=outs,
        in_specs=specs,
        out_specs=jax.tree.map(lambda _: pl.BlockSpec(memory_space=pltpu.VMEM), outs),
        scratch_shapes=scratch,
        compiler_params=pltpu.CompilerParams(vmem_limit_bytes=40 * 2**20),
        cost_estimate=pl.CostEstimate(flops=flops, bytes_accessed=4 * 2**20, transcendentals=0),
    )(*args)


def shape(dims, dtype):
    return jax.ShapeDtypeStruct(dims, dtype)


def by_position(own, other, place):
    return jnp.where(place == 0, jnp.stack([own, other]), jnp.stack([other, own]))


def filter_spectra(z, own, got):
    consts = (jnp.asarray(FIRST, BF16), jnp.asarray(SECOND, BF16), jnp.asarray(COS_TW, F32), jnp.asarray(SIN_TW, F32))
    return call(
        filter_kernel,
        (shape((1024, 256), F32), shape((1024, 256), F32)),
        [SCALARS] + whole(6),
        [pltpu.VMEM((512, 128), F32)],
        4 * 10**8,
        (z, own, got, *consts),
    )


def convolve(z, signal, low, every, piece):
    consts = [jnp.asarray(t, BF16) for t in (FIRST, SECOND, BACK, LAST)]
    consts += [jnp.asarray(t, F32) for t in (COS_TW, SIN_TW)]
    return call(
        conv_kernel,
        shape((32, 48, 128), BF16),
        [SCALARS] + whole(10),
        [pltpu.VMEM((512, 128), F32)],
        6 * 10**8,
        (z, signal, low, every, piece, *consts),
    )


def gather_weights(w_in, long_filter, ctx):
    core, z = ctx % 2, ctx // 32
    halves = w_in.transpose(1, 0, 2).reshape(3, 64, 2, 128)
    taps = long_filter.reshape(256, 2, 128)

    def half_of(which):
        weights = lax.dynamic_index_in_dim(halves, which, 2, False).reshape(192, 128)
        return jnp.concatenate([weights, lax.dynamic_index_in_dim(taps, which, 1, False)], axis=0)

    keep = half_of(core)
    got = lax.ppermute(half_of(1 - core), "ctx", PERM_CORE)
    both = by_position(keep, got, core)
    own = both[:, :192].reshape(2, 3, 64, 128).transpose(1, 0, 2, 3).reshape(384, 128)
    taps = both[:, 192:].reshape(2, 2, 128, 4, 4, 8).transpose(4, 3, 0, 1, 5, 2).reshape(4, 128, 128)
    other = lax.ppermute(own, "ctx", PERM_Z)
    low = jnp.where(z == 0, own, other)
    high = jnp.where(z == 0, other, own)

    along_y = jnp.stack([high] + [lax.ppermute(high, "ctx", PERM_Y[k]) for k in (1, 2, 3)])
    low = jnp.concatenate([jnp.broadcast_to(low, (4, 384, 128)), taps], axis=1)
    low = lax.all_to_all(low, "ctx", 0, 0, axis_index_groups=GROUPS_X, tiled=True)
    taps = low[:, 384:].reshape(4, 4, 32, 128).transpose(1, 0, 2, 3).reshape(4, 128, 128)
    low = jnp.broadcast_to(low[:, :384].reshape(1, 1536, 128), (4, 1536, 128))
    low = jnp.concatenate([low, taps], axis=1)
    low = lax.all_to_all(low, "ctx", 0, 0, axis_index_groups=GROUPS_Y, tiled=True)
    highs = [along_y] + [lax.ppermute(along_y, "ctx", PERM_X[k]) for k in (1, 2, 3)]
    return low, highs, low[:, 1536:].reshape(512, 128)


def output_weights(w_out, w_unembed, z):
    partial = mm(w_out, w_unembed)
    piece = lax.psum_scatter(partial, "tp", scatter_dimension=0, tiled=True).astype(BF16).reshape(16, 128)
    same = lax.ppermute(piece, ("ctx", "tp"), ROUTE_SAME)
    flip = lax.ppermute(piece, ("ctx", "tp"), ROUTE_FLIP)
    return by_position(same, flip, z).reshape(8, 4, 128).transpose(1, 0, 2).reshape(32, 128)


def per_device(tokens_in, pre_gain, w_in, w_out, long_filter, w_unembed, target_ids, score_mask):
    ctx, tp = lax.axis_index("ctx"), lax.axis_index("tp")
    core, z = ctx % 2, ctx // 32
    z_at = z.reshape(1).astype(jnp.int32)
    low, highs, taps = gather_weights(w_in, long_filter, ctx)
    piece = output_weights(w_out, w_unembed, z)

    stream = tokens_in.astype(F32)
    scale = lax.rsqrt(jnp.mean(stream * stream, axis=1, keepdims=True) + NORM_EPS)
    normed = (stream * scale * pre_gain.astype(F32)).astype(BF16)
    beside = lax.ppermute(normed, "ctx", PERM_CORE)

    at = jnp.stack([(ctx // 8) % 4, (ctx // 2) % 4, core]).astype(jnp.int32)
    signal, gate = call(
        proj_kernel,
        (shape((2, 16, 32, 128), BF16), shape((2, 2, 128, 128), BF16)),
        [SCALARS] + whole(7),
        [],
        16 * 10**8,
        (at, normed, beside, low, *highs),
    )
    signal = lax.all_to_all(
        signal.reshape(32, 32, 128), "ctx", 0, 0, axis_index_groups=GROUPS_CORE, tiled=True
    ).reshape(2, 512, 128)
    gate_keep = lax.dynamic_index_in_dim(gate, core, 0, False)
    gate_got = lax.ppermute(lax.dynamic_index_in_dim(gate, 1 - core, 0, False), "ctx", PERM_CORE)

    spectra = filter_spectra(z_at, taps, lax.ppermute(taps, "ctx", PERM_Z_UP))
    conv = convolve(z_at, signal, *spectra, piece)
    conv = lax.all_to_all(conv, "ctx", 0, 0, axis_index_groups=GROUPS_PLANE, tiled=True)

    width = w_unembed.shape[0]
    base = mm(lax.dynamic_slice_in_dim(tokens_in, tp * width, width, 1), w_unembed)
    logits = call(
        mix_kernel,
        shape((256, 512), BF16),
        [SCALARS] + whole(4),
        [],
        10**8,
        (core.reshape(1).astype(jnp.int32), conv, gate_keep, gate_got, base),
    )
    logits = lax.all_to_all(logits.reshape(4, 64, 512), "tp", 0, 0, axis_index_groups=GROUPS_TP, tiled=True)
    logits = jnp.sum(logits.astype(F32), axis=0).astype(BF16)
    far = lax.ppermute(logits, "tp", [(i, i ^ 4) for i in range(8)])
    logits = logits.astype(F32) + far.astype(F32)

    row_top = jnp.max(logits, axis=1, keepdims=True)
    log_total = row_top[:, 0] + jnp.log(jnp.sum(jnp.exp(logits - row_top), axis=1))
    ids = lax.dynamic_slice_in_dim(target_ids, (tp % 4) * 64, 64, 0)
    vocab_index = lax.broadcasted_iota(jnp.int32, (64, 512), 1)
    picked = jnp.sum(jnp.where(vocab_index == ids[:, None], logits, 0.0), axis=1)
    scores = jnp.broadcast_to((picked - log_total)[None, None, :], (4, 8, 64))
    scores = lax.all_to_all(scores, "tp", 0, 0, axis_index_groups=GROUPS_TP, tiled=True)
    return scores[:, 0].reshape(256) * score_mask.astype(F32)


def solution(mesh):
    return jax.shard_map(
        per_device,
        mesh=mesh,
        in_specs=(
            P("ctx", None),
            P(),
            P("ctx", None, "tp"),
            P("ctx", "tp"),
            P("ctx", "tp"),
            P("tp", None),
            P("ctx"),
            P("ctx"),
        ),
        out_specs=P("ctx"),
        check_vma=False,
    )
```

```python
import math

import jax
import jax.numpy as jnp
import numpy as np
from jax import lax
from jax.experimental import pallas as pl
from jax.experimental.pallas import tpu as pltpu
from jax.sharding import PartitionSpec as P

NORM_EPS = 1e-05
F32 = jnp.float32
BF16 = jnp.bfloat16

COORDS = [(z, y, x, c) for z in range(2) for y in range(4) for x in range(4) for c in range(2)]


def ctx_id(z, y, x, c):
    return ((z * 4 + y) * 4 + x) * 2 + c


def ctx_perm(move):
    return [(ctx_id(*at), ctx_id(*move(*at))) for at in COORDS]


PERM_CORE = ctx_perm(lambda z, y, x, c: (z, y, x, 1 - c))
PERM_Z = ctx_perm(lambda z, y, x, c: (1 - z, y, x, c))
PERM_Z_UP = [(i, i + 32) for i in range(32)]
PERM_X = [ctx_perm(lambda z, y, x, c, k=k: (z, y, (x + k) % 4, c)) for k in range(4)]
PERM_Y = [ctx_perm(lambda z, y, x, c, k=k: (z, (y + k) % 4, x, c)) for k in range(4)]
GROUPS_X = [[ctx_id(z, y, x, c) for x in range(4)] for z in range(2) for y in range(4) for c in range(2)]
GROUPS_Y = [[ctx_id(z, y, x, c) for y in range(4)] for z in range(2) for x in range(4) for c in range(2)]
GROUPS_PLANE = [
    [ctx_id(z, y, x, c) for y in range(4) for x in range(4) for c in range(2)] for z in range(2)
]
GROUPS_CORE = [
    [ctx_id(z, y, x, c) for y in range(4) for x in range(4)] for z in range(2) for c in range(2)
]
GROUPS_TP = [[0, 1, 2, 3], [4, 5, 6, 7]]


def weight_route():
    pairs = []
    for i in range(64):
        for j in range(8):
            plane, core, chip, z = i // 8, (i % 8) // 4, (i % 4) * 4 + j // 2, j % 2
            pairs.append((i * 8 + j, (z * 32 + chip * 2 + core) * 8 + plane))
    return pairs


ROUTE = weight_route()


def tables():
    index = np.arange(128)
    inner = 2.0 * math.pi * (np.outer(index, index) % 128) / 128
    outer = 2.0 * math.pi * np.outer(index, index) / 16384
    cos, sin = np.cos(inner), np.sin(inner)
    first = np.concatenate([cos[:, :64], -sin[:, :64]], axis=0)
    second = np.block([[cos, -sin], [sin, cos]])
    back = np.block([[cos, sin], [-sin, cos]])
    last = np.concatenate([cos[:64], -sin[:64]], axis=1) / 16384.0
    return (first, second, back, last, np.cos(outer), np.sin(outer))


FIRST, SECOND, BACK, LAST, COS_TW, SIN_TW = tables()


def mm(left, right):
    return jnp.dot(left, right, preferred_element_type=F32)


def whole(count):
    return [pl.BlockSpec(memory_space=pltpu.VMEM)] * count


SCALARS = pl.BlockSpec(memory_space=pltpu.SMEM)


def spectrum(rows, scratch, first, second, cos_tw, sin_tw):
    scratch[...] = rows
    cube = jnp.concatenate([scratch[pl.ds(c, 64, stride=8), :] for c in range(8)], axis=1)
    step = mm(first, cube.astype(BF16))
    parts = []
    for c in range(8):
        real, imag = step[:128, c * 128 : c * 128 + 128], step[128:, c * 128 : c * 128 + 128]
        parts.append(
            jnp.concatenate(
                [(real * cos_tw + imag * sin_tw).astype(BF16), (imag * cos_tw - real * sin_tw).astype(BF16)],
                axis=1,
            )
        )
    return mm(jnp.concatenate(parts, axis=0), second)


def filter_kernel(z_ref, own_ref, got_ref, first, second, cos_tw, sin_tw, low_ref, all_ref, scratch):
    upper = z_ref[0] == 1
    own, got = own_ref[...].astype(F32), got_ref[...].astype(F32)
    args = (scratch, first[...], second[...], cos_tw[...], sin_tw[...])
    low = spectrum(jnp.where(upper, got, own), *args)
    high = spectrum(own, *args)
    odd = lax.broadcasted_iota(jnp.int32, (1024, 256), 0) & 1
    low_ref[...] = low
    all_ref[...] = jnp.where(odd == 1, -low, low) + high


def conv_kernel(
    z_ref, sig_ref, before_ref, low_ref, all_ref, piece_ref, first, second, back, last, cos_tw_ref, sin_tw_ref, out_ref, scratch
):
    cos_tw, sin_tw = cos_tw_ref[...], sin_tw_ref[...]
    args = (scratch, first[...], second[...], cos_tw, sin_tw)
    own = spectrum(sig_ref[...].astype(F32), *args)
    old = spectrum(jnp.where(z_ref[0] == 1, before_ref[...].astype(F32), 0.0), *args)
    low, every = low_ref[...], all_ref[...]
    own_r, own_i, old_r, old_i = own[:, :128], own[:, 128:], old[:, :128], old[:, 128:]
    low_r, low_i, all_r, all_i = low[:, :128], low[:, 128:], every[:, :128], every[:, 128:]
    real = own_r * low_r - own_i * low_i + old_r * all_r - old_i * all_i
    imag = own_r * low_i + own_i * low_r + old_r * all_i + old_i * all_r
    half = mm(jnp.concatenate([real.astype(BF16), imag.astype(BF16)], axis=1), back[...])
    parts = []
    for c in range(8):
        real, imag = half[c * 128 : c * 128 + 128, :128], half[c * 128 : c * 128 + 128, 128:]
        parts.append(
            jnp.concatenate(
                [(real * cos_tw - imag * sin_tw).astype(BF16), (imag * cos_tw + real * sin_tw).astype(BF16)],
                axis=0,
            )
        )
    result = mm(last[...], jnp.concatenate(parts, axis=1))
    for c in range(8):
        scratch[pl.ds(c, 64, stride=8), :] = result[:, c * 128 : c * 128 + 128]
    piece = piece_ref[...]
    for d in range(32):
        out_ref[d, :16] = scratch[d * 16 : d * 16 + 16].astype(BF16)
        out_ref[d, 16:] = piece


def weight_block(ref, lead, row):
    return jnp.concatenate([ref[lead, row + 128 * g : row + 128 * g + 128, :] for g in range(3)], axis=1)


def columns(ref, start, count):
    return ref[:, pl.ds(pl.multiple_of(start, 128), count)]


def near_kernel(at_ref, own_ref, beside_ref, near_ref, out_ref):
    start = at_ref[3] * 2048
    for part, tokens in enumerate((own_ref, beside_ref)):
        total = jnp.zeros((256, 384), F32)
        for y in range(4):
            for x in (0, 2):
                left = columns(tokens, start + (y * 4 + x) * 128, 256)
                right = [weight_block(near_ref, y, x * 384), weight_block(near_ref, y, x * 384 + 384)]
                total += mm(left, jnp.concatenate(right, axis=0))
        out_ref[part] = total


def proj_kernel(at_ref, own_ref, beside_ref, near_ref, f0, f1, f2, f3, sig_ref, gate_ref):
    y_at, x_at, core = at_ref[0], at_ref[1], at_ref[2]
    start = 2048 - at_ref[3] * 2048
    for part, tokens in enumerate((own_ref, beside_ref)):
        total = near_ref[part]
        for step, ref in enumerate((f0, f1, f2, f3)):
            x = lax.rem(x_at + 4 - step, 4)
            for k in (0, 2):
                left = [columns(tokens, start + (lax.rem(y_at + 4 - j, 4) * 4 + x) * 128, 128) for j in (k, k + 1)]
                right = [weight_block(ref, k, 0), weight_block(ref, k + 1, 0)]
                total += mm(jnp.concatenate(left, axis=1), jnp.concatenate(right, axis=0))
        proj = total.astype(BF16).astype(F32)
        gated = proj[:, 128:256] * proj[:, 256:]
        place = core if part == 0 else 1 - core
        first, second = gated[:128].T, gated[128:].T
        for p in range(16):
            rows = jnp.concatenate([first[p * 8 : p * 8 + 8], second[p * 8 : p * 8 + 8]], axis=0).astype(BF16)
            sig_ref[p, pl.ds(pl.multiple_of(place * 16, 16), 16), :] = rows
        gate_ref[place, 0] = proj[:128, :128].T.astype(BF16)
        gate_ref[place, 1] = proj[128:, :128].T.astype(BF16)


def mix_kernel(core_ref, got_ref, keep_ref, other_ref, base_ref, out_ref):
    core = core_ref[0]
    keep, other = keep_ref[...].astype(F32), other_ref[...].astype(F32)
    conv = got_ref[:, :16, :].astype(F32)
    for rb in range(2):
        total = base_ref[rb * 128 : rb * 128 + 128, :]
        for c in range(2):
            cube = jnp.concatenate([conv[p * 2 + c, rb * 8 : rb * 8 + 8] for p in range(16)], axis=0)
            gate = jnp.where(core == c, keep[rb], other[rb])
            mixed = (gate * cube).T.astype(BF16)
            weights = []
            for p in range(16):
                piece = got_ref[p * 2 + c, 16:, :].astype(F32)
                weights.append(jnp.concatenate([piece[v * 8 : v * 8 + 8] for v in range(4)], axis=1))
            total += mm(mixed, jnp.concatenate(weights, axis=0).astype(BF16))
        out_ref[rb * 128 : rb * 128 + 128, :] = total.astype(BF16)


def call(kernel, outs, specs, scratch, flops, args):
    return pl.pallas_call(
        kernel,
        out_shape=outs,
        in_specs=specs,
        out_specs=jax.tree.map(lambda _: pl.BlockSpec(memory_space=pltpu.VMEM), outs),
        scratch_shapes=scratch,
        compiler_params=pltpu.CompilerParams(vmem_limit_bytes=40 * 2**20),
        cost_estimate=pl.CostEstimate(flops=flops, bytes_accessed=4 * 2**20, transcendentals=0),
    )(*args)


def shape(dims, dtype):
    return jax.ShapeDtypeStruct(dims, dtype)


def by_position(own, other, place):
    return jnp.where(place == 0, jnp.stack([own, other]), jnp.stack([other, own]))


def filter_spectra(z, own, got):
    consts = (jnp.asarray(FIRST, BF16), jnp.asarray(SECOND, BF16), jnp.asarray(COS_TW, F32), jnp.asarray(SIN_TW, F32))
    return call(
        filter_kernel,
        (shape((1024, 256), F32), shape((1024, 256), F32)),
        [SCALARS] + whole(6),
        [pltpu.VMEM((512, 128), F32)],
        4 * 10**8,
        (z, own, got, *consts),
    )


def convolve(z, signal, before, low, every, piece):
    consts = [jnp.asarray(t, BF16) for t in (FIRST, SECOND, BACK, LAST)]
    consts += [jnp.asarray(t, F32) for t in (COS_TW, SIN_TW)]
    return call(
        conv_kernel,
        shape((32, 48, 128), BF16),
        [SCALARS] + whole(11),
        [pltpu.VMEM((512, 128), F32)],
        6 * 10**8,
        (z, signal, before, low, every, piece, *consts),
    )


def gather_weights(w_in, long_filter, ctx):
    core = ctx % 2
    halves = w_in.transpose(1, 0, 2).reshape(3, 64, 2, 128)
    taps = long_filter.reshape(256, 2, 128)

    def half_of(which):
        weights = lax.dynamic_index_in_dim(halves, which, 2, False).reshape(192, 128)
        return jnp.concatenate([weights, lax.dynamic_index_in_dim(taps, which, 1, False)], axis=0)

    keep = half_of(core)
    got = lax.ppermute(half_of(1 - core), "ctx", PERM_CORE)
    both = by_position(keep, got, core)
    near = both[:, :192].reshape(2, 3, 64, 128).transpose(1, 0, 2, 3).reshape(384, 128)
    far = lax.ppermute(near, "ctx", PERM_Z)
    taps = both[:, 192:].reshape(2, 2, 128, 4, 4, 8).transpose(4, 3, 0, 1, 5, 2).reshape(4, 128, 128)

    near = jnp.concatenate([jnp.broadcast_to(near, (4, 384, 128)), taps], axis=1)
    near = lax.all_to_all(near, "ctx", 0, 0, axis_index_groups=GROUPS_X, tiled=True)
    taps = near[:, 384:].reshape(4, 4, 32, 128).transpose(1, 0, 2, 3).reshape(4, 128, 128)
    near = jnp.broadcast_to(near[:, :384].reshape(1, 1536, 128), (4, 1536, 128))
    near = jnp.concatenate([near, taps], axis=1)
    near = lax.all_to_all(near, "ctx", 0, 0, axis_index_groups=GROUPS_Y, tiled=True)

    along_y = jnp.stack([far] + [lax.ppermute(far, "ctx", PERM_Y[k]) for k in (1, 2, 3)])
    fars = [along_y] + [lax.ppermute(along_y, "ctx", PERM_X[k]) for k in (1, 2, 3)]
    return near, fars, near[:, 1536:].reshape(512, 128)


def output_weights(w_out, w_unembed, tp):
    partial = mm(w_out, w_unembed)
    partial = lax.all_gather(jnp.concatenate([partial, partial]), "tp", axis=0)
    rows = lax.dynamic_slice_in_dim(partial, (tp // 2) * 8, 8, 1)
    rows = jnp.sum(rows, axis=0).astype(BF16).reshape(8, 4, 128).transpose(1, 0, 2).reshape(32, 128)
    return lax.ppermute(rows, ("ctx", "tp"), ROUTE)


def per_device(tokens_in, pre_gain, w_in, w_out, long_filter, w_unembed, target_ids, score_mask):
    ctx, tp = lax.axis_index("ctx"), lax.axis_index("tp")
    core, z = ctx % 2, ctx // 32
    z_at = z.reshape(1).astype(jnp.int32)
    near, fars, taps = gather_weights(w_in, long_filter, ctx)
    piece = output_weights(w_out, w_unembed, tp)

    stream = tokens_in.astype(F32)
    scale = lax.rsqrt(jnp.mean(stream * stream, axis=1, keepdims=True) + NORM_EPS)
    normed = (stream * scale * pre_gain.astype(F32)).astype(BF16)
    beside = lax.ppermute(normed, "ctx", PERM_CORE)

    at = jnp.stack([(ctx // 8) % 4, (ctx // 2) % 4, core, z]).astype(jnp.int32)
    sums = call(
        near_kernel, shape((2, 256, 384), F32), [SCALARS] + whole(3), [], 8 * 10**8, (at, normed, beside, near)
    )
    signal, gate = call(
        proj_kernel,
        (shape((16, 32, 128), BF16), shape((2, 2, 128, 128), BF16)),
        [SCALARS] + whole(7),
        [],
        8 * 10**8,
        (at, normed, beside, sums, *fars),
    )
    signal = lax.all_to_all(signal, "ctx", 0, 0, axis_index_groups=GROUPS_CORE, tiled=True).reshape(512, 128)
    before = lax.ppermute(signal, "ctx", PERM_Z_UP)
    gate_keep = lax.dynamic_index_in_dim(gate, core, 0, False)
    gate_got = lax.ppermute(lax.dynamic_index_in_dim(gate, 1 - core, 0, False), "ctx", PERM_CORE)

    spectra = filter_spectra(z_at, taps, lax.ppermute(taps, "ctx", PERM_Z_UP))
    conv = convolve(z_at, signal, before, *spectra, piece)
    conv = lax.all_to_all(conv, "ctx", 0, 0, axis_index_groups=GROUPS_PLANE, tiled=True)

    width = w_unembed.shape[0]
    base = mm(lax.dynamic_slice_in_dim(tokens_in, tp * width, width, 1), w_unembed)
    logits = call(
        mix_kernel,
        shape((256, 512), BF16),
        [SCALARS] + whole(4),
        [],
        10**8,
        (core.reshape(1).astype(jnp.int32), conv, gate_keep, gate_got, base),
    )
    logits = lax.all_to_all(logits.reshape(4, 64, 512), "tp", 0, 0, axis_index_groups=GROUPS_TP, tiled=True)
    logits = jnp.sum(logits.astype(F32), axis=0).astype(BF16)
    far = lax.ppermute(logits, "tp", [(i, i ^ 4) for i in range(8)])
    logits = logits.astype(F32) + far.astype(F32)

    row_top = jnp.max(logits, axis=1, keepdims=True)
    log_total = row_top[:, 0] + jnp.log(jnp.sum(jnp.exp(logits - row_top), axis=1))
    ids = lax.dynamic_slice_in_dim(target_ids, (tp % 4) * 64, 64, 0)
    vocab_index = lax.broadcasted_iota(jnp.int32, (64, 512), 1)
    picked = jnp.sum(jnp.where(vocab_index == ids[:, None], logits, 0.0), axis=1)
    scores = jnp.broadcast_to((picked - log_total)[None, None, :], (4, 8, 64))
    scores = lax.all_to_all(scores, "tp", 0, 0, axis_index_groups=GROUPS_TP, tiled=True)
    return scores[:, 0].reshape(256) * score_mask.astype(F32)


def solution(mesh):
    return jax.shard_map(
        per_device,
        mesh=mesh,
        in_specs=(
            P("ctx", None),
            P(),
            P("ctx", None, "tp"),
            P("ctx", "tp"),
            P("ctx", "tp"),
            P("tp", None),
            P("ctx"),
            P("ctx"),
        ),
        out_specs=P("ctx"),
        check_vma=False,
    )
```

```python
import math

import jax
import jax.numpy as jnp
import numpy as np
from jax import lax
from jax.experimental import pallas as pl
from jax.experimental.pallas import tpu as pltpu
from jax.sharding import PartitionSpec as P

NORM_EPS = 1e-05
F32 = jnp.float32
BF16 = jnp.bfloat16

COORDS = [(z, y, x, c) for z in range(2) for y in range(4) for x in range(4) for c in range(2)]


def ctx_id(z, y, x, c):
    return ((z * 4 + y) * 4 + x) * 2 + c


def ctx_perm(move):
    return [(ctx_id(*at), ctx_id(*move(*at))) for at in COORDS]


PERM_CORE = ctx_perm(lambda z, y, x, c: (z, y, x, 1 - c))
PERM_Z = ctx_perm(lambda z, y, x, c: (1 - z, y, x, c))
PERM_Z_UP = [(i, i + 32) for i in range(32)]
PERM_X = [ctx_perm(lambda z, y, x, c, k=k: (z, y, (x + k) % 4, c)) for k in range(4)]
PERM_Y = [ctx_perm(lambda z, y, x, c, k=k: (z, (y + k) % 4, x, c)) for k in range(4)]
GROUPS_X = [[ctx_id(z, y, x, c) for x in range(4)] for z in range(2) for y in range(4) for c in range(2)]
GROUPS_Y = [[ctx_id(z, y, x, c) for y in range(4)] for z in range(2) for x in range(4) for c in range(2)]
GROUPS_PLANE = [
    [ctx_id(z, y, x, c) for y in range(4) for x in range(4) for c in range(2)] for z in range(2)
]
GROUPS_CORE = [
    [ctx_id(z, y, x, c) for y in range(4) for x in range(4)] for z in range(2) for c in range(2)
]
GROUPS_TP = [[0, 1, 2, 3], [4, 5, 6, 7]]


def weight_route():
    pairs = []
    for i in range(64):
        for j in range(8):
            plane, core, chip, z = i // 8, (i % 8) // 4, (i % 4) * 4 + j // 2, j % 2
            pairs.append((i * 8 + j, (z * 32 + chip * 2 + core) * 8 + plane))
    return pairs


ROUTE = weight_route()


def tables():
    index = np.arange(128)
    inner = 2.0 * math.pi * (np.outer(index, index) % 128) / 128
    outer = 2.0 * math.pi * np.outer(index, index) / 16384
    cos, sin = np.cos(inner), np.sin(inner)
    first = np.concatenate([cos[:, :64], -sin[:, :64]], axis=0)
    second = np.block([[cos, -sin], [sin, cos]])
    back = np.block([[cos, sin], [-sin, cos]])
    last = np.concatenate([cos[:64], -sin[:64]], axis=1) / 16384.0
    return (first, second, back, last, np.cos(outer), np.sin(outer))


FIRST, SECOND, BACK, LAST, COS_TW, SIN_TW = tables()
MATRICES = np.concatenate([np.pad(FIRST, ((0, 0), (0, 192))), SECOND, BACK, LAST])
TWIDDLES = np.concatenate([COS_TW, SIN_TW], axis=1)


def mm(left, right):
    return jnp.dot(left, right, preferred_element_type=F32)


def whole(count):
    return [pl.BlockSpec(memory_space=pltpu.VMEM)] * count


SCALARS = pl.BlockSpec(memory_space=pltpu.SMEM)


def spectrum(scratch, matrices, twiddles):
    cos_tw, sin_tw = twiddles[:, :128], twiddles[:, 128:]
    cube = jnp.concatenate([scratch[pl.ds(c, 64, stride=8), :] for c in range(8)], axis=1)
    step = mm(matrices[:256, :64], cube.astype(BF16))
    parts = []
    for c in range(8):
        real, imag = step[:128, c * 128 : c * 128 + 128], step[128:, c * 128 : c * 128 + 128]
        parts.append(
            jnp.concatenate(
                [(real * cos_tw + imag * sin_tw).astype(BF16), (imag * cos_tw - real * sin_tw).astype(BF16)],
                axis=1,
            )
        )
    return mm(jnp.concatenate(parts, axis=0), matrices[256:512, :])


def filter_kernel(z_ref, got_ref, matrices, twiddles, low_ref, all_ref, scratch):
    upper = z_ref[0] == 1
    for p in range(16):
        scratch[p * 32 : p * 32 + 32] = got_ref[p, 32:64].astype(F32)
    high = spectrum(scratch, matrices, twiddles)
    for p in range(16):
        scratch[p * 32 : p * 32 + 32] = jnp.where(upper, got_ref[p, 64:].astype(F32), got_ref[p, 32:64].astype(F32))
    low = spectrum(scratch, matrices, twiddles)
    odd = lax.broadcasted_iota(jnp.int32, (1024, 256), 0) & 1
    low_ref[...] = low
    all_ref[...] = jnp.where(odd == 1, -low, low) + high


def conv_kernel(z_ref, sig_ref, before_ref, low_ref, all_ref, piece_ref, matrices, twiddles, out_ref, scratch):
    cos_tw, sin_tw = twiddles[:, :128], twiddles[:, 128:]
    scratch[...] = sig_ref[...].astype(F32)
    own = spectrum(scratch, matrices, twiddles)
    scratch[...] = jnp.where(z_ref[0] == 1, before_ref[...].astype(F32), 0.0)
    old = spectrum(scratch, matrices, twiddles)
    low, every = low_ref[...], all_ref[...]
    own_r, own_i, old_r, old_i = own[:, :128], own[:, 128:], old[:, :128], old[:, 128:]
    low_r, low_i, all_r, all_i = low[:, :128], low[:, 128:], every[:, :128], every[:, 128:]
    real = own_r * low_r - own_i * low_i + old_r * all_r - old_i * all_i
    imag = own_r * low_i + own_i * low_r + old_r * all_i + old_i * all_r
    half = mm(jnp.concatenate([real.astype(BF16), imag.astype(BF16)], axis=1), matrices[512:768, :])
    parts = []
    for c in range(8):
        real, imag = half[c * 128 : c * 128 + 128, :128], half[c * 128 : c * 128 + 128, 128:]
        parts.append(
            jnp.concatenate(
                [(real * cos_tw - imag * sin_tw).astype(BF16), (imag * cos_tw + real * sin_tw).astype(BF16)],
                axis=0,
            )
        )
    result = mm(matrices[768:, :], jnp.concatenate(parts, axis=1))
    for c in range(8):
        scratch[pl.ds(c, 64, stride=8), :] = result[:, c * 128 : c * 128 + 128]
    piece = piece_ref[...]
    for d in range(32):
        out_ref[d, :16] = scratch[d * 16 : d * 16 + 16].astype(BF16)
        out_ref[d, 16:] = piece


def weight_block(ref, lead, row):
    return jnp.concatenate([ref[lead, row + 128 * g : row + 128 * g + 128, :] for g in range(3)], axis=1)


def columns(ref, start, count):
    return ref[:, pl.ds(pl.multiple_of(start, 128), count)]


def near_kernel(at_ref, own_ref, beside_ref, near_ref, out_ref):
    start = at_ref[3] * 2048
    for part, tokens in enumerate((own_ref, beside_ref)):
        total = jnp.zeros((256, 384), F32)
        for y in range(4):
            for x in (0, 2):
                left = columns(tokens, start + (y * 4 + x) * 128, 256)
                right = [weight_block(near_ref, y, x * 384), weight_block(near_ref, y, x * 384 + 384)]
                total += mm(left, jnp.concatenate(right, axis=0))
        out_ref[part] = total


def proj_kernel(at_ref, own_ref, beside_ref, near_ref, taps_ref, f0, f1, f2, f3, sig_ref, gate_ref):
    y_at, x_at, core = at_ref[0], at_ref[1], at_ref[2]
    start = 2048 - at_ref[3] * 2048
    for part, tokens in enumerate((own_ref, beside_ref)):
        total = near_ref[part]
        for step, ref in enumerate((f0, f1, f2, f3)):
            x = lax.rem(x_at + 4 - step, 4)
            for k in (0, 2):
                left = [columns(tokens, start + (lax.rem(y_at + 4 - j, 4) * 4 + x) * 128, 128) for j in (k, k + 1)]
                right = [weight_block(ref, k, 0), weight_block(ref, k + 1, 0)]
                total += mm(jnp.concatenate(left, axis=1), jnp.concatenate(right, axis=0))
        proj = total.astype(BF16).astype(F32)
        gated = proj[:, 128:256] * proj[:, 256:]
        place = core if part == 0 else 1 - core
        first, second = gated[:128].T, gated[128:].T
        for p in range(16):
            rows = jnp.concatenate([first[p * 8 : p * 8 + 8], second[p * 8 : p * 8 + 8]], axis=0).astype(BF16)
            sig_ref[p, pl.ds(pl.multiple_of(place * 16, 16), 16), :] = rows
        gate_ref[place, 0] = proj[:128, :128].T.astype(BF16)
        gate_ref[place, 1] = proj[128:, :128].T.astype(BF16)
    for p in range(16):
        sig_ref[p, 32:, :] = taps_ref[p]


def mix_kernel(core_ref, got_ref, keep_ref, other_ref, base_ref, out_ref):
    core = core_ref[0]
    keep, other = keep_ref[...].astype(F32), other_ref[...].astype(F32)
    conv = got_ref[:, :16, :].astype(F32)
    for rb in range(2):
        total = base_ref[rb * 128 : rb * 128 + 128, :]
        for c in range(2):
            cube = jnp.concatenate([conv[p * 2 + c, rb * 8 : rb * 8 + 8] for p in range(16)], axis=0)
            gate = jnp.where(core == c, keep[rb], other[rb])
            mixed = (gate * cube).T.astype(BF16)
            weights = []
            for p in range(16):
                piece = got_ref[p * 2 + c, 16:, :].astype(F32)
                weights.append(jnp.concatenate([piece[v * 8 : v * 8 + 8] for v in range(4)], axis=1))
            total += mm(mixed, jnp.concatenate(weights, axis=0).astype(BF16))
        out_ref[rb * 128 : rb * 128 + 128, :] = total.astype(BF16)


def call(kernel, outs, specs, scratch, flops, args):
    return pl.pallas_call(
        kernel,
        out_shape=outs,
        in_specs=specs,
        out_specs=jax.tree.map(lambda _: pl.BlockSpec(memory_space=pltpu.VMEM), outs),
        scratch_shapes=scratch,
        compiler_params=pltpu.CompilerParams(vmem_limit_bytes=40 * 2**20),
        cost_estimate=pl.CostEstimate(flops=flops, bytes_accessed=4 * 2**20, transcendentals=0),
    )(*args)


def shape(dims, dtype):
    return jax.ShapeDtypeStruct(dims, dtype)


def by_position(own, other, place):
    return jnp.where(place == 0, jnp.stack([own, other]), jnp.stack([other, own]))


def filter_spectra(z, got):
    return call(
        filter_kernel,
        (shape((1024, 256), F32), shape((1024, 256), F32)),
        [SCALARS] + whole(3),
        [pltpu.VMEM((512, 128), F32)],
        4 * 10**8,
        (z, got, jnp.asarray(MATRICES, BF16), jnp.asarray(TWIDDLES, F32)),
    )


def convolve(z, signal, before, low, every, piece):
    return call(
        conv_kernel,
        shape((32, 48, 128), BF16),
        [SCALARS] + whole(7),
        [pltpu.VMEM((512, 128), F32)],
        6 * 10**8,
        (z, signal, before, low, every, piece, jnp.asarray(MATRICES, BF16), jnp.asarray(TWIDDLES, F32)),
    )


def gather_weights(w_in, ctx):
    core = ctx % 2
    halves = w_in.transpose(1, 0, 2).reshape(3, 64, 2, 128)
    keep = lax.dynamic_index_in_dim(halves, core, 2, False)
    got = lax.ppermute(lax.dynamic_index_in_dim(halves, 1 - core, 2, False), "ctx", PERM_CORE)
    near = jnp.concatenate(
        [jnp.where(core == 0, keep, got), jnp.where(core == 0, got, keep)], axis=1
    ).reshape(384, 128)
    far = lax.ppermute(near, "ctx", PERM_Z)

    near = lax.all_to_all(
        jnp.broadcast_to(near, (4, 384, 128)), "ctx", 0, 0, axis_index_groups=GROUPS_X, tiled=True
    )
    near, far = lax.optimization_barrier((near, far))
    near = jnp.broadcast_to(near.reshape(1, 1536, 128), (4, 1536, 128))
    near = lax.all_to_all(near, "ctx", 0, 0, axis_index_groups=GROUPS_Y, tiled=True)

    along_y = jnp.stack([far] + [lax.ppermute(far, "ctx", PERM_Y[k]) for k in (1, 2, 3)])
    fars = [along_y] + [lax.ppermute(along_y, "ctx", PERM_X[k]) for k in (1, 2, 3)]
    return near, fars, got


def gather_filter(long_filter, ctx):
    core = ctx % 2
    taps = long_filter.reshape(256, 2, 128)
    keep = lax.dynamic_index_in_dim(taps, core, 1, False)
    got = lax.ppermute(lax.dynamic_index_in_dim(taps, 1 - core, 1, False), "ctx", PERM_CORE)
    taps = by_position(keep, got, core).reshape(2, 2, 128, 16, 8).transpose(3, 0, 1, 4, 2).reshape(16, 32, 128)
    return jnp.concatenate([taps, lax.ppermute(taps, "ctx", PERM_Z_UP)], axis=1)


def output_weights(w_out, w_unembed, near):
    partial = mm(w_out, w_unembed).astype(BF16).reshape(4, 1, 8, 4, 128).transpose(0, 1, 3, 2, 4)
    partial = jnp.broadcast_to(partial.reshape(4, 1, 32, 128), (4, 2, 32, 128)).reshape(8, 32, 128)
    partial, _ = lax.optimization_barrier((partial, near))
    partial = lax.all_to_all(partial, "tp", 0, 0, tiled=True)
    return jnp.sum(partial.astype(F32), axis=0).astype(BF16)


def per_device(tokens_in, pre_gain, w_in, w_out, long_filter, w_unembed, target_ids, score_mask):
    ctx, tp = lax.axis_index("ctx"), lax.axis_index("tp")
    core, z = ctx % 2, ctx // 32
    z_at = z.reshape(1).astype(jnp.int32)
    near, fars, first = gather_weights(w_in, ctx)
    tokens_in, long_filter, w_out, _ = lax.optimization_barrier((tokens_in, long_filter, w_out, first))
    taps = gather_filter(long_filter, ctx)
    piece = output_weights(w_out, w_unembed, near)

    stream = tokens_in.astype(F32)
    scale = lax.rsqrt(jnp.mean(stream * stream, axis=1, keepdims=True) + NORM_EPS)
    normed = (stream * scale * pre_gain.astype(F32)).astype(BF16)
    beside = lax.ppermute(normed, "ctx", PERM_CORE)

    at = jnp.stack([(ctx // 8) % 4, (ctx // 2) % 4, core, z]).astype(jnp.int32)
    sums = call(
        near_kernel, shape((2, 256, 384), F32), [SCALARS] + whole(3), [], 8 * 10**8, (at, normed, beside, near)
    )
    signal, gate = call(
        proj_kernel,
        (shape((16, 96, 128), BF16), shape((2, 2, 128, 128), BF16)),
        [SCALARS] + whole(8),
        [],
        8 * 10**8,
        (at, normed, beside, sums, taps, *fars),
    )
    signal, piece = lax.optimization_barrier((signal, piece))
    piece = lax.ppermute(piece, ("ctx", "tp"), ROUTE)
    got = lax.all_to_all(signal, "ctx", 0, 0, axis_index_groups=GROUPS_CORE, tiled=True)
    signal = got[:, :32].reshape(512, 128)
    before = lax.ppermute(signal, "ctx", PERM_Z_UP)
    gate_keep = lax.dynamic_index_in_dim(gate, core, 0, False)
    gate_got = lax.ppermute(lax.dynamic_index_in_dim(gate, 1 - core, 0, False), "ctx", PERM_CORE)

    spectra = filter_spectra(z_at, got)
    conv = convolve(z_at, signal, before, *spectra, piece)
    conv = lax.all_to_all(conv, "ctx", 0, 0, axis_index_groups=GROUPS_PLANE, tiled=True)

    width = w_unembed.shape[0]
    base = mm(lax.dynamic_slice_in_dim(tokens_in, tp * width, width, 1), w_unembed)
    logits = call(
        mix_kernel,
        shape((256, 512), BF16),
        [SCALARS] + whole(4),
        [],
        10**8,
        (core.reshape(1).astype(jnp.int32), conv, gate_keep, gate_got, base),
    )
    logits = lax.all_to_all(logits.reshape(4, 64, 512), "tp", 0, 0, axis_index_groups=GROUPS_TP, tiled=True)
    logits = jnp.sum(logits.astype(F32), axis=0).astype(BF16)
    far = lax.ppermute(logits, "tp", [(i, i ^ 4) for i in range(8)])
    logits = logits.astype(F32) + far.astype(F32)

    row_top = jnp.max(logits, axis=1, keepdims=True)
    log_total = row_top[:, 0] + jnp.log(jnp.sum(jnp.exp(logits - row_top), axis=1))
    ids = lax.dynamic_slice_in_dim(target_ids, (tp % 4) * 64, 64, 0)
    vocab_index = lax.broadcasted_iota(jnp.int32, (64, 512), 1)
    picked = jnp.sum(jnp.where(vocab_index == ids[:, None], logits, 0.0), axis=1)
    scores = jnp.broadcast_to((picked - log_total)[None, None, :], (4, 8, 64))
    scores = lax.all_to_all(scores, "tp", 0, 0, axis_index_groups=GROUPS_TP, tiled=True)
    return scores[:, 0].reshape(256) * score_mask.astype(F32)


def solution(mesh):
    return jax.shard_map(
        per_device,
        mesh=mesh,
        in_specs=(
            P("ctx", None),
            P(),
            P("ctx", None, "tp"),
            P("ctx", "tp"),
            P("ctx", "tp"),
            P("tp", None),
            P("ctx"),
            P("ctx"),
        ),
        out_specs=P("ctx"),
        check_vma=False,
    )
```

```python
import math

import jax
import jax.numpy as jnp
import numpy as np
from jax import lax
from jax.experimental import pallas as pl
from jax.experimental.pallas import tpu as pltpu
from jax.sharding import PartitionSpec as P

NORM_EPS = 1e-05
F32 = jnp.float32
BF16 = jnp.bfloat16

COORDS = [(z, y, x, c) for z in range(2) for y in range(4) for x in range(4) for c in range(2)]


def ctx_id(z, y, x, c):
    return ((z * 4 + y) * 4 + x) * 2 + c


def ctx_perm(move):
    return [(ctx_id(*at), ctx_id(*move(*at))) for at in COORDS]


PERM_CORE = ctx_perm(lambda z, y, x, c: (z, y, x, 1 - c))
PERM_Z = ctx_perm(lambda z, y, x, c: (1 - z, y, x, c))
PERM_Z_UP = [(i, i + 32) for i in range(32)]
PERM_X = [ctx_perm(lambda z, y, x, c, k=k: (z, y, (x + k) % 4, c)) for k in range(4)]
PERM_Y = [ctx_perm(lambda z, y, x, c, k=k: (z, (y + k) % 4, x, c)) for k in range(4)]
GROUPS_X = [[ctx_id(z, y, x, c) for x in range(4)] for z in range(2) for y in range(4) for c in range(2)]
GROUPS_Y = [[ctx_id(z, y, x, c) for y in range(4)] for z in range(2) for x in range(4) for c in range(2)]
GROUPS_PLANE = [
    [ctx_id(z, y, x, c) for y in range(4) for x in range(4) for c in range(2)] for z in range(2)
]
GROUPS_CORE = [
    [ctx_id(z, y, x, c) for y in range(4) for x in range(4)] for z in range(2) for c in range(2)
]
GROUPS_TP = [[0, 1, 2, 3], [4, 5, 6, 7]]


def weight_route():
    pairs = []
    for i in range(64):
        for j in range(8):
            plane, core, chip, z = i // 8, (i % 8) // 4, (i % 4) * 4 + j // 2, j % 2
            pairs.append((i * 8 + j, (z * 32 + chip * 2 + core) * 8 + plane))
    return pairs


ROUTE = weight_route()


def tables():
    index = np.arange(128)
    inner = 2.0 * math.pi * (np.outer(index, index) % 128) / 128
    outer = 2.0 * math.pi * np.outer(index, index) / 16384
    cos, sin = np.cos(inner), np.sin(inner)
    first = np.concatenate([cos[:, :64], -sin[:, :64]], axis=0)
    second = np.block([[cos, -sin], [sin, cos]])
    back = np.block([[cos, sin], [-sin, cos]])
    last = np.concatenate([cos[:64], -sin[:64]], axis=1) / 16384.0
    return (first, second, back, last, np.cos(outer), np.sin(outer))


FIRST, SECOND, BACK, LAST, COS_TW, SIN_TW = tables()
MATRICES = np.concatenate([np.pad(FIRST, ((0, 0), (0, 192))), SECOND, BACK, LAST])
TWIDDLES = np.concatenate([COS_TW, SIN_TW], axis=1)


def mm(left, right):
    return jnp.dot(left, right, preferred_element_type=F32)


def whole(count):
    return [pl.BlockSpec(memory_space=pltpu.VMEM)] * count


SCALARS = pl.BlockSpec(memory_space=pltpu.SMEM)


def spectrum(scratch, matrices, twiddles):
    cos_tw, sin_tw = twiddles[:, :128], twiddles[:, 128:]
    cube = jnp.concatenate([scratch[pl.ds(c, 64, stride=8), :] for c in range(8)], axis=1)
    step = mm(matrices[:256, :64], cube.astype(BF16))
    parts = []
    for c in range(8):
        real, imag = step[:128, c * 128 : c * 128 + 128], step[128:, c * 128 : c * 128 + 128]
        parts.append(
            jnp.concatenate(
                [(real * cos_tw + imag * sin_tw).astype(BF16), (imag * cos_tw - real * sin_tw).astype(BF16)],
                axis=1,
            )
        )
    return mm(jnp.concatenate(parts, axis=0), matrices[256:512, :])


def filter_kernel(z_ref, got_ref, matrices, twiddles, low_ref, all_ref, scratch):
    upper = z_ref[0] == 1
    for p in range(16):
        scratch[p * 32 : p * 32 + 32] = got_ref[p, 32:64].astype(F32)
    high = spectrum(scratch, matrices, twiddles)
    for p in range(16):
        scratch[p * 32 : p * 32 + 32] = jnp.where(upper, got_ref[p, 64:].astype(F32), got_ref[p, 32:64].astype(F32))
    low = spectrum(scratch, matrices, twiddles)
    odd = lax.broadcasted_iota(jnp.int32, (1024, 256), 0) & 1
    low_ref[...] = low
    all_ref[...] = jnp.where(odd == 1, -low, low) + high


def conv_kernel(z_ref, sig_ref, before_ref, low_ref, all_ref, piece_ref, matrices, twiddles, out_ref, scratch):
    cos_tw, sin_tw = twiddles[:, :128], twiddles[:, 128:]
    scratch[...] = sig_ref[...].astype(F32)
    own = spectrum(scratch, matrices, twiddles)
    scratch[...] = jnp.where(z_ref[0] == 1, before_ref[...].astype(F32), 0.0)
    old = spectrum(scratch, matrices, twiddles)
    low, every = low_ref[...], all_ref[...]
    own_r, own_i, old_r, old_i = own[:, :128], own[:, 128:], old[:, :128], old[:, 128:]
    low_r, low_i, all_r, all_i = low[:, :128], low[:, 128:], every[:, :128], every[:, 128:]
    real = own_r * low_r - own_i * low_i + old_r * all_r - old_i * all_i
    imag = own_r * low_i + own_i * low_r + old_r * all_i + old_i * all_r
    half = mm(jnp.concatenate([real.astype(BF16), imag.astype(BF16)], axis=1), matrices[512:768, :])
    parts = []
    for c in range(8):
        real, imag = half[c * 128 : c * 128 + 128, :128], half[c * 128 : c * 128 + 128, 128:]
        parts.append(
            jnp.concatenate(
                [(real * cos_tw - imag * sin_tw).astype(BF16), (imag * cos_tw + real * sin_tw).astype(BF16)],
                axis=0,
            )
        )
    result = mm(matrices[768:, :], jnp.concatenate(parts, axis=1))
    for c in range(8):
        scratch[pl.ds(c, 64, stride=8), :] = result[:, c * 128 : c * 128 + 128]
    piece = piece_ref[...]
    for d in range(32):
        out_ref[d, :16] = scratch[d * 16 : d * 16 + 16].astype(BF16)
        out_ref[d, 16:] = piece


def weight_block(ref, lead, row):
    return jnp.concatenate([ref[lead, row + 128 * g : row + 128 * g + 128, :] for g in range(3)], axis=1)


def columns(ref, start, count):
    return ref[:, pl.ds(pl.multiple_of(start, 128), count)]


def near_kernel(at_ref, own_ref, beside_ref, near_ref, out_ref):
    start = at_ref[3] * 2048
    for part, tokens in enumerate((own_ref, beside_ref)):
        total = jnp.zeros((256, 384), F32)
        for y in range(4):
            for x in (0, 2):
                left = columns(tokens, start + (y * 4 + x) * 128, 256)
                right = [weight_block(near_ref, y, x * 384), weight_block(near_ref, y, x * 384 + 384)]
                total += mm(left, jnp.concatenate(right, axis=0))
        out_ref[part] = total


def proj_kernel(at_ref, own_ref, beside_ref, near_ref, taps_ref, f0, f1, f2, f3, sig_ref, gate_ref):
    y_at, x_at, core = at_ref[0], at_ref[1], at_ref[2]
    start = 2048 - at_ref[3] * 2048
    for part, tokens in enumerate((own_ref, beside_ref)):
        total = near_ref[part]
        for step, ref in enumerate((f0, f1, f2, f3)):
            x = lax.rem(x_at + 4 - step, 4)
            for k in (0, 2):
                left = [columns(tokens, start + (lax.rem(y_at + 4 - j, 4) * 4 + x) * 128, 128) for j in (k, k + 1)]
                right = [weight_block(ref, k, 0), weight_block(ref, k + 1, 0)]
                total += mm(jnp.concatenate(left, axis=1), jnp.concatenate(right, axis=0))
        proj = total.astype(BF16).astype(F32)
        gated = proj[:, 128:256] * proj[:, 256:]
        place = core if part == 0 else 1 - core
        first, second = gated[:128].T, gated[128:].T
        for p in range(16):
            rows = jnp.concatenate([first[p * 8 : p * 8 + 8], second[p * 8 : p * 8 + 8]], axis=0).astype(BF16)
            sig_ref[p, pl.ds(pl.multiple_of(place * 16, 16), 16), :] = rows
        gate_ref[place, 0] = proj[:128, :128].T.astype(BF16)
        gate_ref[place, 1] = proj[128:, :128].T.astype(BF16)
    for p in range(16):
        sig_ref[p, 32:, :] = taps_ref[p]


def mix_kernel(core_ref, got_ref, keep_ref, other_ref, base_ref, out_ref):
    core = core_ref[0]
    keep, other = keep_ref[...].astype(F32), other_ref[...].astype(F32)
    conv = got_ref[:, :16, :].astype(F32)
    for rb in range(2):
        total = base_ref[rb * 128 : rb * 128 + 128, :]
        for c in range(2):
            cube = jnp.concatenate([conv[p * 2 + c, rb * 8 : rb * 8 + 8] for p in range(16)], axis=0)
            gate = jnp.where(core == c, keep[rb], other[rb])
            mixed = (gate * cube).T.astype(BF16)
            weights = []
            for p in range(16):
                piece = got_ref[p * 2 + c, 16:, :].astype(F32)
                weights.append(jnp.concatenate([piece[v * 8 : v * 8 + 8] for v in range(4)], axis=1))
            total += mm(mixed, jnp.concatenate(weights, axis=0).astype(BF16))
        out_ref[rb * 128 : rb * 128 + 128, :] = total.astype(BF16)


def call(kernel, outs, specs, scratch, flops, args):
    return pl.pallas_call(
        kernel,
        out_shape=outs,
        in_specs=specs,
        out_specs=jax.tree.map(lambda _: pl.BlockSpec(memory_space=pltpu.VMEM), outs),
        scratch_shapes=scratch,
        compiler_params=pltpu.CompilerParams(vmem_limit_bytes=40 * 2**20),
        cost_estimate=pl.CostEstimate(flops=flops, bytes_accessed=4 * 2**20, transcendentals=0),
    )(*args)


def shape(dims, dtype):
    return jax.ShapeDtypeStruct(dims, dtype)


def by_position(own, other, place):
    return jnp.where(place == 0, jnp.stack([own, other]), jnp.stack([other, own]))


def filter_spectra(z, got):
    return call(
        filter_kernel,
        (shape((1024, 256), F32), shape((1024, 256), F32)),
        [SCALARS] + whole(3),
        [pltpu.VMEM((512, 128), F32)],
        4 * 10**8,
        (z, got, jnp.asarray(MATRICES, BF16), jnp.asarray(TWIDDLES, F32)),
    )


def convolve(z, signal, before, low, every, piece):
    return call(
        conv_kernel,
        shape((32, 48, 128), BF16),
        [SCALARS] + whole(7),
        [pltpu.VMEM((512, 128), F32)],
        6 * 10**8,
        (z, signal, before, low, every, piece, jnp.asarray(MATRICES, BF16), jnp.asarray(TWIDDLES, F32)),
    )


def halves_of(array, axis, core):
    keep = lax.dynamic_slice_in_dim(array, core * 128, 128, axis)
    return keep, lax.dynamic_slice_in_dim(array, 128 - core * 128, 128, axis)


def product(w_out, w_unembed):
    partial = mm(w_out, w_unembed).astype(BF16).reshape(4, 1, 8, 4, 128).transpose(0, 1, 3, 2, 4)
    return jnp.broadcast_to(partial.reshape(4, 1, 32, 128), (4, 2, 32, 128)).reshape(8, 32, 128)


def filter_pieces(own, low, core):
    keep, give = halves_of(jnp.stack([own, low]), 2, core)
    taps = by_position(keep, lax.ppermute(give, "ctx", PERM_CORE), core)
    return taps.reshape(2, 2, 2, 128, 16, 8).transpose(4, 1, 0, 2, 5, 3).reshape(16, 64, 128)


def norm_kernel(tokens_ref, gain_ref, out_ref):
    stream = tokens_ref[...].astype(F32)
    scale = lax.rsqrt(jnp.mean(stream * stream, axis=1, keepdims=True) + NORM_EPS)
    out_ref[...] = (stream * scale * gain_ref[...].astype(F32)).astype(BF16)


def norm(tokens, gain):
    return pl.pallas_call(
        norm_kernel,
        out_shape=shape((256, 4096), BF16),
        grid=(4,),
        in_specs=[pl.BlockSpec((64, 4096), lambda i: (i, 0)), pl.BlockSpec((1, 4096), lambda i: (0, 0))],
        out_specs=pl.BlockSpec((64, 4096), lambda i: (i, 0)),
        cost_estimate=pl.CostEstimate(flops=5 * 2**20, bytes_accessed=4 * 2**20, transcendentals=256),
    )(tokens, gain.reshape(1, 4096))


def per_device(tokens_in, pre_gain, w_in, w_out, long_filter, w_unembed, target_ids, score_mask):
    ctx, tp = lax.axis_index("ctx"), lax.axis_index("tp")
    core, z = ctx % 2, ctx // 32
    z_at = z.reshape(1).astype(jnp.int32)

    keep, give = halves_of(w_in.transpose(1, 0, 2), 2, core)
    got = lax.ppermute(give, "ctx", PERM_CORE)
    near = jnp.concatenate([jnp.where(core == 0, keep, got), jnp.where(core == 0, got, keep)], axis=1)
    near = near.reshape(384, 128)
    far = lax.ppermute(near, "ctx", PERM_Z)
    low_taps = lax.ppermute(long_filter, "ctx", PERM_Z_UP)
    terms = lax.all_to_all(product(w_out, w_unembed), "tp", 0, 0, tiled=True)
    near, far, low_taps, terms, tokens_in = lax.optimization_barrier((near, far, low_taps, terms, tokens_in))

    near = lax.all_to_all(
        jnp.broadcast_to(near, (4, 384, 128)), "ctx", 0, 0, axis_index_groups=GROUPS_X, tiled=True
    )
    far = jnp.stack([far] + [lax.ppermute(far, "ctx", PERM_Y[k]) for k in (1, 2, 3)])
    near, far, low_taps, terms, tokens_in = lax.optimization_barrier((near, far, low_taps, terms, tokens_in))

    near = jnp.broadcast_to(near.reshape(1, 1536, 128), (4, 1536, 128))
    near = lax.all_to_all(near, "ctx", 0, 0, axis_index_groups=GROUPS_Y, tiled=True)
    fars = [far] + [lax.ppermute(far, "ctx", PERM_X[k]) for k in (1, 2, 3)]
    normed = norm(tokens_in, pre_gain)
    beside = lax.ppermute(normed, "ctx", PERM_CORE)
    piece = lax.ppermute(jnp.sum(terms.astype(F32), axis=0).astype(BF16), ("ctx", "tp"), ROUTE)
    taps = filter_pieces(long_filter, low_taps, core)

    at = jnp.stack([(ctx // 8) % 4, (ctx // 2) % 4, core, z]).astype(jnp.int32)
    sums = call(
        near_kernel, shape((2, 256, 384), F32), [SCALARS] + whole(3), [], 8 * 10**8, (at, normed, beside, near)
    )
    signal, gate = call(
        proj_kernel,
        (shape((16, 96, 128), BF16), shape((2, 2, 128, 128), BF16)),
        [SCALARS] + whole(8),
        [],
        8 * 10**8,
        (at, normed, beside, sums, taps, *fars),
    )
    got = lax.all_to_all(signal, "ctx", 0, 0, axis_index_groups=GROUPS_CORE, tiled=True)
    signal = got[:, :32].reshape(512, 128)
    before = lax.ppermute(signal, "ctx", PERM_Z_UP)
    gate_keep = lax.dynamic_index_in_dim(gate, core, 0, False)
    gate_got = lax.ppermute(lax.dynamic_index_in_dim(gate, 1 - core, 0, False), "ctx", PERM_CORE)

    spectra = filter_spectra(z_at, got)
    conv = convolve(z_at, signal, before, *spectra, piece)
    conv = lax.all_to_all(conv, "ctx", 0, 0, axis_index_groups=GROUPS_PLANE, tiled=True)

    width = w_unembed.shape[0]
    base = mm(lax.dynamic_slice_in_dim(tokens_in, tp * width, width, 1), w_unembed)
    logits = call(
        mix_kernel,
        shape((256, 512), BF16),
        [SCALARS] + whole(4),
        [],
        10**8,
        (core.reshape(1).astype(jnp.int32), conv, gate_keep, gate_got, base),
    )
    logits = lax.all_to_all(logits.reshape(4, 64, 512), "tp", 0, 0, axis_index_groups=GROUPS_TP, tiled=True)
    logits = jnp.sum(logits.astype(F32), axis=0).astype(BF16)
    far = lax.ppermute(logits, "tp", [(i, i ^ 4) for i in range(8)])
    logits = logits.astype(F32) + far.astype(F32)

    row_top = jnp.max(logits, axis=1, keepdims=True)
    log_total = row_top[:, 0] + jnp.log(jnp.sum(jnp.exp(logits - row_top), axis=1))
    ids = lax.dynamic_slice_in_dim(target_ids, (tp % 4) * 64, 64, 0)
    mask = lax.dynamic_slice_in_dim(score_mask, (tp % 4) * 64, 64, 0)
    vocab_index = lax.broadcasted_iota(jnp.int32, (64, 512), 1)
    picked = jnp.sum(jnp.where(vocab_index == ids[:, None], logits, 0.0), axis=1)
    scores = (picked - log_total) * mask.astype(F32)
    scores = jnp.broadcast_to(scores[None, :], (4, 64))
    scores = lax.all_to_all(scores, "tp", 0, 0, axis_index_groups=GROUPS_TP, tiled=True)
    return scores.reshape(256)


def solution(mesh):
    return jax.shard_map(
        per_device,
        mesh=mesh,
        in_specs=(
            P("ctx", None),
            P(),
            P("ctx", None, "tp"),
            P("ctx", "tp"),
            P("ctx", "tp"),
            P("tp", None),
            P("ctx"),
            P("ctx"),
        ),
        out_specs=P("ctx"),
        check_vma=False,
    )
```

```python
import math

import jax
import jax.numpy as jnp
import numpy as np
from jax import lax
from jax.experimental import pallas as pl
from jax.experimental.pallas import tpu as pltpu
from jax.sharding import PartitionSpec as P

NORM_EPS = 1e-05
F32 = jnp.float32
BF16 = jnp.bfloat16

COORDS = [(z, y, x, c) for z in range(2) for y in range(4) for x in range(4) for c in range(2)]


def ctx_id(z, y, x, c):
    return ((z * 4 + y) * 4 + x) * 2 + c


def ctx_perm(move):
    return [(ctx_id(*at), ctx_id(*move(*at))) for at in COORDS]


PERM_CORE = ctx_perm(lambda z, y, x, c: (z, y, x, 1 - c))
PERM_Z = ctx_perm(lambda z, y, x, c: (1 - z, y, x, c))
PERM_Z_UP = [(i, i + 32) for i in range(32)]
PERM_X = [ctx_perm(lambda z, y, x, c, k=k: (z, y, (x + k) % 4, c)) for k in range(4)]
PERM_Y = [ctx_perm(lambda z, y, x, c, k=k: (z, (y + k) % 4, x, c)) for k in range(4)]
GROUPS_X = [[ctx_id(z, y, x, c) for x in range(4)] for z in range(2) for y in range(4) for c in range(2)]
GROUPS_Y = [[ctx_id(z, y, x, c) for y in range(4)] for z in range(2) for x in range(4) for c in range(2)]
GROUPS_PLANE = [
    [ctx_id(z, y, x, c) for y in range(4) for x in range(4) for c in range(2)] for z in range(2)
]
GROUPS_CORE = [
    [ctx_id(z, y, x, c) for y in range(4) for x in range(4)] for z in range(2) for c in range(2)
]
GROUPS_TP = [[0, 1, 2, 3], [4, 5, 6, 7]]


def weight_route():
    pairs = []
    for i in range(64):
        for j in range(8):
            plane, core, chip, z = i // 8, (i % 8) // 4, (i % 4) * 4 + j // 2, j % 2
            pairs.append((i * 8 + j, (z * 32 + chip * 2 + core) * 8 + plane))
    return pairs


ROUTE = weight_route()


def tables():
    index = np.arange(128)
    inner = 2.0 * math.pi * (np.outer(index, index) % 128) / 128
    outer = 2.0 * math.pi * np.outer(index, index) / 16384
    cos, sin = np.cos(inner), np.sin(inner)
    first = np.concatenate([cos[:, :64], -sin[:, :64]], axis=0)
    second = np.block([[cos, -sin], [sin, cos]])
    back = np.block([[cos, sin], [-sin, cos]])
    last = np.concatenate([cos[:64], -sin[:64]], axis=1) / 16384.0
    return (first, second, back, last, np.cos(outer), np.sin(outer))


FIRST, SECOND, BACK, LAST, COS_TW, SIN_TW = tables()
MATRICES = np.concatenate([np.pad(FIRST, ((0, 0), (0, 192))), SECOND, BACK, LAST])
TWIDDLES = np.concatenate([COS_TW, SIN_TW], axis=1)


def mm(left, right):
    return jnp.dot(left, right, preferred_element_type=F32)


def whole(count):
    return [pl.BlockSpec(memory_space=pltpu.VMEM)] * count


SCALARS = pl.BlockSpec(memory_space=pltpu.SMEM)


def spectrum(scratch, matrices, twiddles):
    cos_tw, sin_tw = twiddles[:, :128], twiddles[:, 128:]
    cube = jnp.concatenate([scratch[pl.ds(c, 64, stride=8), :] for c in range(8)], axis=1)
    step = mm(matrices[:256, :64], cube.astype(BF16))
    parts = []
    for c in range(8):
        real, imag = step[:128, c * 128 : c * 128 + 128], step[128:, c * 128 : c * 128 + 128]
        parts.append(
            jnp.concatenate(
                [(real * cos_tw + imag * sin_tw).astype(BF16), (imag * cos_tw - real * sin_tw).astype(BF16)],
                axis=1,
            )
        )
    return mm(jnp.concatenate(parts, axis=0), matrices[256:512, :])


def filter_kernel(z_ref, got_ref, matrices, twiddles, low_ref, all_ref, scratch):
    upper = z_ref[0] == 1
    for p in range(16):
        scratch[p * 32 : p * 32 + 32] = got_ref[p, 32:64].astype(F32)
    high = spectrum(scratch, matrices, twiddles)
    for p in range(16):
        scratch[p * 32 : p * 32 + 32] = jnp.where(upper, got_ref[p, 64:].astype(F32), got_ref[p, 32:64].astype(F32))
    low = spectrum(scratch, matrices, twiddles)
    odd = lax.broadcasted_iota(jnp.int32, (1024, 256), 0) & 1
    low_ref[...] = low
    all_ref[...] = jnp.where(odd == 1, -low, low) + high


def conv_kernel(z_ref, sig_ref, before_ref, low_ref, all_ref, piece_ref, matrices, twiddles, out_ref, scratch):
    cos_tw, sin_tw = twiddles[:, :128], twiddles[:, 128:]
    scratch[...] = sig_ref[...].astype(F32)
    own = spectrum(scratch, matrices, twiddles)
    scratch[...] = jnp.where(z_ref[0] == 1, before_ref[...].astype(F32), 0.0)
    old = spectrum(scratch, matrices, twiddles)
    low, every = low_ref[...], all_ref[...]
    own_r, own_i, old_r, old_i = own[:, :128], own[:, 128:], old[:, :128], old[:, 128:]
    low_r, low_i, all_r, all_i = low[:, :128], low[:, 128:], every[:, :128], every[:, 128:]
    real = own_r * low_r - own_i * low_i + old_r * all_r - old_i * all_i
    imag = own_r * low_i + own_i * low_r + old_r * all_i + old_i * all_r
    half = mm(jnp.concatenate([real.astype(BF16), imag.astype(BF16)], axis=1), matrices[512:768, :])
    parts = []
    for c in range(8):
        real, imag = half[c * 128 : c * 128 + 128, :128], half[c * 128 : c * 128 + 128, 128:]
        parts.append(
            jnp.concatenate(
                [(real * cos_tw - imag * sin_tw).astype(BF16), (imag * cos_tw + real * sin_tw).astype(BF16)],
                axis=0,
            )
        )
    result = mm(matrices[768:, :], jnp.concatenate(parts, axis=1))
    for c in range(8):
        scratch[pl.ds(c, 64, stride=8), :] = result[:, c * 128 : c * 128 + 128]
    piece = piece_ref[...]
    for d in range(32):
        out_ref[d, :16] = scratch[d * 16 : d * 16 + 16].astype(BF16)
        out_ref[d, 16:] = piece


def weight_block(ref, lead, row):
    return jnp.concatenate([ref[lead, row + 128 * g : row + 128 * g + 128, :] for g in range(3)], axis=1)


def near_kernel(at_ref, own_ref, beside_ref, gain_ref, near_ref, normed_ref, out_ref):
    start = at_ref[3] * 2048
    gain = gain_ref[...].astype(F32)
    for part, tokens in enumerate((own_ref, beside_ref)):

        @pl.loop(0, 8)
        def _(i):
            rows = pl.ds(pl.multiple_of(i * 32, 32), 32)
            stream = tokens[rows, :].astype(F32)
            scale = lax.rsqrt(jnp.mean(stream * stream, axis=1, keepdims=True) + NORM_EPS)
            normed_ref[part, rows, :] = (stream * scale * gain).astype(BF16)

        total = jnp.zeros((256, 384), F32)
        for y in range(4):
            for x in (0, 2):
                left = normed_ref[part, :, pl.ds(pl.multiple_of(start + (y * 4 + x) * 128, 128), 256)]
                right = [weight_block(near_ref, y, x * 384), weight_block(near_ref, y, x * 384 + 384)]
                total += mm(left, jnp.concatenate(right, axis=0))
        out_ref[part] = total


def proj_kernel(at_ref, normed_ref, near_ref, taps_ref, f0, f1, f2, f3, sig_ref, gate_ref):
    y_at, x_at, core = at_ref[0], at_ref[1], at_ref[2]
    start = 2048 - at_ref[3] * 2048
    for part in range(2):
        total = near_ref[part]
        for step, ref in enumerate((f0, f1, f2, f3)):
            x = lax.rem(x_at + 4 - step, 4)
            for k in (0, 2):
                starts = [start + (lax.rem(y_at + 4 - j, 4) * 4 + x) * 128 for j in (k, k + 1)]
                left = [normed_ref[part, :, pl.ds(pl.multiple_of(at, 128), 128)] for at in starts]
                right = [weight_block(ref, k, 0), weight_block(ref, k + 1, 0)]
                total += mm(jnp.concatenate(left, axis=1), jnp.concatenate(right, axis=0))
        proj = total.astype(BF16).astype(F32)
        gated = proj[:, 128:256] * proj[:, 256:]
        place = core if part == 0 else 1 - core
        first, second = gated[:128].T, gated[128:].T
        for p in range(16):
            rows = jnp.concatenate([first[p * 8 : p * 8 + 8], second[p * 8 : p * 8 + 8]], axis=0).astype(BF16)
            sig_ref[p, pl.ds(pl.multiple_of(place * 16, 16), 16), :] = rows
        gate_ref[place, 0] = proj[:128, :128].T.astype(BF16)
        gate_ref[place, 1] = proj[128:, :128].T.astype(BF16)
    for p in range(16):
        sig_ref[p, 32:, :] = taps_ref[p]


def mix_kernel(core_ref, got_ref, keep_ref, other_ref, base_ref, out_ref):
    core = core_ref[0]
    keep, other = keep_ref[...].astype(F32), other_ref[...].astype(F32)
    conv = got_ref[:, :16, :].astype(F32)
    for rb in range(2):
        total = base_ref[rb * 128 : rb * 128 + 128, :]
        for c in range(2):
            cube = jnp.concatenate([conv[p * 2 + c, rb * 8 : rb * 8 + 8] for p in range(16)], axis=0)
            gate = jnp.where(core == c, keep[rb], other[rb])
            mixed = (gate * cube).T.astype(BF16)
            weights = []
            for p in range(16):
                piece = got_ref[p * 2 + c, 16:, :].astype(F32)
                weights.append(jnp.concatenate([piece[v * 8 : v * 8 + 8] for v in range(4)], axis=1))
            total += mm(mixed, jnp.concatenate(weights, axis=0).astype(BF16))
        out_ref[rb * 128 : rb * 128 + 128, :] = total.astype(BF16)


def call(kernel, outs, specs, scratch, flops, args):
    return pl.pallas_call(
        kernel,
        out_shape=outs,
        in_specs=specs,
        out_specs=jax.tree.map(lambda _: pl.BlockSpec(memory_space=pltpu.VMEM), outs),
        scratch_shapes=scratch,
        compiler_params=pltpu.CompilerParams(vmem_limit_bytes=40 * 2**20),
        cost_estimate=pl.CostEstimate(flops=flops, bytes_accessed=4 * 2**20, transcendentals=0),
    )(*args)


def shape(dims, dtype):
    return jax.ShapeDtypeStruct(dims, dtype)


def by_position(own, other, place):
    return jnp.where(place == 0, jnp.stack([own, other]), jnp.stack([other, own]))


def filter_spectra(z, got):
    return call(
        filter_kernel,
        (shape((1024, 256), F32), shape((1024, 256), F32)),
        [SCALARS] + whole(3),
        [pltpu.VMEM((512, 128), F32)],
        4 * 10**8,
        (z, got, jnp.asarray(MATRICES, BF16), jnp.asarray(TWIDDLES, F32)),
    )


def convolve(z, signal, before, low, every, piece):
    return call(
        conv_kernel,
        shape((32, 48, 128), BF16),
        [SCALARS] + whole(7),
        [pltpu.VMEM((512, 128), F32)],
        6 * 10**8,
        (z, signal, before, low, every, piece, jnp.asarray(MATRICES, BF16), jnp.asarray(TWIDDLES, F32)),
    )


def halves_of(array, axis, core):
    keep = lax.dynamic_slice_in_dim(array, core * 128, 128, axis)
    return keep, lax.dynamic_slice_in_dim(array, 128 - core * 128, 128, axis)


def product(w_out, w_unembed):
    partial = mm(w_out, w_unembed).astype(BF16).reshape(4, 1, 8, 4, 128).transpose(0, 1, 3, 2, 4)
    return jnp.broadcast_to(partial.reshape(4, 1, 32, 128), (4, 2, 32, 128)).reshape(8, 32, 128)


def filter_pieces(own, low, core):
    keep, give = halves_of(jnp.stack([own, low]), 2, core)
    taps = by_position(keep, lax.ppermute(give, "ctx", PERM_CORE), core)
    return taps.reshape(2, 2, 2, 128, 16, 8).transpose(4, 1, 0, 2, 5, 3).reshape(16, 64, 128)


def per_device(tokens_in, pre_gain, w_in, w_out, long_filter, w_unembed, target_ids, score_mask):
    ctx, tp = lax.axis_index("ctx"), lax.axis_index("tp")
    core, z = ctx % 2, ctx // 32
    z_at = z.reshape(1).astype(jnp.int32)

    keep, give = halves_of(w_in.transpose(1, 0, 2), 2, core)
    got = lax.ppermute(give, "ctx", PERM_CORE)
    near = jnp.concatenate([jnp.where(core == 0, keep, got), jnp.where(core == 0, got, keep)], axis=1)
    near, filter_in, tokens = lax.optimization_barrier((near.reshape(384, 128), long_filter, tokens_in))
    far = lax.ppermute(near, "ctx", PERM_Z)
    low_taps = lax.ppermute(filter_in, "ctx", PERM_Z_UP)
    near = lax.all_to_all(
        jnp.broadcast_to(near, (4, 384, 128)), "ctx", 0, 0, axis_index_groups=GROUPS_X, tiled=True
    )
    near, far, low_taps, tokens = lax.optimization_barrier((near, far, low_taps, tokens))

    near = jnp.broadcast_to(near.reshape(1, 1536, 128), (4, 1536, 128))
    near = lax.all_to_all(near, "ctx", 0, 0, axis_index_groups=GROUPS_Y, tiled=True)
    far = jnp.stack([far] + [lax.ppermute(far, "ctx", PERM_Y[k]) for k in (1, 2, 3)])
    far, tokens, low_taps = lax.optimization_barrier((far, tokens, low_taps))

    fars = [far] + [lax.ppermute(far, "ctx", PERM_X[k]) for k in (1, 2, 3)]
    beside = lax.ppermute(tokens, "ctx", PERM_CORE)
    terms, near, low_taps = lax.optimization_barrier((product(w_out, w_unembed), near, low_taps))
    terms = lax.all_to_all(terms, "tp", 0, 0, tiled=True)
    taps = filter_pieces(long_filter, low_taps, core)

    at = jnp.stack([(ctx // 8) % 4, (ctx // 2) % 4, core, z]).astype(jnp.int32)
    normed, sums = call(
        near_kernel,
        (shape((2, 256, 4096), BF16), shape((2, 256, 384), F32)),
        [SCALARS] + whole(4),
        [],
        8 * 10**8,
        (at, tokens_in, beside, pre_gain.reshape(1, 4096), near),
    )
    signal, gate = call(
        proj_kernel,
        (shape((16, 96, 128), BF16), shape((2, 2, 128, 128), BF16)),
        [SCALARS] + whole(7),
        [],
        8 * 10**8,
        (at, normed, sums, taps, *fars),
    )
    signal, terms = lax.optimization_barrier((signal, terms))
    piece = lax.ppermute(jnp.sum(terms.astype(F32), axis=0).astype(BF16), ("ctx", "tp"), ROUTE)
    got = lax.all_to_all(signal, "ctx", 0, 0, axis_index_groups=GROUPS_CORE, tiled=True)
    signal = got[:, :32].reshape(512, 128)
    before = lax.ppermute(signal, "ctx", PERM_Z_UP)
    gate_keep = lax.dynamic_index_in_dim(gate, core, 0, False)
    gate_got = lax.ppermute(lax.dynamic_index_in_dim(gate, 1 - core, 0, False), "ctx", PERM_CORE)

    spectra = filter_spectra(z_at, got)
    conv = convolve(z_at, signal, before, *spectra, piece)
    conv = lax.all_to_all(conv, "ctx", 0, 0, axis_index_groups=GROUPS_PLANE, tiled=True)

    width = w_unembed.shape[0]
    base = mm(lax.dynamic_slice_in_dim(tokens_in, tp * width, width, 1), w_unembed)
    logits = call(
        mix_kernel,
        shape((256, 512), BF16),
        [SCALARS] + whole(4),
        [],
        10**8,
        (core.reshape(1).astype(jnp.int32), conv, gate_keep, gate_got, base),
    )
    logits = lax.all_to_all(logits.reshape(4, 64, 512), "tp", 0, 0, axis_index_groups=GROUPS_TP, tiled=True)
    logits = jnp.sum(logits.astype(F32), axis=0).astype(BF16)
    far = lax.ppermute(logits, "tp", [(i, i ^ 4) for i in range(8)])
    logits = logits.astype(F32) + far.astype(F32)

    row_top = jnp.max(logits, axis=1, keepdims=True)
    log_total = row_top[:, 0] + jnp.log(jnp.sum(jnp.exp(logits - row_top), axis=1))
    ids = lax.dynamic_slice_in_dim(target_ids, (tp % 4) * 64, 64, 0)
    mask = lax.dynamic_slice_in_dim(score_mask, (tp % 4) * 64, 64, 0)
    vocab_index = lax.broadcasted_iota(jnp.int32, (64, 512), 1)
    picked = jnp.sum(jnp.where(vocab_index == ids[:, None], logits, 0.0), axis=1)
    scores = (picked - log_total) * mask.astype(F32)
    scores = jnp.broadcast_to(scores[None, :], (4, 64))
    scores = lax.all_to_all(scores, "tp", 0, 0, axis_index_groups=GROUPS_TP, tiled=True)
    return scores.reshape(256)


def solution(mesh):
    return jax.shard_map(
        per_device,
        mesh=mesh,
        in_specs=(
            P("ctx", None),
            P(),
            P("ctx", None, "tp"),
            P("ctx", "tp"),
            P("ctx", "tp"),
            P("tp", None),
            P("ctx"),
            P("ctx"),
        ),
        out_specs=P("ctx"),
        check_vma=False,
    )
```

```python
import math

import jax
import jax.numpy as jnp
import numpy as np
from jax import lax
from jax.experimental import pallas as pl
from jax.experimental.pallas import tpu as pltpu
from jax.sharding import PartitionSpec as P

NORM_EPS = 1e-05
F32 = jnp.float32
BF16 = jnp.bfloat16

COORDS = [(z, y, x, c) for z in range(2) for y in range(4) for x in range(4) for c in range(2)]


def ctx_id(z, y, x, c):
    return ((z * 4 + y) * 4 + x) * 2 + c


def ctx_perm(move):
    return [(ctx_id(*at), ctx_id(*move(*at))) for at in COORDS]


PERM_CORE = ctx_perm(lambda z, y, x, c: (z, y, x, 1 - c))
PERM_Z = ctx_perm(lambda z, y, x, c: (1 - z, y, x, c))
PERM_Z_UP = [(i, i + 32) for i in range(32)]
PERM_X = [ctx_perm(lambda z, y, x, c, k=k: (z, y, (x + k) % 4, c)) for k in range(4)]
PERM_Y = [ctx_perm(lambda z, y, x, c, k=k: (z, (y + k) % 4, x, c)) for k in range(4)]
GROUPS_X = [[ctx_id(z, y, x, c) for x in range(4)] for z in range(2) for y in range(4) for c in range(2)]
GROUPS_Y = [[ctx_id(z, y, x, c) for y in range(4)] for z in range(2) for x in range(4) for c in range(2)]
GROUPS_PLANE = [
    [ctx_id(z, y, x, c) for y in range(4) for x in range(4) for c in range(2)] for z in range(2)
]
GROUPS_CORE = [
    [ctx_id(z, y, x, c) for y in range(4) for x in range(4)] for z in range(2) for c in range(2)
]
GROUPS_TP = [[0, 1, 2, 3], [4, 5, 6, 7]]


def weight_route():
    pairs = []
    for i in range(64):
        for j in range(8):
            plane, core, chip, z = i // 8, (i % 8) // 4, (i % 4) * 4 + j // 2, j % 2
            pairs.append((i * 8 + j, (z * 32 + chip * 2 + core) * 8 + plane))
    return pairs


ROUTE = weight_route()


def tables():
    index = np.arange(128)
    inner = 2.0 * math.pi * (np.outer(index, index) % 128) / 128
    outer = 2.0 * math.pi * np.outer(index, index) / 16384
    cos, sin = np.cos(inner), np.sin(inner)
    first = np.concatenate([cos[:, :64], -sin[:, :64]], axis=0)
    second = np.block([[cos, -sin], [sin, cos]])
    back = np.block([[cos, sin], [-sin, cos]])
    last = np.concatenate([cos[:64], -sin[:64]], axis=1) / 16384.0
    return (first, second, back, last, np.cos(outer), np.sin(outer))


FIRST, SECOND, BACK, LAST, COS_TW, SIN_TW = tables()
MATRICES = np.concatenate([np.pad(FIRST, ((0, 0), (0, 192))), SECOND, BACK, LAST])
TWIDDLES = np.concatenate([COS_TW, SIN_TW], axis=1)


def mm(left, right):
    return jnp.dot(left, right, preferred_element_type=F32)


def whole(count):
    return [pl.BlockSpec(memory_space=pltpu.VMEM)] * count


SCALARS = pl.BlockSpec(memory_space=pltpu.SMEM)


def spectrum(scratch, matrices, twiddles):
    cos_tw, sin_tw = twiddles[:, :128], twiddles[:, 128:]
    cube = jnp.concatenate([scratch[pl.ds(c, 64, stride=8), :] for c in range(8)], axis=1)
    step = mm(matrices[:256, :64], cube.astype(BF16))
    parts = []
    for c in range(8):
        real, imag = step[:128, c * 128 : c * 128 + 128], step[128:, c * 128 : c * 128 + 128]
        parts.append(
            jnp.concatenate(
                [(real * cos_tw + imag * sin_tw).astype(BF16), (imag * cos_tw - real * sin_tw).astype(BF16)],
                axis=1,
            )
        )
    return mm(jnp.concatenate(parts, axis=0), matrices[256:512, :])


def rows_of(scratch, ref, at):
    for p in range(16):
        scratch[p * 32 : p * 32 + 32] = ref[p, at : at + 32].astype(F32)


def spectra_kernel(got_ref, matrices, twiddles, signal_ref, filter_ref, scratch):
    rows_of(scratch, got_ref, 0)
    signal_ref[...] = spectrum(scratch, matrices, twiddles)
    rows_of(scratch, got_ref, 32)
    filter_ref[...] = spectrum(scratch, matrices, twiddles)


def conv_kernel(z_ref, signal_ref, filter_ref, before_ref, piece_ref, matrices, twiddles, out_ref, scratch):
    upper = z_ref[0] == 1
    cos_tw, sin_tw = twiddles[:, :128], twiddles[:, 128:]
    own, high = signal_ref[...], filter_ref[...]
    rows_of(scratch, before_ref, 0)
    old = jnp.where(upper, spectrum(scratch, matrices, twiddles), 0.0)
    rows_of(scratch, before_ref, 32)
    low = jnp.where(upper, spectrum(scratch, matrices, twiddles), high)
    odd = lax.broadcasted_iota(jnp.int32, (1024, 256), 0) & 1
    every = jnp.where(odd == 1, -low, low) + high
    own_r, own_i, old_r, old_i = own[:, :128], own[:, 128:], old[:, :128], old[:, 128:]
    low_r, low_i, all_r, all_i = low[:, :128], low[:, 128:], every[:, :128], every[:, 128:]
    real = own_r * low_r - own_i * low_i + old_r * all_r - old_i * all_i
    imag = own_r * low_i + own_i * low_r + old_r * all_i + old_i * all_r
    half = mm(jnp.concatenate([real.astype(BF16), imag.astype(BF16)], axis=1), matrices[512:768, :])
    parts = []
    for c in range(8):
        real, imag = half[c * 128 : c * 128 + 128, :128], half[c * 128 : c * 128 + 128, 128:]
        parts.append(
            jnp.concatenate(
                [(real * cos_tw - imag * sin_tw).astype(BF16), (imag * cos_tw + real * sin_tw).astype(BF16)],
                axis=0,
            )
        )
    result = mm(matrices[768:, :], jnp.concatenate(parts, axis=1))
    for c in range(8):
        scratch[pl.ds(c, 64, stride=8), :] = result[:, c * 128 : c * 128 + 128]
    piece = piece_ref[...]
    for d in range(32):
        out_ref[d, :16] = scratch[d * 16 : d * 16 + 16].astype(BF16)
        out_ref[d, 16:] = piece


def weight_block(ref, lead, row):
    return jnp.concatenate([ref[lead, row + 128 * g : row + 128 * g + 128, :] for g in range(3)], axis=1)


def near_kernel(at_ref, own_ref, beside_ref, gain_ref, near_ref, normed_ref, out_ref):
    start = at_ref[3] * 2048
    gain = gain_ref[...].astype(F32)
    for part, tokens in enumerate((own_ref, beside_ref)):

        @pl.loop(0, 8)
        def _(i):
            rows = pl.ds(pl.multiple_of(i * 32, 32), 32)
            stream = tokens[rows, :].astype(F32)
            scale = lax.rsqrt(jnp.mean(stream * stream, axis=1, keepdims=True) + NORM_EPS)
            normed_ref[part, rows, :] = (stream * scale * gain).astype(BF16)

        total = jnp.zeros((256, 384), F32)
        for y in range(4):
            for x in (0, 2):
                left = normed_ref[part, :, pl.ds(pl.multiple_of(start + (y * 4 + x) * 128, 128), 256)]
                right = [weight_block(near_ref, y, x * 384), weight_block(near_ref, y, x * 384 + 384)]
                total += mm(left, jnp.concatenate(right, axis=0))
        out_ref[part] = total


def put_pieces(ref, row, place, block):
    first, second = block[:128].T, block[128:].T
    for p in range(16):
        rows = jnp.concatenate([first[p * 8 : p * 8 + 8], second[p * 8 : p * 8 + 8]], axis=0).astype(BF16)
        ref[p, pl.ds(pl.multiple_of(row + place * 16, 16), 16), :] = rows


def proj_kernel(at_ref, normed_ref, near_ref, keep_ref, got_ref, f0, f1, f2, f3, sig_ref, gate_ref):
    y_at, x_at, core = at_ref[0], at_ref[1], at_ref[2]
    start = 2048 - at_ref[3] * 2048
    for part in range(2):
        total = near_ref[part]
        for step, ref in enumerate((f0, f1, f2, f3)):
            x = lax.rem(x_at + 4 - step, 4)
            for k in (0, 2):
                starts = [start + (lax.rem(y_at + 4 - j, 4) * 4 + x) * 128 for j in (k, k + 1)]
                left = [normed_ref[part, :, pl.ds(pl.multiple_of(at, 128), 128)] for at in starts]
                right = [weight_block(ref, k, 0), weight_block(ref, k + 1, 0)]
                total += mm(jnp.concatenate(left, axis=1), jnp.concatenate(right, axis=0))
        proj = total.astype(BF16).astype(F32)
        place = core if part == 0 else 1 - core
        put_pieces(sig_ref, 0, place, proj[:, 128:256] * proj[:, 256:])
        put_pieces(sig_ref, 32, place, (keep_ref if part == 0 else got_ref)[...].astype(F32))
        gate_ref[place, 0] = proj[:128, :128].T.astype(BF16)
        gate_ref[place, 1] = proj[128:, :128].T.astype(BF16)


def mix_kernel(core_ref, got_ref, keep_ref, other_ref, base_ref, out_ref):
    core = core_ref[0]
    keep, other = keep_ref[...].astype(F32), other_ref[...].astype(F32)
    conv = got_ref[:, :16, :].astype(F32)
    for rb in range(2):
        total = base_ref[rb * 128 : rb * 128 + 128, :]
        for c in range(2):
            cube = jnp.concatenate([conv[p * 2 + c, rb * 8 : rb * 8 + 8] for p in range(16)], axis=0)
            gate = jnp.where(core == c, keep[rb], other[rb])
            mixed = (gate * cube).T.astype(BF16)
            weights = []
            for p in range(16):
                piece = got_ref[p * 2 + c, 16:, :].astype(F32)
                weights.append(jnp.concatenate([piece[v * 8 : v * 8 + 8] for v in range(4)], axis=1))
            total += mm(mixed, jnp.concatenate(weights, axis=0).astype(BF16))
        out_ref[rb * 128 : rb * 128 + 128, :] = total.astype(BF16)


def call(kernel, outs, specs, scratch, flops, args):
    return pl.pallas_call(
        kernel,
        out_shape=outs,
        in_specs=specs,
        out_specs=jax.tree.map(lambda _: pl.BlockSpec(memory_space=pltpu.VMEM), outs),
        scratch_shapes=scratch,
        compiler_params=pltpu.CompilerParams(vmem_limit_bytes=40 * 2**20),
        cost_estimate=pl.CostEstimate(flops=flops, bytes_accessed=4 * 2**20, transcendentals=0),
    )(*args)


def shape(dims, dtype):
    return jax.ShapeDtypeStruct(dims, dtype)


def by_position(own, other, place):
    return jnp.where(place == 0, jnp.stack([own, other]), jnp.stack([other, own]))


def spectra(got):
    return call(
        spectra_kernel,
        (shape((1024, 256), F32), shape((1024, 256), F32)),
        whole(3),
        [pltpu.VMEM((512, 128), F32)],
        4 * 10**8,
        (got, jnp.asarray(MATRICES, BF16), jnp.asarray(TWIDDLES, F32)),
    )


def convolve(z, signal, taps, before, piece):
    return call(
        conv_kernel,
        shape((32, 48, 128), BF16),
        [SCALARS] + whole(6),
        [pltpu.VMEM((512, 128), F32)],
        6 * 10**8,
        (z, signal, taps, before, piece, jnp.asarray(MATRICES, BF16), jnp.asarray(TWIDDLES, F32)),
    )


def halves_of(array, axis, core):
    keep = lax.dynamic_slice_in_dim(array, core * 128, 128, axis)
    return keep, lax.dynamic_slice_in_dim(array, 128 - core * 128, 128, axis)


def product(w_out, w_unembed):
    partial = mm(w_out, w_unembed).astype(BF16).reshape(4, 1, 8, 4, 128).transpose(0, 1, 3, 2, 4)
    return jnp.broadcast_to(partial.reshape(4, 1, 32, 128), (4, 2, 32, 128)).reshape(8, 32, 128)


def per_device(tokens_in, pre_gain, w_in, w_out, long_filter, w_unembed, target_ids, score_mask):
    ctx, tp = lax.axis_index("ctx"), lax.axis_index("tp")
    core, z = ctx % 2, ctx // 32
    z_at = z.reshape(1).astype(jnp.int32)

    keep, give = halves_of(w_in.transpose(1, 0, 2), 2, core)
    got = lax.ppermute(give, "ctx", PERM_CORE)
    near = jnp.concatenate([jnp.where(core == 0, keep, got), jnp.where(core == 0, got, keep)], axis=1)
    near, w_out, tokens = lax.optimization_barrier((near.reshape(384, 128), w_out, tokens_in))
    beside = lax.ppermute(tokens, "ctx", PERM_CORE)
    terms = lax.all_to_all(product(w_out, w_unembed), "tp", 0, 0, tiled=True)
    far = lax.ppermute(near, "ctx", PERM_Z)
    near, far, terms, beside = lax.optimization_barrier((near, far, terms, beside))

    near = lax.all_to_all(
        jnp.broadcast_to(near, (4, 384, 128)), "ctx", 0, 0, axis_index_groups=GROUPS_X, tiled=True
    )
    far = jnp.stack([far] + [lax.ppermute(far, "ctx", PERM_Y[k]) for k in (1, 2, 3)])
    near, far, terms, long_filter = lax.optimization_barrier((near, far, terms, long_filter))

    near = jnp.broadcast_to(near.reshape(1, 1536, 128), (4, 1536, 128))
    near = lax.all_to_all(near, "ctx", 0, 0, axis_index_groups=GROUPS_Y, tiled=True)
    fars = [far] + [lax.ppermute(far, "ctx", PERM_X[k]) for k in (1, 2, 3)]
    taps, give = halves_of(long_filter, 1, core)
    taps_got = lax.ppermute(give, "ctx", PERM_CORE)
    piece = lax.ppermute(jnp.sum(terms.astype(F32), axis=0).astype(BF16), ("ctx", "tp"), ROUTE)

    at = jnp.stack([(ctx // 8) % 4, (ctx // 2) % 4, core, z]).astype(jnp.int32)
    normed, sums = call(
        near_kernel,
        (shape((2, 256, 4096), BF16), shape((2, 256, 384), F32)),
        [SCALARS] + whole(4),
        [],
        8 * 10**8,
        (at, tokens_in, beside, pre_gain.reshape(1, 4096), near),
    )
    signal, gate = call(
        proj_kernel,
        (shape((16, 64, 128), BF16), shape((2, 2, 128, 128), BF16)),
        [SCALARS] + whole(8),
        [],
        8 * 10**8,
        (at, normed, sums, taps, taps_got, *fars),
    )
    got = lax.all_to_all(signal, "ctx", 0, 0, axis_index_groups=GROUPS_CORE, tiled=True)
    before = lax.ppermute(got, "ctx", PERM_Z_UP)
    gate_keep = lax.dynamic_index_in_dim(gate, core, 0, False)
    gate_got = lax.ppermute(lax.dynamic_index_in_dim(gate, 1 - core, 0, False), "ctx", PERM_CORE)

    conv = convolve(z_at, *spectra(got), before, piece)
    conv = lax.all_to_all(conv, "ctx", 0, 0, axis_index_groups=GROUPS_PLANE, tiled=True)

    width = w_unembed.shape[0]
    base = mm(lax.dynamic_slice_in_dim(tokens_in, tp * width, width, 1), w_unembed)
    logits = call(
        mix_kernel,
        shape((256, 512), BF16),
        [SCALARS] + whole(4),
        [],
        10**8,
        (core.reshape(1).astype(jnp.int32), conv, gate_keep, gate_got, base),
    )
    logits = lax.all_to_all(logits.reshape(4, 64, 512), "tp", 0, 0, axis_index_groups=GROUPS_TP, tiled=True)
    logits = jnp.sum(logits.astype(F32), axis=0).astype(BF16)
    far = lax.ppermute(logits, "tp", [(i, i ^ 4) for i in range(8)])
    logits = logits.astype(F32) + far.astype(F32)

    row_top = jnp.max(logits, axis=1, keepdims=True)
    log_total = row_top[:, 0] + jnp.log(jnp.sum(jnp.exp(logits - row_top), axis=1))
    ids = lax.dynamic_slice_in_dim(target_ids, (tp % 4) * 64, 64, 0)
    mask = lax.dynamic_slice_in_dim(score_mask, (tp % 4) * 64, 64, 0)
    vocab_index = lax.broadcasted_iota(jnp.int32, (64, 512), 1)
    picked = jnp.sum(jnp.where(vocab_index == ids[:, None], logits, 0.0), axis=1)
    scores = (picked - log_total) * mask.astype(F32)
    scores = jnp.broadcast_to(scores[None, :], (4, 64))
    scores = lax.all_to_all(scores, "tp", 0, 0, axis_index_groups=GROUPS_TP, tiled=True)
    return scores.reshape(256)


def solution(mesh):
    return jax.shard_map(
        per_device,
        mesh=mesh,
        in_specs=(
            P("ctx", None),
            P(),
            P("ctx", None, "tp"),
            P("ctx", "tp"),
            P("ctx", "tp"),
            P("tp", None),
            P("ctx"),
            P("ctx"),
        ),
        out_specs=P("ctx"),
        check_vma=False,
    )
```

```python
import math

import jax
import jax.numpy as jnp
import numpy as np
from jax import lax
from jax.experimental import pallas as pl
from jax.experimental.pallas import tpu as pltpu
from jax.sharding import PartitionSpec as P

NORM_EPS = 1e-05
F32 = jnp.float32
BF16 = jnp.bfloat16

COORDS = [(z, y, x, c) for z in range(2) for y in range(4) for x in range(4) for c in range(2)]


def ctx_id(z, y, x, c):
    return ((z * 4 + y) * 4 + x) * 2 + c


def ctx_perm(move):
    return [(ctx_id(*at), ctx_id(*move(*at))) for at in COORDS]


PERM_CORE = ctx_perm(lambda z, y, x, c: (z, y, x, 1 - c))
PERM_Z = ctx_perm(lambda z, y, x, c: (1 - z, y, x, c))
PERM_Z_UP = [(i, i + 32) for i in range(32)]
PERM_X = [ctx_perm(lambda z, y, x, c, k=k: (z, y, (x + k) % 4, c)) for k in range(4)]
PERM_Y = [ctx_perm(lambda z, y, x, c, k=k: (z, (y + k) % 4, x, c)) for k in range(4)]
GROUPS_X = [[ctx_id(z, y, x, c) for x in range(4)] for z in range(2) for y in range(4) for c in range(2)]
GROUPS_Y = [[ctx_id(z, y, x, c) for y in range(4)] for z in range(2) for x in range(4) for c in range(2)]
GROUPS_PLANE = [
    [ctx_id(z, y, x, c) for y in range(4) for x in range(4) for c in range(2)] for z in range(2)
]
GROUPS_CORE = [
    [ctx_id(z, y, x, c) for y in range(4) for x in range(4)] for z in range(2) for c in range(2)
]
GROUPS_TP = [[0, 1, 2, 3], [4, 5, 6, 7]]


def term_route(flip):
    pairs = []
    for i in range(64):
        for j in range(8):
            to = ctx_id((j % 2) ^ flip, j // 2, i % 4, (i % 8) // 4)
            pairs.append((i * 8 + j, to * 8 + i // 8))
    return pairs


ROUTES = [term_route(0), term_route(1)]
BLOCK = [(p % 4) * 4 + p // 4 for p in range(16)]


def tables():
    index = np.arange(128)
    inner = 2.0 * math.pi * (np.outer(index, index) % 128) / 128
    outer = 2.0 * math.pi * np.outer(index, index) / 16384
    cos, sin = np.cos(inner), np.sin(inner)
    first = np.concatenate([cos[:, :64], -sin[:, :64]], axis=0)
    second = np.block([[cos, -sin], [sin, cos]])
    back = np.block([[cos, sin], [-sin, cos]])
    last = np.concatenate([cos[:64], -sin[:64]], axis=1) / 16384.0
    return (first, second, back, last, np.cos(outer), np.sin(outer))


FIRST, SECOND, BACK, LAST, COS_TW, SIN_TW = tables()
MATRICES = np.concatenate([np.pad(FIRST, ((0, 0), (0, 192))), SECOND, BACK, LAST])
TWIDDLES = np.concatenate([COS_TW, SIN_TW], axis=1)


def mm(left, right):
    return jnp.dot(left, right, preferred_element_type=F32)


def whole(count):
    return [pl.BlockSpec(memory_space=pltpu.VMEM)] * count


SCALARS = pl.BlockSpec(memory_space=pltpu.SMEM)


def spectrum(scratch, matrices, twiddles):
    cos_tw, sin_tw = twiddles[:, :128], twiddles[:, 128:]
    cube = jnp.concatenate([scratch[pl.ds(c, 64, stride=8), :] for c in range(8)], axis=1)
    step = mm(matrices[:256, :64], cube.astype(BF16))
    parts = []
    for c in range(8):
        real, imag = step[:128, c * 128 : c * 128 + 128], step[128:, c * 128 : c * 128 + 128]
        parts.append(
            jnp.concatenate(
                [(real * cos_tw + imag * sin_tw).astype(BF16), (imag * cos_tw - real * sin_tw).astype(BF16)],
                axis=1,
            )
        )
    return mm(jnp.concatenate(parts, axis=0), matrices[256:512, :])


def rows_of(scratch, ref, at):
    for p in range(16):
        scratch[p * 32 : p * 32 + 32] = ref[p, at : at + 32].astype(F32)


def spectra_kernel(got_ref, matrices, twiddles, signal_ref, filter_ref, scratch):
    rows_of(scratch, got_ref, 0)
    signal_ref[...] = spectrum(scratch, matrices, twiddles)
    rows_of(scratch, got_ref, 32)
    filter_ref[...] = spectrum(scratch, matrices, twiddles)


def conv_kernel(z_ref, signal_ref, filter_ref, before_ref, piece_ref, matrices, twiddles, out_ref, scratch):
    upper = z_ref[0] == 1
    cos_tw, sin_tw = twiddles[:, :128], twiddles[:, 128:]
    own, high = signal_ref[...], filter_ref[...]
    rows_of(scratch, before_ref, 0)
    old = jnp.where(upper, spectrum(scratch, matrices, twiddles), 0.0)
    rows_of(scratch, before_ref, 32)
    low = jnp.where(upper, spectrum(scratch, matrices, twiddles), high)
    odd = lax.broadcasted_iota(jnp.int32, (1024, 256), 0) & 1
    every = jnp.where(odd == 1, -low, low) + high
    own_r, own_i, old_r, old_i = own[:, :128], own[:, 128:], old[:, :128], old[:, 128:]
    low_r, low_i, all_r, all_i = low[:, :128], low[:, 128:], every[:, :128], every[:, 128:]
    real = own_r * low_r - own_i * low_i + old_r * all_r - old_i * all_i
    imag = own_r * low_i + own_i * low_r + old_r * all_i + old_i * all_r
    half = mm(jnp.concatenate([real.astype(BF16), imag.astype(BF16)], axis=1), matrices[512:768, :])
    parts = []
    for c in range(8):
        real, imag = half[c * 128 : c * 128 + 128, :128], half[c * 128 : c * 128 + 128, 128:]
        parts.append(
            jnp.concatenate(
                [(real * cos_tw - imag * sin_tw).astype(BF16), (imag * cos_tw + real * sin_tw).astype(BF16)],
                axis=0,
            )
        )
    result = mm(matrices[768:, :], jnp.concatenate(parts, axis=1))
    for c in range(8):
        scratch[pl.ds(c, 64, stride=8), :] = result[:, c * 128 : c * 128 + 128]
    piece = piece_ref[...]
    for d in range(32):
        out_ref[d, :16] = scratch[d * 16 : d * 16 + 16].astype(BF16)
        out_ref[d, 16:] = piece


def weight_block(ref, lead, row):
    return jnp.concatenate([ref[lead, row + 128 * g : row + 128 * g + 128, :] for g in range(3)], axis=1)


def near_kernel(at_ref, own_ref, beside_ref, gain_ref, near_ref, gained_ref, scale_ref, out_ref, piece_ref):
    start = at_ref[3] * 2048
    gain = gain_ref[...]
    for part, tokens in enumerate((own_ref, beside_ref)):

        @pl.loop(0, 8)
        def _(i):
            rows = pl.ds(pl.multiple_of(i * 32, 32), 32)
            block = tokens[rows, :]
            stream = block.astype(F32)
            mean = jnp.mean(stream * stream, axis=1, keepdims=True)
            scale_ref[part, rows, :] = jnp.broadcast_to(lax.rsqrt(mean + NORM_EPS), (32, 128))
            gained_ref[part, rows, :] = block * gain

        total = jnp.zeros((256, 384), F32)
        for y in range(4):
            for x in (0, 2):
                left = gained_ref[part, :, pl.ds(pl.multiple_of(start + (y * 4 + x) * 128, 128), 256)]
                right = [weight_block(near_ref, y, x * 384), weight_block(near_ref, y, x * 384 + 384)]
                total += mm(left, jnp.concatenate(right, axis=0))
        out_ref[part] = total
    piece_ref[...] = sum(near_ref[y, 1536:, :].astype(F32) for y in range(4)).astype(BF16)


def put_pieces(ref, row, place, block):
    first, second = block[:128].T, block[128:].T
    for p in range(16):
        b = BLOCK[p] * 8
        rows = jnp.concatenate([first[b : b + 8], second[b : b + 8]], axis=0).astype(BF16)
        ref[p, pl.ds(pl.multiple_of(row + place * 16, 16), 16), :] = rows


def proj_kernel(at_ref, gained_ref, scale_ref, near_ref, own_taps, got_taps, f0, f1, f2, f3, sig_ref, gate_ref):
    y_at, x_at, core = at_ref[0], at_ref[1], at_ref[2]
    start = 2048 - at_ref[3] * 2048
    half = pl.ds(pl.multiple_of(core * 128, 128), 128)
    for part in range(2):
        total = near_ref[part]
        for step, ref in enumerate((f0, f1, f2, f3)):
            x = lax.rem(x_at + 4 - step, 4)
            for k in (0, 2):
                starts = [start + (lax.rem(y_at + 4 - j, 4) * 4 + x) * 128 for j in (k, k + 1)]
                left = [gained_ref[part, :, pl.ds(pl.multiple_of(at, 128), 128)] for at in starts]
                right = [weight_block(ref, k, 0), weight_block(ref, k + 1, 0)]
                total += mm(jnp.concatenate(left, axis=1), jnp.concatenate(right, axis=0))
        scale = scale_ref[part]
        proj = (total * jnp.concatenate([scale, scale, scale], axis=1)).astype(BF16).astype(F32)
        place = core if part == 0 else 1 - core
        put_pieces(sig_ref, 0, place, proj[:, 128:256] * proj[:, 256:])
        put_pieces(sig_ref, 32, place, (own_taps if part == 0 else got_taps)[:, half].astype(F32))
        gate_ref[place, 0] = proj[:128, :128].T.astype(BF16)
        gate_ref[place, 1] = proj[128:, :128].T.astype(BF16)


def mix_kernel(core_ref, got_ref, keep_ref, other_ref, base_ref, out_ref):
    core = core_ref[0]
    keep, other = keep_ref[...].astype(F32), other_ref[...].astype(F32)
    conv = got_ref[:, :16, :].astype(F32)
    for rb in range(2):
        total = base_ref[rb * 128 : rb * 128 + 128, :]
        for c in range(2):
            cube = jnp.concatenate([conv[BLOCK[b] * 2 + c, rb * 8 : rb * 8 + 8] for b in range(16)], axis=0)
            gate = jnp.where(core == c, keep[rb], other[rb])
            mixed = (gate * cube).T.astype(BF16)
            weights = []
            for b in range(16):
                piece = got_ref[BLOCK[b] * 2 + c, 16:, :].astype(F32)
                weights.append(jnp.concatenate([piece[v * 8 : v * 8 + 8] for v in range(4)], axis=1))
            total += mm(mixed, jnp.concatenate(weights, axis=0).astype(BF16))
        out_ref[rb * 128 : rb * 128 + 128, :] = total.astype(BF16)


def call(kernel, outs, specs, scratch, flops, args):
    return pl.pallas_call(
        kernel,
        out_shape=outs,
        in_specs=specs,
        out_specs=jax.tree.map(lambda _: pl.BlockSpec(memory_space=pltpu.VMEM), outs),
        scratch_shapes=scratch,
        compiler_params=pltpu.CompilerParams(vmem_limit_bytes=40 * 2**20),
        cost_estimate=pl.CostEstimate(flops=flops, bytes_accessed=4 * 2**20, transcendentals=0),
    )(*args)


def shape(dims, dtype):
    return jax.ShapeDtypeStruct(dims, dtype)


def by_position(own, other, place):
    return jnp.where(place == 0, jnp.stack([own, other]), jnp.stack([other, own]))


def spectra(got):
    return call(
        spectra_kernel,
        (shape((1024, 256), F32), shape((1024, 256), F32)),
        whole(3),
        [pltpu.VMEM((512, 128), F32)],
        4 * 10**8,
        (got, jnp.asarray(MATRICES, BF16), jnp.asarray(TWIDDLES, F32)),
    )


def convolve(z, signal, taps, before, piece):
    return call(
        conv_kernel,
        shape((32, 48, 128), BF16),
        [SCALARS] + whole(6),
        [pltpu.VMEM((512, 128), F32)],
        6 * 10**8,
        (z, signal, taps, before, piece, jnp.asarray(MATRICES, BF16), jnp.asarray(TWIDDLES, F32)),
    )


def half_of(array, axis, which):
    return lax.dynamic_slice_in_dim(array, which * 128, 128, axis)


def product(w_out, w_unembed):
    partial = mm(w_out, w_unembed).astype(BF16).reshape(4, 8, 4, 128)
    return partial.transpose(0, 2, 1, 3).reshape(128, 128)


def per_device(tokens_in, pre_gain, w_in, w_out, long_filter, w_unembed, target_ids, score_mask):
    ctx, tp = lax.axis_index("ctx"), lax.axis_index("tp")
    core, z = ctx % 2, ctx // 32
    z_at = z.reshape(1).astype(jnp.int32)

    w_in = w_in.transpose(1, 0, 2)
    got = half_of(lax.ppermute(w_in, "ctx", PERM_CORE), 2, core)
    keep = half_of(w_in, 2, core)
    near = jnp.concatenate([jnp.where(core == 0, keep, got), jnp.where(core == 0, got, keep)], axis=1)
    near, tokens = lax.optimization_barrier((near.reshape(384, 128), tokens_in))
    beside = lax.ppermute(tokens, "ctx", PERM_CORE)
    far = lax.ppermute(near, "ctx", PERM_Z)
    near, w_out, taps, beside = lax.optimization_barrier((near, w_out, long_filter, beside))
    taps_got = lax.ppermute(taps, "ctx", PERM_CORE)
    term = product(w_out, w_unembed)
    terms = [lax.ppermute(term, ("ctx", "tp"), route) for route in ROUTES]
    near = lax.all_to_all(
        jnp.broadcast_to(near, (4, 384, 128)), "ctx", 0, 0, axis_index_groups=GROUPS_X, tiled=True
    )

    far = jnp.stack([far] + [lax.ppermute(far, "ctx", PERM_Y[k]) for k in (1, 2, 3)])
    pieces = (terms[0].astype(F32) + terms[1].astype(F32)).astype(BF16).reshape(4, 32, 128)
    near, far, pieces = lax.optimization_barrier((near, far, pieces))

    near = jnp.concatenate([jnp.broadcast_to(near.reshape(1, 1536, 128), (4, 1536, 128)), pieces], axis=1)
    near = lax.all_to_all(near, "ctx", 0, 0, axis_index_groups=GROUPS_Y, tiled=True)
    fars = [far] + [lax.ppermute(far, "ctx", PERM_X[k]) for k in (1, 2, 3)]

    at = jnp.stack([(ctx // 8) % 4, (ctx // 2) % 4, core, z]).astype(jnp.int32)
    gained, scale, sums, piece = call(
        near_kernel,
        (shape((2, 256, 4096), BF16), shape((2, 256, 128), F32), shape((2, 256, 384), F32), shape((32, 128), BF16)),
        [SCALARS] + whole(4),
        [],
        8 * 10**8,
        (at, tokens_in, beside, pre_gain.reshape(1, 4096), near),
    )
    signal, gate = call(
        proj_kernel,
        (shape((16, 64, 128), BF16), shape((2, 2, 128, 128), BF16)),
        [SCALARS] + whole(9),
        [],
        8 * 10**8,
        (at, gained, scale, sums, taps, taps_got, *fars),
    )
    got = lax.all_to_all(signal, "ctx", 0, 0, axis_index_groups=GROUPS_CORE, tiled=True)
    before = lax.ppermute(got, "ctx", PERM_Z_UP)
    gate_keep = lax.dynamic_index_in_dim(gate, core, 0, False)
    gate_got = lax.ppermute(lax.dynamic_index_in_dim(gate, 1 - core, 0, False), "ctx", PERM_CORE)

    conv = convolve(z_at, *spectra(got), before, piece)
    conv = lax.all_to_all(conv, "ctx", 0, 0, axis_index_groups=GROUPS_PLANE, tiled=True)

    width = w_unembed.shape[0]
    base = mm(lax.dynamic_slice_in_dim(tokens_in, tp * width, width, 1), w_unembed)
    logits = call(
        mix_kernel,
        shape((256, 512), BF16),
        [SCALARS] + whole(4),
        [],
        10**8,
        (core.reshape(1).astype(jnp.int32), conv, gate_keep, gate_got, base),
    )
    logits = lax.all_to_all(logits.reshape(4, 64, 512), "tp", 0, 0, axis_index_groups=GROUPS_TP, tiled=True)
    logits = jnp.sum(logits.astype(F32), axis=0).astype(BF16)
    far = lax.ppermute(logits, "tp", [(i, i ^ 4) for i in range(8)])
    logits = logits.astype(F32) + far.astype(F32)

    row_top = jnp.max(logits, axis=1, keepdims=True)
    log_total = row_top[:, 0] + jnp.log(jnp.sum(jnp.exp(logits - row_top), axis=1))
    ids = lax.dynamic_slice_in_dim(target_ids, (tp % 4) * 64, 64, 0)
    mask = lax.dynamic_slice_in_dim(score_mask, (tp % 4) * 64, 64, 0)
    vocab_index = lax.broadcasted_iota(jnp.int32, (64, 512), 1)
    picked = jnp.sum(jnp.where(vocab_index == ids[:, None], logits, 0.0), axis=1)
    scores = (picked - log_total) * mask.astype(F32)
    scores = jnp.broadcast_to(scores[None, :], (4, 64))
    scores = lax.all_to_all(scores, "tp", 0, 0, axis_index_groups=GROUPS_TP, tiled=True)
    return scores.reshape(256)


def solution(mesh):
    return jax.shard_map(
        per_device,
        mesh=mesh,
        in_specs=(
            P("ctx", None),
            P(),
            P("ctx", None, "tp"),
            P("ctx", "tp"),
            P("ctx", "tp"),
            P("tp", None),
            P("ctx"),
            P("ctx"),
        ),
        out_specs=P("ctx"),
        check_vma=False,
    )
```

```python
import math

import jax
import jax.numpy as jnp
import numpy as np
from jax import lax
from jax.experimental import pallas as pl
from jax.experimental.pallas import tpu as pltpu
from jax.sharding import PartitionSpec as P

NORM_EPS = 1e-05
F32 = jnp.float32
BF16 = jnp.bfloat16

COORDS = [(z, y, x, c) for z in range(2) for y in range(4) for x in range(4) for c in range(2)]


def ctx_id(z, y, x, c):
    return ((z * 4 + y) * 4 + x) * 2 + c


def ctx_perm(move):
    return [(ctx_id(*at), ctx_id(*move(*at))) for at in COORDS]


PERM_CORE = ctx_perm(lambda z, y, x, c: (z, y, x, 1 - c))
PERM_Z = ctx_perm(lambda z, y, x, c: (1 - z, y, x, c))
PERM_Z_UP = [(i, i + 32) for i in range(32)]
PERM_X = [ctx_perm(lambda z, y, x, c, k=k: (z, y, (x + k) % 4, c)) for k in range(4)]
PERM_Y = [ctx_perm(lambda z, y, x, c, k=k: (z, (y + k) % 4, x, c)) for k in range(4)]
GROUPS_X = [[ctx_id(z, y, x, c) for x in range(4)] for z in range(2) for y in range(4) for c in range(2)]
GROUPS_Y = [[ctx_id(z, y, x, c) for y in range(4)] for z in range(2) for x in range(4) for c in range(2)]
GROUPS_PLANE = [
    [ctx_id(z, y, x, c) for y in range(4) for x in range(4) for c in range(2)] for z in range(2)
]
GROUPS_CORE = [
    [ctx_id(z, y, x, c) for y in range(4) for x in range(4)] for z in range(2) for c in range(2)
]
GROUPS_TP = [[0, 1, 2, 3], [4, 5, 6, 7]]


def tables():
    index = np.arange(128)
    inner = 2.0 * math.pi * (np.outer(index, index) % 128) / 128
    outer = 2.0 * math.pi * np.outer(index, index) / 16384
    cos, sin = np.cos(inner), np.sin(inner)
    first = np.concatenate([cos[:, :64], -sin[:, :64]], axis=0)
    second = np.block([[cos, -sin], [sin, cos]])
    back = np.block([[cos, sin], [-sin, cos]])
    last = np.concatenate([cos[:64], -sin[:64]], axis=1) / 16384.0
    return (first, second, back, last, np.cos(outer), np.sin(outer))


FIRST, SECOND, BACK, LAST, COS_TW, SIN_TW = tables()
MATRICES = np.concatenate([np.pad(FIRST, ((0, 0), (0, 192))), SECOND, BACK, LAST])
TWIDDLES = np.concatenate([COS_TW, SIN_TW], axis=1)


def mm(left, right):
    return jnp.dot(left, right, preferred_element_type=F32)


def whole(count):
    return [pl.BlockSpec(memory_space=pltpu.VMEM)] * count


SCALARS = pl.BlockSpec(memory_space=pltpu.SMEM)


def spectrum(scratch, matrices, twiddles):
    cos_tw, sin_tw = twiddles[:, :128], twiddles[:, 128:]
    cube = jnp.concatenate([scratch[pl.ds(c, 64, stride=8), :] for c in range(8)], axis=1)
    step = mm(matrices[:256, :64], cube.astype(BF16))
    parts = []
    for c in range(8):
        real, imag = step[:128, c * 128 : c * 128 + 128], step[128:, c * 128 : c * 128 + 128]
        parts.append(
            jnp.concatenate(
                [(real * cos_tw + imag * sin_tw).astype(BF16), (imag * cos_tw - real * sin_tw).astype(BF16)],
                axis=1,
            )
        )
    return mm(jnp.concatenate(parts, axis=0), matrices[256:512, :])


def rows_of(scratch, ref, at):
    for p in range(16):
        scratch[p * 32 : p * 32 + 32] = ref[p, at : at + 32].astype(F32)


def spectra_kernel(got_ref, matrices, twiddles, signal_ref, filter_ref, scratch):
    rows_of(scratch, got_ref, 0)
    signal_ref[...] = spectrum(scratch, matrices, twiddles)
    rows_of(scratch, got_ref, 32)
    filter_ref[...] = spectrum(scratch, matrices, twiddles)


def conv_kernel(z_ref, signal_ref, filter_ref, before_ref, piece_ref, matrices, twiddles, out_ref, scratch):
    upper = z_ref[0] == 1
    cos_tw, sin_tw = twiddles[:, :128], twiddles[:, 128:]
    own, high = signal_ref[...], filter_ref[...]
    rows_of(scratch, before_ref, 0)
    old = jnp.where(upper, spectrum(scratch, matrices, twiddles), 0.0)
    rows_of(scratch, before_ref, 32)
    low = jnp.where(upper, spectrum(scratch, matrices, twiddles), high)
    odd = lax.broadcasted_iota(jnp.int32, (1024, 256), 0) & 1
    every = jnp.where(odd == 1, -low, low) + high
    own_r, own_i, old_r, old_i = own[:, :128], own[:, 128:], old[:, :128], old[:, 128:]
    low_r, low_i, all_r, all_i = low[:, :128], low[:, 128:], every[:, :128], every[:, 128:]
    real = own_r * low_r - own_i * low_i + old_r * all_r - old_i * all_i
    imag = own_r * low_i + own_i * low_r + old_r * all_i + old_i * all_r
    half = mm(jnp.concatenate([real.astype(BF16), imag.astype(BF16)], axis=1), matrices[512:768, :])
    parts = []
    for c in range(8):
        real, imag = half[c * 128 : c * 128 + 128, :128], half[c * 128 : c * 128 + 128, 128:]
        parts.append(
            jnp.concatenate(
                [(real * cos_tw - imag * sin_tw).astype(BF16), (imag * cos_tw + real * sin_tw).astype(BF16)],
                axis=0,
            )
        )
    result = mm(matrices[768:, :], jnp.concatenate(parts, axis=1))
    for c in range(8):
        scratch[pl.ds(c, 64, stride=8), :] = result[:, c * 128 : c * 128 + 128]
    piece = sum(piece_ref[j].astype(F32) for j in range(8)).astype(BF16)
    for d in range(32):
        out_ref[d, :16] = scratch[d * 16 : d * 16 + 16].astype(BF16)
        out_ref[d, 16:] = piece


def weight_block(ref, lead, row):
    return jnp.concatenate([ref[lead, row + 128 * g : row + 128 * g + 128, :] for g in range(3)], axis=1)


def norm_kernel(own_hbm, beside_hbm, gain_ref, gained_ref, scale_ref, tokens, sems):
    gain = gain_ref[...]
    copies = []
    for part, ref in enumerate((own_hbm, beside_hbm)):
        for i in range(4):
            rows = slice(i * 64, i * 64 + 64)
            copies.append(pltpu.make_async_copy(ref.at[rows], tokens.at[part, rows], sems.at[part, i]))
    for copy in copies:
        copy.start()
    for k, copy in enumerate(copies):
        copy.wait()
        part, i = k // 4, k % 4
        for half in range(2):
            rows = slice(i * 64 + half * 32, i * 64 + half * 32 + 32)
            block = tokens[part, rows, :]
            stream = block.astype(F32)
            mean = jnp.mean(stream * stream, axis=1, keepdims=True)
            scale_ref[part, rows, :] = jnp.broadcast_to(lax.rsqrt(mean + NORM_EPS), (32, 128))
            gained_ref[part, rows, :] = block * gain


def near_kernel(at_ref, gained_ref, near_ref, out_ref):
    start = at_ref[3] * 2048
    for part in range(2):
        total = jnp.zeros((256, 384), F32)
        for y in range(4):
            for x in (0, 2):
                left = gained_ref[part, :, pl.ds(pl.multiple_of(start + (y * 4 + x) * 128, 128), 256)]
                right = [weight_block(near_ref, y, x * 384), weight_block(near_ref, y, x * 384 + 384)]
                total += mm(left, jnp.concatenate(right, axis=0))
        out_ref[part] = total


def product_kernel(rows_ref, unembed_ref, out_ref):
    blocks = []
    for z in range(2):
        for y in range(4):
            block = rows_ref[y, 1536 + z * 32 : 1568 + z * 32, :].astype(F32)
            blocks.append(jnp.concatenate([block[v * 8 : v * 8 + 8] for v in range(4)], axis=1))
    terms = mm(jnp.concatenate(blocks, axis=0).astype(BF16), unembed_ref[...])
    for j in range(8):
        parts = [terms[j * 8 : j * 8 + 8, v * 128 : v * 128 + 128] for v in range(4)]
        out_ref[j] = jnp.concatenate(parts, axis=0).astype(BF16)


def put_pieces(ref, row, place, block):
    first, second = block[:128].T, block[128:].T
    for p in range(16):
        b = p * 8
        rows = jnp.concatenate([first[b : b + 8], second[b : b + 8]], axis=0).astype(BF16)
        ref[p, pl.ds(pl.multiple_of(row + place * 16, 16), 16), :] = rows


def proj_kernel(at_ref, gained_ref, scale_ref, near_ref, own_taps, got_taps, f0, f1, f2, f3, sig_ref, gate_ref):
    y_at, x_at, core = at_ref[0], at_ref[1], at_ref[2]
    start = 2048 - at_ref[3] * 2048
    half = pl.ds(pl.multiple_of(core * 128, 128), 128)
    for part in range(2):
        total = near_ref[part]
        for step, ref in enumerate((f0, f1, f2, f3)):
            x = lax.rem(x_at + 4 - step, 4)
            for k in (0, 2):
                starts = [start + (lax.rem(y_at + 4 - j, 4) * 4 + x) * 128 for j in (k, k + 1)]
                left = [gained_ref[part, :, pl.ds(pl.multiple_of(at, 128), 128)] for at in starts]
                right = [weight_block(ref, k, 0), weight_block(ref, k + 1, 0)]
                total += mm(jnp.concatenate(left, axis=1), jnp.concatenate(right, axis=0))
        scale = scale_ref[part]
        proj = (total * jnp.concatenate([scale, scale, scale], axis=1)).astype(BF16).astype(F32)
        place = core if part == 0 else 1 - core
        put_pieces(sig_ref, 0, place, proj[:, 128:256] * proj[:, 256:])
        put_pieces(sig_ref, 32, place, (own_taps if part == 0 else got_taps)[:, half].astype(F32))
        gate_ref[place, 0] = proj[:128, :128].T.astype(BF16)
        gate_ref[place, 1] = proj[128:, :128].T.astype(BF16)


def mix_kernel(core_ref, got_ref, keep_ref, other_ref, base_ref, out_ref):
    core = core_ref[0]
    keep, other = keep_ref[...].astype(F32), other_ref[...].astype(F32)
    conv = got_ref[:, :16, :].astype(F32)
    for rb in range(2):
        total = base_ref[rb * 128 : rb * 128 + 128, :]
        for c in range(2):
            cube = jnp.concatenate([conv[b * 2 + c, rb * 8 : rb * 8 + 8] for b in range(16)], axis=0)
            gate = jnp.where(core == c, keep[rb], other[rb])
            mixed = (gate * cube).T.astype(BF16)
            weights = []
            for b in range(16):
                x, holder, y = (c * 16 + b) // 8, b % 8 // 4, b % 4
                piece = got_ref[(y * 4 + x) * 2 + holder, 16:, :].astype(F32)
                weights.append(jnp.concatenate([piece[v * 8 : v * 8 + 8] for v in range(4)], axis=1))
            total += mm(mixed, jnp.concatenate(weights, axis=0).astype(BF16))
        out_ref[rb * 128 : rb * 128 + 128, :] = total.astype(BF16)


def call(kernel, outs, specs, scratch, flops, args):
    return pl.pallas_call(
        kernel,
        out_shape=outs,
        in_specs=specs,
        out_specs=jax.tree.map(lambda _: pl.BlockSpec(memory_space=pltpu.VMEM), outs),
        scratch_shapes=scratch,
        compiler_params=pltpu.CompilerParams(vmem_limit_bytes=40 * 2**20),
        cost_estimate=pl.CostEstimate(flops=flops, bytes_accessed=4 * 2**20, transcendentals=0),
    )(*args)


def shape(dims, dtype):
    return jax.ShapeDtypeStruct(dims, dtype)


def by_position(own, other, place):
    return jnp.where(place == 0, jnp.stack([own, other]), jnp.stack([other, own]))


def spectra(got):
    return call(
        spectra_kernel,
        (shape((1024, 256), F32), shape((1024, 256), F32)),
        whole(3),
        [pltpu.VMEM((512, 128), F32)],
        4 * 10**8,
        (got, jnp.asarray(MATRICES, BF16), jnp.asarray(TWIDDLES, F32)),
    )


def convolve(z, signal, taps, before, piece):
    return call(
        conv_kernel,
        shape((32, 48, 128), BF16),
        [SCALARS] + whole(6),
        [pltpu.VMEM((512, 128), F32)],
        6 * 10**8,
        (z, signal, taps, before, piece, jnp.asarray(MATRICES, BF16), jnp.asarray(TWIDDLES, F32)),
    )


def half_of(array, axis, which):
    return lax.dynamic_slice_in_dim(array, which * 128, 128, axis)


def per_device(tokens_in, pre_gain, w_in, w_out, long_filter, w_unembed, target_ids, score_mask):
    ctx, tp = lax.axis_index("ctx"), lax.axis_index("tp")
    core, z = ctx % 2, ctx // 32
    z_at = z.reshape(1).astype(jnp.int32)

    w_in = w_in.transpose(1, 0, 2)
    got = half_of(lax.ppermute(w_in, "ctx", PERM_CORE), 2, core)
    keep = half_of(w_in, 2, core)
    near = jnp.concatenate([jnp.where(core == 0, keep, got), jnp.where(core == 0, got, keep)], axis=1)
    near, taps = lax.optimization_barrier((near.reshape(384, 128), long_filter))
    taps_got = lax.ppermute(taps, "ctx", PERM_CORE)
    rows = w_out.reshape(4, 8, 4, 128).transpose(0, 2, 1, 3).reshape(128, 128)
    far = lax.ppermute(jnp.concatenate([near, rows]), "ctx", PERM_Z)
    near, tokens, taps_got = lax.optimization_barrier((near, tokens_in, taps_got))
    beside = lax.ppermute(tokens, "ctx", PERM_CORE)
    near = lax.all_to_all(
        jnp.broadcast_to(near, (4, 384, 128)), "ctx", 0, 0, axis_index_groups=GROUPS_X, tiled=True
    )

    rows = by_position(rows.reshape(4, 32, 128), far[384:].reshape(4, 32, 128), z)
    far = far[:384]
    far = jnp.stack([far] + [lax.ppermute(far, "ctx", PERM_Y[k]) for k in (1, 2, 3)])
    near, far, rows = lax.optimization_barrier((near, far, rows))

    near = jnp.broadcast_to(near.reshape(1, 1536, 128), (4, 1536, 128))
    near = jnp.concatenate([near, rows[0], rows[1]], axis=1)
    near = lax.all_to_all(near, "ctx", 0, 0, axis_index_groups=GROUPS_Y, tiled=True)
    fars = [far] + [lax.ppermute(far, "ctx", PERM_X[k]) for k in (1, 2, 3)]

    at = jnp.stack([(ctx // 8) % 4, (ctx // 2) % 4, core, z]).astype(jnp.int32)
    gained, scale = call(
        norm_kernel,
        (shape((2, 256, 4096), BF16), shape((2, 256, 128), F32)),
        [pl.BlockSpec(memory_space=pl.ANY)] * 2 + whole(1),
        [pltpu.VMEM((2, 256, 4096), BF16), pltpu.SemaphoreType.DMA((2, 4))],
        10**7,
        (tokens_in, beside, pre_gain.reshape(1, 4096)),
    )
    sums = call(
        near_kernel, shape((2, 256, 384), F32), [SCALARS] + whole(2), [], 8 * 10**8, (at, gained, near)
    )
    signal, gate = call(
        proj_kernel,
        (shape((16, 64, 128), BF16), shape((2, 2, 128, 128), BF16)),
        [SCALARS] + whole(9),
        [],
        8 * 10**8,
        (at, gained, scale, sums, taps, taps_got, *fars),
    )
    got = lax.all_to_all(signal, "ctx", 0, 0, axis_index_groups=GROUPS_CORE, tiled=True)
    before = lax.ppermute(got, "ctx", PERM_Z_UP)
    terms = call(product_kernel, shape((8, 32, 128), BF16), whole(2), [], 4 * 10**7, (near, w_unembed))
    terms, _ = lax.optimization_barrier((terms, got))
    piece = lax.all_to_all(terms, "tp", 0, 0, tiled=True)
    gate_keep = lax.dynamic_index_in_dim(gate, core, 0, False)
    gate_got = lax.ppermute(lax.dynamic_index_in_dim(gate, 1 - core, 0, False), "ctx", PERM_CORE)

    conv = convolve(z_at, *spectra(got), before, piece)
    conv = lax.all_to_all(conv, "ctx", 0, 0, axis_index_groups=GROUPS_PLANE, tiled=True)

    width = w_unembed.shape[0]
    base = mm(lax.dynamic_slice_in_dim(tokens_in, tp * width, width, 1), w_unembed)
    logits = call(
        mix_kernel,
        shape((256, 512), BF16),
        [SCALARS] + whole(4),
        [],
        10**8,
        (core.reshape(1).astype(jnp.int32), conv, gate_keep, gate_got, base),
    )
    logits = lax.all_to_all(logits.reshape(4, 64, 512), "tp", 0, 0, axis_index_groups=GROUPS_TP, tiled=True)
    logits = jnp.sum(logits.astype(F32), axis=0).astype(BF16)
    far = lax.ppermute(logits, "tp", [(i, i ^ 4) for i in range(8)])
    logits = logits.astype(F32) + far.astype(F32)

    row_top = jnp.max(logits, axis=1, keepdims=True)
    log_total = row_top[:, 0] + jnp.log(jnp.sum(jnp.exp(logits - row_top), axis=1))
    ids = lax.dynamic_slice_in_dim(target_ids, (tp % 4) * 64, 64, 0)
    mask = lax.dynamic_slice_in_dim(score_mask, (tp % 4) * 64, 64, 0)
    vocab_index = lax.broadcasted_iota(jnp.int32, (64, 512), 1)
    picked = jnp.sum(jnp.where(vocab_index == ids[:, None], logits, 0.0), axis=1)
    scores = (picked - log_total) * mask.astype(F32)
    scores = jnp.broadcast_to(scores[None, :], (4, 64))
    scores = lax.all_to_all(scores, "tp", 0, 0, axis_index_groups=GROUPS_TP, tiled=True)
    return scores.reshape(256)


def solution(mesh):
    return jax.shard_map(
        per_device,
        mesh=mesh,
        in_specs=(
            P("ctx", None),
            P(),
            P("ctx", None, "tp"),
            P("ctx", "tp"),
            P("ctx", "tp"),
            P("tp", None),
            P("ctx"),
            P("ctx"),
        ),
        out_specs=P("ctx"),
        check_vma=False,
    )
```

```python
import math

import jax
import jax.numpy as jnp
import numpy as np
from jax import lax
from jax.experimental import pallas as pl
from jax.experimental.pallas import tpu as pltpu
from jax.sharding import PartitionSpec as P

NORM_EPS = 1e-05
F32 = jnp.float32
BF16 = jnp.bfloat16

COORDS = [(z, y, x, c) for z in range(2) for y in range(4) for x in range(4) for c in range(2)]


def ctx_id(z, y, x, c):
    return ((z * 4 + y) * 4 + x) * 2 + c


def ctx_perm(move):
    return [(ctx_id(*at), ctx_id(*move(*at))) for at in COORDS]


PERM_CORE = ctx_perm(lambda z, y, x, c: (z, y, x, 1 - c))
PERM_Z = ctx_perm(lambda z, y, x, c: (1 - z, y, x, c))
PERM_Z_UP = [(i, i + 32) for i in range(32)]
PERM_X = [ctx_perm(lambda z, y, x, c, k=k: (z, y, (x + k) % 4, c)) for k in range(4)]
PERM_Y = [ctx_perm(lambda z, y, x, c, k=k: (z, (y + k) % 4, x, c)) for k in range(4)]
GROUPS_X = [[ctx_id(z, y, x, c) for x in range(4)] for z in range(2) for y in range(4) for c in range(2)]
GROUPS_Y = [[ctx_id(z, y, x, c) for y in range(4)] for z in range(2) for x in range(4) for c in range(2)]
GROUPS_PLANE = [
    [ctx_id(z, y, x, c) for y in range(4) for x in range(4) for c in range(2)] for z in range(2)
]
GROUPS_CORE = [
    [ctx_id(z, y, x, c) for y in range(4) for x in range(4)] for z in range(2) for c in range(2)
]
GROUPS_TP = [[0, 1, 2, 3], [4, 5, 6, 7]]


def tables():
    index = np.arange(128)
    inner = 2.0 * math.pi * (np.outer(index, index) % 128) / 128
    outer = 2.0 * math.pi * np.outer(index, index) / 16384
    cos, sin = np.cos(inner), np.sin(inner)
    first = np.concatenate([cos[:, :64], -sin[:, :64]], axis=0)
    second = np.block([[cos, -sin], [sin, cos]])
    back = np.block([[cos, sin], [-sin, cos]])
    last = np.concatenate([cos[:64], -sin[:64]], axis=1) / 16384.0
    return (first, second, back, last, np.cos(outer), np.sin(outer))


FIRST, SECOND, BACK, LAST, COS_TW, SIN_TW = tables()
MATRICES = np.concatenate([np.pad(FIRST, ((0, 0), (0, 192))), SECOND, BACK, LAST])
TWIDDLES = np.concatenate([COS_TW, SIN_TW], axis=1)


def mm(left, right):
    return jnp.dot(left, right, preferred_element_type=F32)


def whole(count):
    return [pl.BlockSpec(memory_space=pltpu.VMEM)] * count


SCALARS = pl.BlockSpec(memory_space=pltpu.SMEM)


def spectrum(scratch, matrices, twiddles):
    cos_tw, sin_tw = twiddles[:, :128], twiddles[:, 128:]
    cube = jnp.concatenate([scratch[pl.ds(c, 64, stride=8), :] for c in range(8)], axis=1)
    step = mm(matrices[:256, :64], cube.astype(BF16))
    parts = []
    for c in range(8):
        real, imag = step[:128, c * 128 : c * 128 + 128], step[128:, c * 128 : c * 128 + 128]
        parts.append(
            jnp.concatenate(
                [(real * cos_tw + imag * sin_tw).astype(BF16), (imag * cos_tw - real * sin_tw).astype(BF16)],
                axis=1,
            )
        )
    return mm(jnp.concatenate(parts, axis=0), matrices[256:512, :])


def rows_of(scratch, ref, at):
    for p in range(16):
        scratch[p * 32 : p * 32 + 32] = ref[p, at : at + 32].astype(F32)


def spectra_kernel(got_ref, matrices, twiddles, signal_ref, filter_ref, scratch):
    rows_of(scratch, got_ref, 0)
    signal_ref[...] = spectrum(scratch, matrices, twiddles)
    rows_of(scratch, got_ref, 32)
    filter_ref[...] = spectrum(scratch, matrices, twiddles)


def conv_kernel(z_ref, signal_ref, filter_ref, before_ref, piece_ref, matrices, twiddles, out_ref, scratch):
    upper = z_ref[0] == 1
    cos_tw, sin_tw = twiddles[:, :128], twiddles[:, 128:]
    own, high = signal_ref[...], filter_ref[...]
    rows_of(scratch, before_ref, 0)
    old = jnp.where(upper, spectrum(scratch, matrices, twiddles), 0.0)
    rows_of(scratch, before_ref, 32)
    low = jnp.where(upper, spectrum(scratch, matrices, twiddles), high)
    odd = lax.broadcasted_iota(jnp.int32, (1024, 256), 0) & 1
    every = jnp.where(odd == 1, -low, low) + high
    own_r, own_i, old_r, old_i = own[:, :128], own[:, 128:], old[:, :128], old[:, 128:]
    low_r, low_i, all_r, all_i = low[:, :128], low[:, 128:], every[:, :128], every[:, 128:]
    real = own_r * low_r - own_i * low_i + old_r * all_r - old_i * all_i
    imag = own_r * low_i + own_i * low_r + old_r * all_i + old_i * all_r
    half = mm(jnp.concatenate([real.astype(BF16), imag.astype(BF16)], axis=1), matrices[512:768, :])
    parts = []
    for c in range(8):
        real, imag = half[c * 128 : c * 128 + 128, :128], half[c * 128 : c * 128 + 128, 128:]
        parts.append(
            jnp.concatenate(
                [(real * cos_tw - imag * sin_tw).astype(BF16), (imag * cos_tw + real * sin_tw).astype(BF16)],
                axis=0,
            )
        )
    result = mm(matrices[768:, :], jnp.concatenate(parts, axis=1))
    for c in range(8):
        scratch[pl.ds(c, 64, stride=8), :] = result[:, c * 128 : c * 128 + 128]
    piece = sum(piece_ref[j].astype(F32) for j in range(8)).astype(BF16)
    for d in range(32):
        out_ref[d, :16] = scratch[d * 16 : d * 16 + 16].astype(BF16)
        out_ref[d, 16:] = piece


def weight_block(ref, lead, row):
    return jnp.concatenate([ref[lead, row + 128 * g : row + 128 * g + 128, :] for g in range(3)], axis=1)


def norm_kernel(own_hbm, beside_hbm, gain_ref, gained_ref, scale_ref, tokens, sems):
    gain = gain_ref[...]
    copies = []
    for part, ref in enumerate((own_hbm, beside_hbm)):
        for i in range(4):
            rows = slice(i * 64, i * 64 + 64)
            copies.append(pltpu.make_async_copy(ref.at[rows], tokens.at[part, rows], sems.at[part, i]))
    for copy in copies:
        copy.start()
    for k, copy in enumerate(copies):
        copy.wait()
        part, i = k // 4, k % 4
        for half in range(2):
            rows = slice(i * 64 + half * 32, i * 64 + half * 32 + 32)
            block = tokens[part, rows, :]
            stream = block.astype(F32)
            mean = jnp.mean(stream * stream, axis=1, keepdims=True)
            scale_ref[part, rows, :] = jnp.broadcast_to(lax.rsqrt(mean + NORM_EPS), (32, 128))
            gained_ref[part, rows, :] = block * gain


def near_kernel(at_ref, gained_ref, near_ref, out_ref):
    start = at_ref[3] * 2048
    for part in range(2):
        total = jnp.zeros((256, 384), F32)
        for y in range(4):
            for x in (0, 2):
                left = gained_ref[part, :, pl.ds(pl.multiple_of(start + (y * 4 + x) * 128, 128), 256)]
                right = [weight_block(near_ref, y, x * 384), weight_block(near_ref, y, x * 384 + 384)]
                total += mm(left, jnp.concatenate(right, axis=0))
        out_ref[part] = total


def product_kernel(rows_ref, unembed_ref, out_ref):
    blocks = []
    for z in range(2):
        for y in range(4):
            block = rows_ref[y, 1536 + z * 32 : 1568 + z * 32, :].astype(F32)
            blocks.append(jnp.concatenate([block[v * 8 : v * 8 + 8] for v in range(4)], axis=1))
    terms = mm(jnp.concatenate(blocks, axis=0).astype(BF16), unembed_ref[...])
    for j in range(8):
        parts = [terms[j * 8 : j * 8 + 8, v * 128 : v * 128 + 128] for v in range(4)]
        out_ref[j] = jnp.concatenate(parts, axis=0).astype(BF16)


def put_pieces(ref, row, place, block):
    first, second = block[:128].T, block[128:].T
    for p in range(16):
        b = p * 8
        rows = jnp.concatenate([first[b : b + 8], second[b : b + 8]], axis=0).astype(BF16)
        ref[p, pl.ds(pl.multiple_of(row + place * 16, 16), 16), :] = rows


def proj_kernel(at_ref, gained_ref, scale_ref, near_ref, own_taps, got_taps, f0, f1, f2, f3, sig_ref, gate_ref):
    y_at, x_at, core = at_ref[0], at_ref[1], at_ref[2]
    start = 2048 - at_ref[3] * 2048
    half = pl.ds(pl.multiple_of(core * 128, 128), 128)
    for part in range(2):
        total = near_ref[part]
        for step, ref in enumerate((f0, f1, f2, f3)):
            x = lax.rem(x_at + 4 - step, 4)
            for k in (0, 2):
                starts = [start + (lax.rem(y_at + 4 - j, 4) * 4 + x) * 128 for j in (k, k + 1)]
                left = [gained_ref[part, :, pl.ds(pl.multiple_of(at, 128), 128)] for at in starts]
                right = [weight_block(ref, k, 0), weight_block(ref, k + 1, 0)]
                total += mm(jnp.concatenate(left, axis=1), jnp.concatenate(right, axis=0))
        scale = scale_ref[part]
        proj = (total * jnp.concatenate([scale, scale, scale], axis=1)).astype(BF16).astype(F32)
        place = core if part == 0 else 1 - core
        put_pieces(sig_ref, 0, place, proj[:, 128:256] * proj[:, 256:])
        put_pieces(sig_ref, 32, place, (own_taps if part == 0 else got_taps)[:, half].astype(F32))
        gate_ref[place, 0] = proj[:128, :128].T.astype(BF16)
        gate_ref[place, 1] = proj[128:, :128].T.astype(BF16)


def mix_kernel(core_ref, got_ref, keep_ref, other_ref, base_ref, out_ref):
    core = core_ref[0]
    keep, other = keep_ref[...].astype(F32), other_ref[...].astype(F32)
    conv = got_ref[:, :16, :].astype(F32)
    for rb in range(2):
        total = base_ref[rb * 128 : rb * 128 + 128, :]
        for c in range(2):
            cube = jnp.concatenate([conv[b * 2 + c, rb * 8 : rb * 8 + 8] for b in range(16)], axis=0)
            gate = jnp.where(core == c, keep[rb], other[rb])
            mixed = (gate * cube).T.astype(BF16)
            weights = []
            for b in range(16):
                x, holder, y = (c * 16 + b) // 8, b % 8 // 4, b % 4
                piece = got_ref[(y * 4 + x) * 2 + holder, 16:, :].astype(F32)
                weights.append(jnp.concatenate([piece[v * 8 : v * 8 + 8] for v in range(4)], axis=1))
            total += mm(mixed, jnp.concatenate(weights, axis=0).astype(BF16))
        out_ref[rb * 128 : rb * 128 + 128, :] = total.astype(BF16)


def call(kernel, outs, specs, scratch, flops, args, mib=8):
    return pl.pallas_call(
        kernel,
        out_shape=outs,
        in_specs=specs,
        out_specs=jax.tree.map(lambda _: pl.BlockSpec(memory_space=pltpu.VMEM), outs),
        scratch_shapes=scratch,
        compiler_params=pltpu.CompilerParams(vmem_limit_bytes=mib * 2**20),
        cost_estimate=pl.CostEstimate(flops=flops, bytes_accessed=4 * 2**20, transcendentals=0),
    )(*args)


def shape(dims, dtype):
    return jax.ShapeDtypeStruct(dims, dtype)


def by_position(own, other, place):
    return jnp.where(place == 0, jnp.stack([own, other]), jnp.stack([other, own]))


def spectra(got):
    return call(
        spectra_kernel,
        (shape((1024, 256), F32), shape((1024, 256), F32)),
        whole(3),
        [pltpu.VMEM((512, 128), F32)],
        4 * 10**8,
        (got, jnp.asarray(MATRICES, BF16), jnp.asarray(TWIDDLES, F32)),
    )


def convolve(z, signal, taps, before, piece):
    return call(
        conv_kernel,
        shape((32, 48, 128), BF16),
        [SCALARS] + whole(6),
        [pltpu.VMEM((512, 128), F32)],
        6 * 10**8,
        (z, signal, taps, before, piece, jnp.asarray(MATRICES, BF16), jnp.asarray(TWIDDLES, F32)),
        mib=16,
    )


def half_of(array, axis, which):
    return lax.dynamic_slice_in_dim(array, which * 128, 128, axis)


def per_device(tokens_in, pre_gain, w_in, w_out, long_filter, w_unembed, target_ids, score_mask):
    ctx, tp = lax.axis_index("ctx"), lax.axis_index("tp")
    core, z = ctx % 2, ctx // 32
    z_at = z.reshape(1).astype(jnp.int32)

    w_in = w_in.transpose(1, 0, 2)
    got = half_of(lax.ppermute(w_in, "ctx", PERM_CORE), 2, core)
    keep = half_of(w_in, 2, core)
    near = jnp.concatenate([jnp.where(core == 0, keep, got), jnp.where(core == 0, got, keep)], axis=1)
    near = lax.optimization_barrier(near.reshape(384, 128))
    rows = w_out.reshape(4, 8, 4, 128).transpose(0, 2, 1, 3).reshape(128, 128)
    far = lax.ppermute(jnp.concatenate([near, rows]), "ctx", PERM_Z)
    near = lax.all_to_all(
        jnp.broadcast_to(near, (4, 384, 128)), "ctx", 0, 0, axis_index_groups=GROUPS_X, tiled=True
    )
    near, tokens, taps = lax.optimization_barrier((near, tokens_in, long_filter))
    beside = lax.ppermute(tokens, "ctx", PERM_CORE)
    taps_got = lax.ppermute(taps, "ctx", PERM_CORE)
    near, far = lax.optimization_barrier((near, far))

    rows = by_position(rows.reshape(4, 32, 128), far[384:].reshape(4, 32, 128), z)
    near = jnp.broadcast_to(near.reshape(1, 1536, 128), (4, 1536, 128))
    near = jnp.concatenate([near, rows[0], rows[1]], axis=1)
    near = lax.all_to_all(near, "ctx", 0, 0, axis_index_groups=GROUPS_Y, tiled=True)
    far = far[:384]
    far = jnp.stack([far] + [lax.ppermute(far, "ctx", PERM_Y[k]) for k in (1, 2, 3)])

    far = lax.optimization_barrier(far)
    fars = [far] + [lax.ppermute(far, "ctx", PERM_X[k]) for k in (1, 2, 3)]
    terms = call(product_kernel, shape((8, 32, 128), BF16), whole(2), [], 4 * 10**7, (near, w_unembed))
    piece = lax.all_to_all(terms, "tp", 0, 0, tiled=True)

    at = jnp.stack([(ctx // 8) % 4, (ctx // 2) % 4, core, z]).astype(jnp.int32)
    gained, scale = call(
        norm_kernel,
        (shape((2, 256, 4096), BF16), shape((2, 256, 128), F32)),
        [pl.BlockSpec(memory_space=pl.ANY)] * 2 + whole(1),
        [pltpu.VMEM((2, 256, 4096), BF16), pltpu.SemaphoreType.DMA((2, 4))],
        10**7,
        (tokens_in, beside, pre_gain.reshape(1, 4096)),
    )
    sums = call(
        near_kernel, shape((2, 256, 384), F32), [SCALARS] + whole(2), [], 8 * 10**8, (at, gained, near)
    )
    signal, gate = call(
        proj_kernel,
        (shape((16, 64, 128), BF16), shape((2, 2, 128, 128), BF16)),
        [SCALARS] + whole(9),
        [],
        8 * 10**8,
        (at, gained, scale, sums, taps, taps_got, *fars),
    )
    signal, piece = lax.optimization_barrier((signal, piece))
    got = lax.all_to_all(signal, "ctx", 0, 0, axis_index_groups=GROUPS_CORE, tiled=True)
    before = lax.ppermute(got, "ctx", PERM_Z_UP)
    gate_keep = lax.dynamic_index_in_dim(gate, core, 0, False)
    gate_got = lax.ppermute(lax.dynamic_index_in_dim(gate, 1 - core, 0, False), "ctx", PERM_CORE)

    conv = convolve(z_at, *spectra(got), before, piece)
    conv = lax.all_to_all(conv, "ctx", 0, 0, axis_index_groups=GROUPS_PLANE, tiled=True)

    width = w_unembed.shape[0]
    base = mm(lax.dynamic_slice_in_dim(tokens_in, tp * width, width, 1), w_unembed)
    logits = call(
        mix_kernel,
        shape((256, 512), BF16),
        [SCALARS] + whole(4),
        [],
        10**8,
        (core.reshape(1).astype(jnp.int32), conv, gate_keep, gate_got, base),
    )
    logits = lax.all_to_all(logits.reshape(4, 64, 512), "tp", 0, 0, axis_index_groups=GROUPS_TP, tiled=True)
    logits = jnp.sum(logits.astype(F32), axis=0).astype(BF16)
    far = lax.ppermute(logits, "tp", [(i, i ^ 4) for i in range(8)])
    logits = logits.astype(F32) + far.astype(F32)

    row_top = jnp.max(logits, axis=1, keepdims=True)
    log_total = row_top[:, 0] + jnp.log(jnp.sum(jnp.exp(logits - row_top), axis=1))
    ids = lax.dynamic_slice_in_dim(target_ids, (tp % 4) * 64, 64, 0)
    mask = lax.dynamic_slice_in_dim(score_mask, (tp % 4) * 64, 64, 0)
    vocab_index = lax.broadcasted_iota(jnp.int32, (64, 512), 1)
    picked = jnp.sum(jnp.where(vocab_index == ids[:, None], logits, 0.0), axis=1)
    scores = (picked - log_total) * mask.astype(F32)
    scores = jnp.broadcast_to(scores[None, :], (4, 64))
    scores = lax.all_to_all(scores, "tp", 0, 0, axis_index_groups=GROUPS_TP, tiled=True)
    return scores.reshape(256)


def solution(mesh):
    return jax.shard_map(
        per_device,
        mesh=mesh,
        in_specs=(
            P("ctx", None),
            P(),
            P("ctx", None, "tp"),
            P("ctx", "tp"),
            P("ctx", "tp"),
            P("tp", None),
            P("ctx"),
            P("ctx"),
        ),
        out_specs=P("ctx"),
        check_vma=False,
    )
```

```python
import math

import jax
import jax.numpy as jnp
import numpy as np
from jax import lax
from jax.experimental import pallas as pl
from jax.experimental.pallas import tpu as pltpu
from jax.sharding import PartitionSpec as P

NORM_EPS = 1e-05
F32 = jnp.float32
BF16 = jnp.bfloat16

COORDS = [(z, y, x, c) for z in range(2) for y in range(4) for x in range(4) for c in range(2)]


def ctx_id(z, y, x, c):
    return ((z * 4 + y) * 4 + x) * 2 + c


def ctx_perm(move):
    return [(ctx_id(*at), ctx_id(*move(*at))) for at in COORDS]


PERM_CORE = ctx_perm(lambda z, y, x, c: (z, y, x, 1 - c))
PERM_Z = ctx_perm(lambda z, y, x, c: (1 - z, y, x, c))
PERM_Z_UP = [(i, i + 32) for i in range(32)]
PERM_X = [ctx_perm(lambda z, y, x, c, k=k: (z, y, (x + k) % 4, c)) for k in range(4)]
PERM_Y = [ctx_perm(lambda z, y, x, c, k=k: (z, (y + k) % 4, x, c)) for k in range(4)]
GROUPS_X = [[ctx_id(z, y, x, c) for x in range(4)] for z in range(2) for y in range(4) for c in range(2)]
GROUPS_Y = [[ctx_id(z, y, x, c) for y in range(4)] for z in range(2) for x in range(4) for c in range(2)]
GROUPS_PLANE = [
    [ctx_id(z, y, x, c) for y in range(4) for x in range(4) for c in range(2)] for z in range(2)
]
GROUPS_CORE = [
    [ctx_id(z, y, x, c) for y in range(4) for x in range(4)] for z in range(2) for c in range(2)
]
GROUPS_TP = [[0, 1, 2, 3], [4, 5, 6, 7]]


def tables():
    index = np.arange(128)
    inner = 2.0 * math.pi * (np.outer(index, index) % 128) / 128
    outer = 2.0 * math.pi * np.outer(index, index) / 16384
    cos, sin = np.cos(inner), np.sin(inner)
    first = np.concatenate([cos[:, :64], -sin[:, :64]], axis=0)
    second = np.block([[cos, -sin], [sin, cos]])
    back = np.block([[cos, sin], [-sin, cos]])
    last = np.concatenate([cos[:64], -sin[:64]], axis=1) / 16384.0
    return (first, second, back, last, np.cos(outer), np.sin(outer))


FIRST, SECOND, BACK, LAST, COS_TW, SIN_TW = tables()
MATRICES = np.concatenate([np.pad(FIRST, ((0, 0), (0, 192))), SECOND, BACK, LAST])
TWIDDLES = np.concatenate([COS_TW, SIN_TW], axis=1)


def mm(left, right):
    return jnp.dot(left, right, preferred_element_type=F32)


def whole(count):
    return [pl.BlockSpec(memory_space=pltpu.VMEM)] * count


SCALARS = pl.BlockSpec(memory_space=pltpu.SMEM)


def spectrum(scratch, matrices, twiddles):
    cos_tw, sin_tw = twiddles[:, :128], twiddles[:, 128:]
    cube = jnp.concatenate([scratch[pl.ds(c, 64, stride=8), :] for c in range(8)], axis=1)
    step = mm(matrices[:256, :64], cube.astype(BF16))
    parts = []
    for c in range(8):
        real, imag = step[:128, c * 128 : c * 128 + 128], step[128:, c * 128 : c * 128 + 128]
        parts.append(
            jnp.concatenate(
                [(real * cos_tw + imag * sin_tw).astype(BF16), (imag * cos_tw - real * sin_tw).astype(BF16)],
                axis=1,
            )
        )
    return mm(jnp.concatenate(parts, axis=0), matrices[256:512, :])


def rows_of(scratch, ref, at):
    for p in range(16):
        scratch[p * 32 : p * 32 + 32] = ref[p, at : at + 32].astype(F32)


def spectra_kernel(got_ref, matrices, twiddles, signal_ref, filter_ref, scratch):
    rows_of(scratch, got_ref, 0)
    signal_ref[...] = spectrum(scratch, matrices, twiddles)
    rows_of(scratch, got_ref, 32)
    filter_ref[...] = spectrum(scratch, matrices, twiddles)


def conv_kernel(z_ref, signal_ref, filter_ref, before_ref, piece_ref, matrices, twiddles, out_ref, scratch):
    upper = z_ref[0] == 1
    cos_tw, sin_tw = twiddles[:, :128], twiddles[:, 128:]
    own, high = signal_ref[...], filter_ref[...]
    rows_of(scratch, before_ref, 0)
    old = jnp.where(upper, spectrum(scratch, matrices, twiddles), 0.0)
    rows_of(scratch, before_ref, 32)
    low = jnp.where(upper, spectrum(scratch, matrices, twiddles), high)
    odd = lax.broadcasted_iota(jnp.int32, (1024, 256), 0) & 1
    every = jnp.where(odd == 1, -low, low) + high
    own_r, own_i, old_r, old_i = own[:, :128], own[:, 128:], old[:, :128], old[:, 128:]
    low_r, low_i, all_r, all_i = low[:, :128], low[:, 128:], every[:, :128], every[:, 128:]
    real = own_r * low_r - own_i * low_i + old_r * all_r - old_i * all_i
    imag = own_r * low_i + own_i * low_r + old_r * all_i + old_i * all_r
    half = mm(jnp.concatenate([real.astype(BF16), imag.astype(BF16)], axis=1), matrices[512:768, :])
    parts = []
    for c in range(8):
        real, imag = half[c * 128 : c * 128 + 128, :128], half[c * 128 : c * 128 + 128, 128:]
        parts.append(
            jnp.concatenate(
                [(real * cos_tw - imag * sin_tw).astype(BF16), (imag * cos_tw + real * sin_tw).astype(BF16)],
                axis=0,
            )
        )
    result = mm(matrices[768:, :], jnp.concatenate(parts, axis=1))
    for c in range(8):
        scratch[pl.ds(c, 64, stride=8), :] = result[:, c * 128 : c * 128 + 128]
    piece = sum(piece_ref[j].astype(F32) for j in range(8)).astype(BF16)
    for d in range(32):
        out_ref[d, :16] = scratch[d * 16 : d * 16 + 16].astype(BF16)
        out_ref[d, 16:] = piece


def weight_block(ref, lead, row):
    return jnp.concatenate([ref[lead, row + 128 * g : row + 128 * g + 128, :] for g in range(3)], axis=1)


def norm_kernel(own_hbm, beside_hbm, gain_ref, gained_ref, scale_ref, tokens, sems):
    gain = gain_ref[...]
    copies = []
    for part, ref in enumerate((own_hbm, beside_hbm)):
        for i in range(4):
            rows = slice(i * 64, i * 64 + 64)
            copies.append(pltpu.make_async_copy(ref.at[rows], tokens.at[part, rows], sems.at[part, i]))
    for copy in copies:
        copy.start()
    for k, copy in enumerate(copies):
        copy.wait()
        part, i = k // 4, k % 4
        for half in range(2):
            rows = slice(i * 64 + half * 32, i * 64 + half * 32 + 32)
            block = tokens[part, rows, :]
            stream = block.astype(F32)
            mean = jnp.mean(stream * stream, axis=1, keepdims=True)
            scale_ref[part, rows, :] = jnp.broadcast_to(lax.rsqrt(mean + NORM_EPS), (32, 128))
            gained_ref[part, rows, :] = block * gain


def near_kernel(at_ref, gained_ref, near_ref, out_ref):
    start = at_ref[3] * 2048
    for part in range(2):
        total = jnp.zeros((256, 384), F32)
        for y in range(4):
            for x in (0, 2):
                left = gained_ref[part, :, pl.ds(pl.multiple_of(start + (y * 4 + x) * 128, 128), 256)]
                right = [weight_block(near_ref, y, x * 384), weight_block(near_ref, y, x * 384 + 384)]
                total += mm(left, jnp.concatenate(right, axis=0))
        out_ref[part] = total


def product_kernel(rows_ref, unembed_ref, out_ref):
    blocks = []
    for z in range(2):
        for y in range(4):
            block = rows_ref[y, 1536 + z * 32 : 1568 + z * 32, :].astype(F32)
            blocks.append(jnp.concatenate([block[v * 8 : v * 8 + 8] for v in range(4)], axis=1))
    terms = mm(jnp.concatenate(blocks, axis=0).astype(BF16), unembed_ref[...])
    for j in range(8):
        parts = [terms[j * 8 : j * 8 + 8, v * 128 : v * 128 + 128] for v in range(4)]
        out_ref[j] = jnp.concatenate(parts, axis=0).astype(BF16)


def put_pieces(ref, row, place, block):
    first, second = block[:128].T, block[128:].T
    for p in range(16):
        b = p * 8
        rows = jnp.concatenate([first[b : b + 8], second[b : b + 8]], axis=0).astype(BF16)
        ref[p, pl.ds(pl.multiple_of(row + place * 16, 16), 16), :] = rows


def proj_kernel(at_ref, gained_ref, scale_ref, near_ref, own_taps, got_taps, f0, f1, f2, f3, sig_ref, gate_ref):
    y_at, x_at, core = at_ref[0], at_ref[1], at_ref[2]
    start = 2048 - at_ref[3] * 2048
    half = pl.ds(pl.multiple_of(core * 128, 128), 128)
    for part in range(2):
        total = near_ref[part]
        for step, ref in enumerate((f0, f1, f2, f3)):
            x = lax.rem(x_at + 4 - step, 4)
            for k in (0, 2):
                starts = [start + (lax.rem(y_at + 4 - j, 4) * 4 + x) * 128 for j in (k, k + 1)]
                left = [gained_ref[part, :, pl.ds(pl.multiple_of(at, 128), 128)] for at in starts]
                right = [weight_block(ref, k, 0), weight_block(ref, k + 1, 0)]
                total += mm(jnp.concatenate(left, axis=1), jnp.concatenate(right, axis=0))
        scale = scale_ref[part]
        proj = (total * jnp.concatenate([scale, scale, scale], axis=1)).astype(BF16).astype(F32)
        place = core if part == 0 else 1 - core
        put_pieces(sig_ref, 0, place, proj[:, 128:256] * proj[:, 256:])
        put_pieces(sig_ref, 32, place, (own_taps if part == 0 else got_taps)[:, half].astype(F32))
        gate_ref[place, 0] = proj[:128, :128].T.astype(BF16)
        gate_ref[place, 1] = proj[128:, :128].T.astype(BF16)


def mix_kernel(core_ref, got_ref, keep_ref, other_ref, base_ref, out_ref):
    core = core_ref[0]
    keep, other = keep_ref[...].astype(F32), other_ref[...].astype(F32)
    conv = got_ref[:, :16, :].astype(F32)
    for rb in range(2):
        total = base_ref[rb * 128 : rb * 128 + 128, :]
        for c in range(2):
            cube = jnp.concatenate([conv[b * 2 + c, rb * 8 : rb * 8 + 8] for b in range(16)], axis=0)
            gate = jnp.where(core == c, keep[rb], other[rb])
            mixed = (gate * cube).T.astype(BF16)
            weights = []
            for b in range(16):
                x, holder, y = (c * 16 + b) // 8, b % 8 // 4, b % 4
                piece = got_ref[(y * 4 + x) * 2 + holder, 16:, :].astype(F32)
                weights.append(jnp.concatenate([piece[v * 8 : v * 8 + 8] for v in range(4)], axis=1))
            total += mm(mixed, jnp.concatenate(weights, axis=0).astype(BF16))
        out_ref[rb * 128 : rb * 128 + 128, :] = total.astype(BF16)


def call(kernel, outs, specs, scratch, flops, args, mib=8):
    return pl.pallas_call(
        kernel,
        out_shape=outs,
        in_specs=specs,
        out_specs=jax.tree.map(lambda _: pl.BlockSpec(memory_space=pltpu.VMEM), outs),
        scratch_shapes=scratch,
        compiler_params=pltpu.CompilerParams(vmem_limit_bytes=mib * 2**20),
        cost_estimate=pl.CostEstimate(flops=flops, bytes_accessed=4 * 2**20, transcendentals=0),
    )(*args)


def shape(dims, dtype):
    return jax.ShapeDtypeStruct(dims, dtype)


def by_position(own, other, place):
    return jnp.where(place == 0, jnp.stack([own, other]), jnp.stack([other, own]))


def spectra(got):
    return call(
        spectra_kernel,
        (shape((1024, 256), F32), shape((1024, 256), F32)),
        whole(3),
        [pltpu.VMEM((512, 128), F32)],
        4 * 10**8,
        (got, jnp.asarray(MATRICES, BF16), jnp.asarray(TWIDDLES, F32)),
    )


def convolve(z, signal, taps, before, piece):
    return call(
        conv_kernel,
        shape((32, 48, 128), BF16),
        [SCALARS] + whole(6),
        [pltpu.VMEM((512, 128), F32)],
        6 * 10**8,
        (z, signal, taps, before, piece, jnp.asarray(MATRICES, BF16), jnp.asarray(TWIDDLES, F32)),
        mib=16,
    )


def half_of(array, axis, which):
    return lax.dynamic_slice_in_dim(array, which * 128, 128, axis)


def per_device(tokens_in, pre_gain, w_in, w_out, long_filter, w_unembed, target_ids, score_mask):
    ctx, tp = lax.axis_index("ctx"), lax.axis_index("tp")
    core, z = ctx % 2, ctx // 32
    z_at = z.reshape(1).astype(jnp.int32)

    w_in = w_in.transpose(1, 0, 2)
    got = half_of(lax.ppermute(w_in, "ctx", PERM_CORE), 2, core)
    keep = half_of(w_in, 2, core)
    near = jnp.concatenate([jnp.where(core == 0, keep, got), jnp.where(core == 0, got, keep)], axis=1)
    near, taps = lax.optimization_barrier((near.reshape(384, 128), long_filter))
    taps_got = lax.ppermute(taps, "ctx", PERM_CORE)
    rows = w_out.reshape(4, 8, 4, 128).transpose(0, 2, 1, 3).reshape(128, 128)
    far = lax.ppermute(jnp.concatenate([near, rows]), "ctx", PERM_Z)
    near, tokens, taps_got = lax.optimization_barrier((near, tokens_in, taps_got))
    beside = lax.ppermute(tokens, "ctx", PERM_CORE)
    near = lax.all_to_all(
        jnp.broadcast_to(near, (4, 384, 128)), "ctx", 0, 0, axis_index_groups=GROUPS_X, tiled=True
    )

    rows = by_position(rows.reshape(4, 32, 128), far[384:].reshape(4, 32, 128), z)
    far = far[:384]
    far = jnp.stack([far] + [lax.ppermute(far, "ctx", PERM_Y[k]) for k in (1, 2, 3)])
    near, far, rows = lax.optimization_barrier((near, far, rows))

    near = jnp.broadcast_to(near.reshape(1, 1536, 128), (4, 1536, 128))
    near = jnp.concatenate([near, rows[0], rows[1]], axis=1)
    near = lax.all_to_all(near, "ctx", 0, 0, axis_index_groups=GROUPS_Y, tiled=True)
    fars = [far] + [lax.ppermute(far, "ctx", PERM_X[k]) for k in (1, 2, 3)]

    at = jnp.stack([(ctx // 8) % 4, (ctx // 2) % 4, core, z]).astype(jnp.int32)
    gained, scale = call(
        norm_kernel,
        (shape((2, 256, 4096), BF16), shape((2, 256, 128), F32)),
        [pl.BlockSpec(memory_space=pl.ANY)] * 2 + whole(1),
        [pltpu.VMEM((2, 256, 4096), BF16), pltpu.SemaphoreType.DMA((2, 4))],
        10**7,
        (tokens_in, beside, pre_gain.reshape(1, 4096)),
    )
    sums = call(
        near_kernel, shape((2, 256, 384), F32), [SCALARS] + whole(2), [], 8 * 10**8, (at, gained, near)
    )
    signal, gate = call(
        proj_kernel,
        (shape((16, 64, 128), BF16), shape((2, 2, 128, 128), BF16)),
        [SCALARS] + whole(9),
        [],
        8 * 10**8,
        (at, gained, scale, sums, taps, taps_got, *fars),
    )
    got = lax.all_to_all(signal, "ctx", 0, 0, axis_index_groups=GROUPS_CORE, tiled=True)
    before = lax.ppermute(got, "ctx", PERM_Z_UP)
    terms = call(product_kernel, shape((8, 32, 128), BF16), whole(2), [], 4 * 10**7, (near, w_unembed))
    terms, _ = lax.optimization_barrier((terms, got))
    piece = lax.all_to_all(terms, "tp", 0, 0, tiled=True)
    gate_keep = lax.dynamic_index_in_dim(gate, core, 0, False)
    gate_got = lax.ppermute(lax.dynamic_index_in_dim(gate, 1 - core, 0, False), "ctx", PERM_CORE)

    conv = convolve(z_at, *spectra(got), before, piece)
    conv = lax.all_to_all(conv, "ctx", 0, 0, axis_index_groups=GROUPS_PLANE, tiled=True)

    width = w_unembed.shape[0]
    base = mm(lax.dynamic_slice_in_dim(tokens_in, tp * width, width, 1), w_unembed)
    logits = call(
        mix_kernel,
        shape((256, 512), BF16),
        [SCALARS] + whole(4),
        [],
        10**8,
        (core.reshape(1).astype(jnp.int32), conv, gate_keep, gate_got, base),
    )
    logits = lax.all_to_all(logits.reshape(4, 64, 512), "tp", 0, 0, axis_index_groups=GROUPS_TP, tiled=True)
    logits = jnp.sum(logits.astype(F32), axis=0).astype(BF16)
    far = lax.ppermute(logits, "tp", [(i, i ^ 4) for i in range(8)])
    logits = logits.astype(F32) + far.astype(F32)

    row_top = jnp.max(logits, axis=1, keepdims=True)
    log_total = row_top[:, 0] + jnp.log(jnp.sum(jnp.exp(logits - row_top), axis=1))
    ids = lax.dynamic_slice_in_dim(target_ids, (tp % 4) * 64, 64, 0)
    mask = lax.dynamic_slice_in_dim(score_mask, (tp % 4) * 64, 64, 0)
    vocab_index = lax.broadcasted_iota(jnp.int32, (64, 512), 1)
    picked = jnp.sum(jnp.where(vocab_index == ids[:, None], logits, 0.0), axis=1)
    scores = (picked - log_total) * mask.astype(F32)
    scores = jnp.broadcast_to(scores[None, :], (4, 64))
    scores = lax.all_to_all(scores, "tp", 0, 0, axis_index_groups=GROUPS_TP, tiled=True)
    return scores.reshape(256)


def solution(mesh):
    return jax.shard_map(
        per_device,
        mesh=mesh,
        in_specs=(
            P("ctx", None),
            P(),
            P("ctx", None, "tp"),
            P("ctx", "tp"),
            P("ctx", "tp"),
            P("tp", None),
            P("ctx"),
            P("ctx"),
        ),
        out_specs=P("ctx"),
        check_vma=False,
    )
```

```python
import math

import jax
import jax.numpy as jnp
import numpy as np
from jax import lax
from jax.experimental import pallas as pl
from jax.experimental.pallas import tpu as pltpu
from jax.sharding import PartitionSpec as P

NORM_EPS = 1e-05
F32 = jnp.float32
BF16 = jnp.bfloat16

COORDS = [(z, y, x, c) for z in range(2) for y in range(4) for x in range(4) for c in range(2)]


def ctx_id(z, y, x, c):
    return ((z * 4 + y) * 4 + x) * 2 + c


def ctx_perm(move):
    return [(ctx_id(*at), ctx_id(*move(*at))) for at in COORDS]


PERM_CORE = ctx_perm(lambda z, y, x, c: (z, y, x, 1 - c))
PERM_Z = ctx_perm(lambda z, y, x, c: (1 - z, y, x, c))
PERM_Z_UP = [(i, i + 32) for i in range(32)]
PERM_X = [ctx_perm(lambda z, y, x, c, k=k: (z, y, (x + k) % 4, c)) for k in range(4)]
PERM_Y = [ctx_perm(lambda z, y, x, c, k=k: (z, (y + k) % 4, x, c)) for k in range(4)]
GROUPS_X = [[ctx_id(z, y, x, c) for x in range(4)] for z in range(2) for y in range(4) for c in range(2)]
GROUPS_Y = [[ctx_id(z, y, x, c) for y in range(4)] for z in range(2) for x in range(4) for c in range(2)]
GROUPS_PLANE = [
    [ctx_id(z, y, x, c) for y in range(4) for x in range(4) for c in range(2)] for z in range(2)
]
GROUPS_CORE = [
    [ctx_id(z, y, x, c) for y in range(4) for x in range(4)] for z in range(2) for c in range(2)
]
GROUPS_TP = [[0, 1, 2, 3], [4, 5, 6, 7]]


def tables():
    index = np.arange(128)
    inner = 2.0 * math.pi * (np.outer(index, index) % 128) / 128
    outer = 2.0 * math.pi * np.outer(index, index) / 16384
    cos, sin = np.cos(inner), np.sin(inner)
    first = np.concatenate([cos[:, :64], -sin[:, :64]], axis=0)
    second = np.block([[cos, -sin], [sin, cos]])
    back = np.block([[cos, sin], [-sin, cos]])
    last = np.concatenate([cos[:64], -sin[:64]], axis=1) / 16384.0
    return (first, second, back, last, np.cos(outer), np.sin(outer))


FIRST, SECOND, BACK, LAST, COS_TW, SIN_TW = tables()
MATRICES = np.concatenate([np.pad(FIRST, ((0, 0), (0, 192))), SECOND, BACK, LAST])
TWIDDLES = np.concatenate([COS_TW, SIN_TW], axis=1)


def mm(left, right):
    return jnp.dot(left, right, preferred_element_type=F32)


def whole(count):
    return [pl.BlockSpec(memory_space=pltpu.VMEM)] * count


SCALARS = pl.BlockSpec(memory_space=pltpu.SMEM)


def spectrum(scratch, matrices, twiddles):
    cos_tw, sin_tw = twiddles[:, :128], twiddles[:, 128:]
    cube = jnp.concatenate([scratch[pl.ds(c, 64, stride=8), :] for c in range(8)], axis=1)
    step = mm(matrices[:256, :64], cube.astype(BF16))
    parts = []
    for c in range(8):
        real, imag = step[:128, c * 128 : c * 128 + 128], step[128:, c * 128 : c * 128 + 128]
        parts.append(
            jnp.concatenate(
                [(real * cos_tw + imag * sin_tw).astype(BF16), (imag * cos_tw - real * sin_tw).astype(BF16)],
                axis=1,
            )
        )
    return mm(jnp.concatenate(parts, axis=0), matrices[256:512, :])


def rows_of(scratch, ref, at):
    for p in range(16):
        scratch[p * 32 : p * 32 + 32] = ref[p, at : at + 32].astype(F32)


def spectra_kernel(got_ref, matrices, twiddles, signal_ref, filter_ref, scratch):
    rows_of(scratch, got_ref, 0)
    signal_ref[...] = spectrum(scratch, matrices, twiddles)
    rows_of(scratch, got_ref, 32)
    filter_ref[...] = spectrum(scratch, matrices, twiddles)


def conv_kernel(z_ref, signal_ref, filter_ref, before_ref, matrices, twiddles, out_ref, scratch):
    upper = z_ref[0] == 1
    cos_tw, sin_tw = twiddles[:, :128], twiddles[:, 128:]
    own, high = signal_ref[...], filter_ref[...]
    rows_of(scratch, before_ref, 0)
    old = jnp.where(upper, spectrum(scratch, matrices, twiddles), 0.0)
    rows_of(scratch, before_ref, 32)
    low = jnp.where(upper, spectrum(scratch, matrices, twiddles), high)
    odd = lax.broadcasted_iota(jnp.int32, (1024, 256), 0) & 1
    every = jnp.where(odd == 1, -low, low) + high
    own_r, own_i, old_r, old_i = own[:, :128], own[:, 128:], old[:, :128], old[:, 128:]
    low_r, low_i, all_r, all_i = low[:, :128], low[:, 128:], every[:, :128], every[:, 128:]
    real = own_r * low_r - own_i * low_i + old_r * all_r - old_i * all_i
    imag = own_r * low_i + own_i * low_r + old_r * all_i + old_i * all_r
    half = mm(jnp.concatenate([real.astype(BF16), imag.astype(BF16)], axis=1), matrices[512:768, :])
    parts = []
    for c in range(8):
        real, imag = half[c * 128 : c * 128 + 128, :128], half[c * 128 : c * 128 + 128, 128:]
        parts.append(
            jnp.concatenate(
                [(real * cos_tw - imag * sin_tw).astype(BF16), (imag * cos_tw + real * sin_tw).astype(BF16)],
                axis=0,
            )
        )
    result = mm(matrices[768:, :], jnp.concatenate(parts, axis=1))
    for c in range(8):
        scratch[pl.ds(c, 64, stride=8), :] = result[:, c * 128 : c * 128 + 128]
    for d in range(32):
        out_ref[d] = scratch[d * 16 : d * 16 + 16].astype(BF16)


def pack_kernel(conv_ref, terms_ref, out_ref):
    piece = sum(terms_ref[j].astype(F32) for j in range(8)).astype(BF16)
    for d in range(32):
        out_ref[d, :16] = conv_ref[d]
        out_ref[d, 16:] = piece


def first_kernel(core_ref, own_ref, got_ref, rows_ref, out_ref):
    core = core_ref[0]
    half = pl.ds(pl.multiple_of(core * 128, 128), 128)
    for g in range(3):
        own, got = own_ref[g, :, half], got_ref[g, :, half]
        out_ref[g * 128 : g * 128 + 64] = jnp.where(core == 0, own, got)
        out_ref[g * 128 + 64 : g * 128 + 128] = jnp.where(core == 0, got, own)
    rows = rows_ref[...].astype(F32)
    blocks = [rows[y * 8 : y * 8 + 8, v * 128 : v * 128 + 128] for y in range(4) for v in range(4)]
    out_ref[384:] = jnp.concatenate(blocks, axis=0).astype(BF16)


def copies_kernel(first_ref, out_ref):
    for k in range(4):
        out_ref[k] = first_ref[:384]


def weight_block(ref, lead, row):
    return jnp.concatenate([ref[lead, row + 128 * g : row + 128 * g + 128, :] for g in range(3)], axis=1)


def near_kernel(
    at_ref, own_hbm, beside_hbm, gain_ref, near_ref, gained_ref, scale_ref, out_ref, tokens, sems
):
    start = at_ref[3] * 2048
    gain = gain_ref[...]
    copies = []
    for part, ref in enumerate((own_hbm, beside_hbm)):
        for i in range(4):
            rows = slice(i * 64, i * 64 + 64)
            copies.append(pltpu.make_async_copy(ref.at[rows], tokens.at[part, rows], sems.at[part, i]))
    for copy in copies:
        copy.start()
    for part in range(2):
        for i in range(4):
            copies[part * 4 + i].wait()
            for half in range(2):
                rows = slice(i * 64 + half * 32, i * 64 + half * 32 + 32)
                block = tokens[part, rows, :]
                stream = block.astype(F32)
                mean = jnp.mean(stream * stream, axis=1, keepdims=True)
                scale_ref[part, rows, :] = jnp.broadcast_to(lax.rsqrt(mean + NORM_EPS), (32, 128))
                gained_ref[part, rows, :] = block * gain
        total = jnp.zeros((256, 384), F32)
        for y in range(4):
            for x in (0, 2):
                left = gained_ref[part, :, pl.ds(pl.multiple_of(start + (y * 4 + x) * 128, 128), 256)]
                right = [weight_block(near_ref, y, x * 384), weight_block(near_ref, y, x * 384 + 384)]
                total += mm(left, jnp.concatenate(right, axis=0))
        out_ref[part] = total


def product_kernel(rows_ref, unembed_ref, out_ref):
    blocks = []
    for z in range(2):
        for y in range(4):
            block = rows_ref[y, 1536 + z * 32 : 1568 + z * 32, :].astype(F32)
            blocks.append(jnp.concatenate([block[v * 8 : v * 8 + 8] for v in range(4)], axis=1))
    terms = mm(jnp.concatenate(blocks, axis=0).astype(BF16), unembed_ref[...])
    for j in range(8):
        parts = [terms[j * 8 : j * 8 + 8, v * 128 : v * 128 + 128] for v in range(4)]
        out_ref[j] = jnp.concatenate(parts, axis=0).astype(BF16)


def put_pieces(ref, row, place, block):
    first, second = block[:128].T, block[128:].T
    for p in range(16):
        b = p * 8
        rows = jnp.concatenate([first[b : b + 8], second[b : b + 8]], axis=0).astype(BF16)
        ref[p, pl.ds(pl.multiple_of(row + place * 16, 16), 16), :] = rows


def proj_kernel(at_ref, gained_ref, scale_ref, near_ref, own_taps, got_taps, f0, f1, f2, f3, sig_ref, gate_ref):
    y_at, x_at, core = at_ref[0], at_ref[1], at_ref[2]
    start = 2048 - at_ref[3] * 2048
    half = pl.ds(pl.multiple_of(core * 128, 128), 128)
    for part in range(2):
        total = near_ref[part]
        for step, ref in enumerate((f0, f1, f2, f3)):
            x = lax.rem(x_at + 4 - step, 4)
            for k in (0, 2):
                starts = [start + (lax.rem(y_at + 4 - j, 4) * 4 + x) * 128 for j in (k, k + 1)]
                left = [gained_ref[part, :, pl.ds(pl.multiple_of(at, 128), 128)] for at in starts]
                right = [weight_block(ref, k, 0), weight_block(ref, k + 1, 0)]
                total += mm(jnp.concatenate(left, axis=1), jnp.concatenate(right, axis=0))
        scale = scale_ref[part]
        proj = (total * jnp.concatenate([scale, scale, scale], axis=1)).astype(BF16).astype(F32)
        place = core if part == 0 else 1 - core
        put_pieces(sig_ref, 0, place, proj[:, 128:256] * proj[:, 256:])
        put_pieces(sig_ref, 32, place, (own_taps if part == 0 else got_taps)[:, half].astype(F32))
        gate_ref[place, 0] = proj[:128, :128].T.astype(BF16)
        gate_ref[place, 1] = proj[128:, :128].T.astype(BF16)


def mix_kernel(core_ref, got_ref, keep_ref, other_ref, base_ref, out_ref):
    core = core_ref[0]
    keep, other = keep_ref[...].astype(F32), other_ref[...].astype(F32)
    conv = got_ref[:, :16, :].astype(F32)
    for rb in range(2):
        total = base_ref[rb * 128 : rb * 128 + 128, :]
        for c in range(2):
            cube = jnp.concatenate([conv[b * 2 + c, rb * 8 : rb * 8 + 8] for b in range(16)], axis=0)
            gate = jnp.where(core == c, keep[rb], other[rb])
            mixed = (gate * cube).T.astype(BF16)
            weights = []
            for b in range(16):
                x, holder, y = (c * 16 + b) // 8, b % 8 // 4, b % 4
                piece = got_ref[(y * 4 + x) * 2 + holder, 16:, :].astype(F32)
                weights.append(jnp.concatenate([piece[v * 8 : v * 8 + 8] for v in range(4)], axis=1))
            total += mm(mixed, jnp.concatenate(weights, axis=0).astype(BF16))
        out_ref[rb * 128 : rb * 128 + 128, :] = total.astype(BF16)


def call(kernel, outs, specs, scratch, flops, args, mib=8):
    return pl.pallas_call(
        kernel,
        out_shape=outs,
        in_specs=specs,
        out_specs=jax.tree.map(lambda _: pl.BlockSpec(memory_space=pltpu.VMEM), outs),
        scratch_shapes=scratch,
        compiler_params=pltpu.CompilerParams(vmem_limit_bytes=mib * 2**20),
        cost_estimate=pl.CostEstimate(flops=flops, bytes_accessed=4 * 2**20, transcendentals=0),
    )(*args)


def shape(dims, dtype):
    return jax.ShapeDtypeStruct(dims, dtype)


def by_position(own, other, place):
    return jnp.where(place == 0, jnp.stack([own, other]), jnp.stack([other, own]))


def spectra(got):
    return call(
        spectra_kernel,
        (shape((1024, 256), F32), shape((1024, 256), F32)),
        whole(3),
        [pltpu.VMEM((512, 128), F32)],
        4 * 10**8,
        (got, jnp.asarray(MATRICES, BF16), jnp.asarray(TWIDDLES, F32)),
    )


def convolve(z, signal, taps, before):
    return call(
        conv_kernel,
        shape((32, 16, 128), BF16),
        [SCALARS] + whole(5),
        [pltpu.VMEM((512, 128), F32)],
        6 * 10**8,
        (z, signal, taps, before, jnp.asarray(MATRICES, BF16), jnp.asarray(TWIDDLES, F32)),
        mib=16,
    )


def per_device(tokens_in, pre_gain, w_in, w_out, long_filter, w_unembed, target_ids, score_mask):
    ctx, tp = lax.axis_index("ctx"), lax.axis_index("tp")
    core, z = ctx % 2, ctx // 32
    z_at = z.reshape(1).astype(jnp.int32)

    core_at = core.reshape(1).astype(jnp.int32)
    w_in = w_in.transpose(1, 0, 2)
    first = call(
        first_kernel,
        shape((512, 128), BF16),
        [SCALARS] + whole(3),
        [],
        10**5,
        (core_at, w_in, lax.ppermute(w_in, "ctx", PERM_CORE), w_out),
    )
    near = call(copies_kernel, shape((4, 384, 128), BF16), whole(1), [], 10**10, (first,))
    near, tokens = lax.optimization_barrier((near, tokens_in))
    beside = lax.ppermute(tokens, "ctx", PERM_CORE)
    near = lax.all_to_all(near, "ctx", 0, 0, axis_index_groups=GROUPS_X, tiled=True)
    far = lax.ppermute(first, "ctx", PERM_Z)

    rows = by_position(first[384:].reshape(4, 32, 128), far[384:].reshape(4, 32, 128), z)
    far = far[:384]
    far = jnp.stack([far] + [lax.ppermute(far, "ctx", PERM_Y[k]) for k in (1, 2, 3)])
    near, far, rows, taps = lax.optimization_barrier((near, far, rows, long_filter))

    near = jnp.broadcast_to(near.reshape(1, 1536, 128), (4, 1536, 128))
    near = jnp.concatenate([near, rows[0], rows[1]], axis=1)
    near = lax.all_to_all(near, "ctx", 0, 0, axis_index_groups=GROUPS_Y, tiled=True)
    fars = [far] + [lax.ppermute(far, "ctx", PERM_X[k]) for k in (1, 2, 3)]
    taps_got = lax.ppermute(taps, "ctx", PERM_CORE)

    at = jnp.stack([(ctx // 8) % 4, (ctx // 2) % 4, core, z]).astype(jnp.int32)
    gained, scale, sums = call(
        near_kernel,
        (shape((2, 256, 4096), BF16), shape((2, 256, 128), F32), shape((2, 256, 384), F32)),
        [SCALARS] + [pl.BlockSpec(memory_space=pl.ANY)] * 2 + whole(2),
        [pltpu.VMEM((2, 256, 4096), BF16), pltpu.SemaphoreType.DMA((2, 4))],
        8 * 10**8,
        (at, tokens_in, beside, pre_gain.reshape(1, 4096), near),
    )
    signal, gate = call(
        proj_kernel,
        (shape((16, 64, 128), BF16), shape((2, 2, 128, 128), BF16)),
        [SCALARS] + whole(9),
        [],
        8 * 10**8,
        (at, gained, scale, sums, taps, taps_got, *fars),
    )
    got = lax.all_to_all(signal, "ctx", 0, 0, axis_index_groups=GROUPS_CORE, tiled=True)
    before = lax.ppermute(got, "ctx", PERM_Z_UP)
    terms = call(product_kernel, shape((8, 32, 128), BF16), whole(2), [], 4 * 10**7, (near, w_unembed))
    terms, _ = lax.optimization_barrier((terms, got))
    terms = lax.all_to_all(terms, "tp", 0, 0, tiled=True)
    gate_keep = lax.dynamic_index_in_dim(gate, core, 0, False)
    gate_got = lax.ppermute(lax.dynamic_index_in_dim(gate, 1 - core, 0, False), "ctx", PERM_CORE)

    conv = convolve(z_at, *spectra(got), before)
    conv = call(pack_kernel, shape((32, 48, 128), BF16), whole(2), [], 10**5, (conv, terms))
    conv = lax.all_to_all(conv, "ctx", 0, 0, axis_index_groups=GROUPS_PLANE, tiled=True)

    width = w_unembed.shape[0]
    base = mm(lax.dynamic_slice_in_dim(tokens_in, tp * width, width, 1), w_unembed)
    logits = call(
        mix_kernel,
        shape((256, 512), BF16),
        [SCALARS] + whole(4),
        [],
        10**8,
        (core_at, conv, gate_keep, gate_got, base),
    )
    logits = lax.all_to_all(logits.reshape(4, 64, 512), "tp", 0, 0, axis_index_groups=GROUPS_TP, tiled=True)
    logits = jnp.sum(logits.astype(F32), axis=0).astype(BF16)
    far = lax.ppermute(logits, "tp", [(i, i ^ 4) for i in range(8)])
    logits = logits.astype(F32) + far.astype(F32)

    row_top = jnp.max(logits, axis=1, keepdims=True)
    log_total = row_top[:, 0] + jnp.log(jnp.sum(jnp.exp(logits - row_top), axis=1))
    ids = lax.dynamic_slice_in_dim(target_ids, (tp % 4) * 64, 64, 0)
    mask = lax.dynamic_slice_in_dim(score_mask, (tp % 4) * 64, 64, 0)
    vocab_index = lax.broadcasted_iota(jnp.int32, (64, 512), 1)
    picked = jnp.sum(jnp.where(vocab_index == ids[:, None], logits, 0.0), axis=1)
    scores = (picked - log_total) * mask.astype(F32)
    scores = jnp.broadcast_to(scores[None, :], (4, 64))
    scores = lax.all_to_all(scores, "tp", 0, 0, axis_index_groups=GROUPS_TP, tiled=True)
    return scores.reshape(256)


def solution(mesh):
    return jax.shard_map(
        per_device,
        mesh=mesh,
        in_specs=(
            P("ctx", None),
            P(),
            P("ctx", None, "tp"),
            P("ctx", "tp"),
            P("ctx", "tp"),
            P("tp", None),
            P("ctx"),
            P("ctx"),
        ),
        out_specs=P("ctx"),
        check_vma=False,
    )
```

```python
import math

import jax
import jax.numpy as jnp
import numpy as np
from jax import lax
from jax.experimental import pallas as pl
from jax.experimental.pallas import tpu as pltpu
from jax.sharding import PartitionSpec as P

NORM_EPS = 1e-05
F32 = jnp.float32
BF16 = jnp.bfloat16

COORDS = [(z, y, x, c) for z in range(2) for y in range(4) for x in range(4) for c in range(2)]


def ctx_id(z, y, x, c):
    return ((z * 4 + y) * 4 + x) * 2 + c


def ctx_perm(move):
    return [(ctx_id(*at), ctx_id(*move(*at))) for at in COORDS]


PERM_CORE = ctx_perm(lambda z, y, x, c: (z, y, x, 1 - c))
PERM_Z = ctx_perm(lambda z, y, x, c: (1 - z, y, x, c))
PERM_Z_UP = [(i, i + 32) for i in range(32)]
PERM_X = [ctx_perm(lambda z, y, x, c, k=k: (z, y, (x + k) % 4, c)) for k in range(4)]
PERM_Y = [ctx_perm(lambda z, y, x, c, k=k: (z, (y + k) % 4, x, c)) for k in range(4)]
GROUPS_X = [[ctx_id(z, y, x, c) for x in range(4)] for z in range(2) for y in range(4) for c in range(2)]
GROUPS_Y = [[ctx_id(z, y, x, c) for y in range(4)] for z in range(2) for x in range(4) for c in range(2)]
GROUPS_PLANE = [
    [ctx_id(z, y, x, c) for y in range(4) for x in range(4) for c in range(2)] for z in range(2)
]
GROUPS_CORE = [
    [ctx_id(z, y, x, c) for y in range(4) for x in range(4)] for z in range(2) for c in range(2)
]
GROUPS_TP = [[0, 1, 2, 3], [4, 5, 6, 7]]


def tables():
    index = np.arange(128)
    inner = 2.0 * math.pi * (np.outer(index, index) % 128) / 128
    outer = 2.0 * math.pi * np.outer(index, index) / 16384
    cos, sin = np.cos(inner), np.sin(inner)
    first = np.concatenate([cos[:, :64], -sin[:, :64]], axis=0)
    second = np.block([[cos, -sin], [sin, cos]])
    back = np.block([[cos, sin], [-sin, cos]])
    last = np.concatenate([cos[:64], -sin[:64]], axis=1) / 16384.0
    return (first, second, back, last, np.cos(outer), np.sin(outer))


FIRST, SECOND, BACK, LAST, COS_TW, SIN_TW = tables()
MATRICES = np.concatenate([np.pad(FIRST, ((0, 0), (0, 192))), SECOND, BACK, LAST])
TWIDDLES = np.concatenate([COS_TW, SIN_TW], axis=1)


def mm(left, right):
    return jnp.dot(left, right, preferred_element_type=F32)


def whole(count):
    return [pl.BlockSpec(memory_space=pltpu.VMEM)] * count


SCALARS = pl.BlockSpec(memory_space=pltpu.SMEM)


def spectrum(scratch, matrices, twiddles):
    cos_tw, sin_tw = twiddles[:, :128], twiddles[:, 128:]
    cube = jnp.concatenate([scratch[pl.ds(c, 64, stride=8), :] for c in range(8)], axis=1)
    step = mm(matrices[:256, :64], cube.astype(BF16))
    parts = []
    for c in range(8):
        real, imag = step[:128, c * 128 : c * 128 + 128], step[128:, c * 128 : c * 128 + 128]
        parts.append(
            jnp.concatenate(
                [(real * cos_tw + imag * sin_tw).astype(BF16), (imag * cos_tw - real * sin_tw).astype(BF16)],
                axis=1,
            )
        )
    return mm(jnp.concatenate(parts, axis=0), matrices[256:512, :])


def rows_of(scratch, ref, at):
    for p in range(16):
        scratch[p * 32 : p * 32 + 32] = ref[p, at : at + 32].astype(F32)


def spectra_kernel(got_ref, matrices, twiddles, signal_ref, filter_ref, scratch):
    rows_of(scratch, got_ref, 0)
    signal_ref[...] = spectrum(scratch, matrices, twiddles)
    rows_of(scratch, got_ref, 32)
    filter_ref[...] = spectrum(scratch, matrices, twiddles)


def conv_kernel(z_ref, signal_ref, filter_ref, before_ref, matrices, twiddles, out_ref, scratch):
    upper = z_ref[0] == 1
    cos_tw, sin_tw = twiddles[:, :128], twiddles[:, 128:]
    own, high = signal_ref[...], filter_ref[...]
    rows_of(scratch, before_ref, 0)
    old = jnp.where(upper, spectrum(scratch, matrices, twiddles), 0.0)
    rows_of(scratch, before_ref, 32)
    low = jnp.where(upper, spectrum(scratch, matrices, twiddles), high)
    odd = lax.broadcasted_iota(jnp.int32, (1024, 256), 0) & 1
    every = jnp.where(odd == 1, -low, low) + high
    own_r, own_i, old_r, old_i = own[:, :128], own[:, 128:], old[:, :128], old[:, 128:]
    low_r, low_i, all_r, all_i = low[:, :128], low[:, 128:], every[:, :128], every[:, 128:]
    real = own_r * low_r - own_i * low_i + old_r * all_r - old_i * all_i
    imag = own_r * low_i + own_i * low_r + old_r * all_i + old_i * all_r
    half = mm(jnp.concatenate([real.astype(BF16), imag.astype(BF16)], axis=1), matrices[512:768, :])
    parts = []
    for c in range(8):
        real, imag = half[c * 128 : c * 128 + 128, :128], half[c * 128 : c * 128 + 128, 128:]
        parts.append(
            jnp.concatenate(
                [(real * cos_tw - imag * sin_tw).astype(BF16), (imag * cos_tw + real * sin_tw).astype(BF16)],
                axis=0,
            )
        )
    result = mm(matrices[768:, :], jnp.concatenate(parts, axis=1))
    for c in range(8):
        scratch[pl.ds(c, 64, stride=8), :] = result[:, c * 128 : c * 128 + 128]
    for d in range(32):
        out_ref[d] = scratch[d * 16 : d * 16 + 16].astype(BF16)


def pack_kernel(conv_ref, terms_ref, out_ref):
    piece = sum(terms_ref[j].astype(F32) for j in range(8)).astype(BF16)
    for d in range(32):
        out_ref[d, :16] = conv_ref[d]
        out_ref[d, 16:] = piece


def copy_kernel(first_ref, out_ref):
    out_ref[...] = first_ref[:384]


def weight_block(ref, lead, row):
    return jnp.concatenate([ref[lead, row + 128 * g : row + 128 * g + 128, :] for g in range(3)], axis=1)


def near_kernel(
    at_ref, own_hbm, beside_hbm, gain_ref, n0, n1, n2, n3, gained_ref, scale_ref, out_ref, tokens, blocks, sems
):
    y_at, x_at, start = at_ref[0], at_ref[1], at_ref[3] * 2048
    gain = gain_ref[...]
    copies = []
    for part, ref in enumerate((own_hbm, beside_hbm)):
        for i in range(4):
            rows = slice(i * 64, i * 64 + 64)
            copies.append(pltpu.make_async_copy(ref.at[rows], tokens.at[part, rows], sems.at[part, i]))
    for step, ref in enumerate((n0, n1, n2, n3)):
        copies.append(pltpu.make_async_copy(ref, blocks.at[step], sems.at[2, step]))
    for copy in copies:
        copy.start()
    for part in range(2):
        for i in range(4):
            copies[part * 4 + i].wait()
            for half in range(2):
                rows = slice(i * 64 + half * 32, i * 64 + half * 32 + 32)
                block = tokens[part, rows, :]
                stream = block.astype(F32)
                mean = jnp.mean(stream * stream, axis=1, keepdims=True)
                scale_ref[part, rows, :] = jnp.broadcast_to(lax.rsqrt(mean + NORM_EPS), (32, 128))
                gained_ref[part, rows, :] = block * gain
    for step in range(4):
        copies[8 + step].wait()
    for part in range(2):
        total = jnp.zeros((256, 384), F32)
        for step in range(4):
            y = lax.rem(y_at + 4 - step, 4)
            for k in (0, 2):
                starts = [start + (y * 4 + lax.rem(x_at + 4 - j, 4)) * 128 for j in (k, k + 1)]
                left = [gained_ref[part, :, pl.ds(pl.multiple_of(at, 128), 128)] for at in starts]
                right = [weight_block(blocks.at[step], k, 0), weight_block(blocks.at[step], k + 1, 0)]
                total += mm(jnp.concatenate(left, axis=1), jnp.concatenate(right, axis=0))
        out_ref[part] = total


def product_kernel(rows_ref, unembed_ref, out_ref):
    blocks = []
    for z in range(2):
        for y in range(4):
            block = rows_ref[y, 384 + z * 32 : 416 + z * 32, :].astype(F32)
            blocks.append(jnp.concatenate([block[v * 8 : v * 8 + 8] for v in range(4)], axis=1))
    terms = mm(jnp.concatenate(blocks, axis=0).astype(BF16), unembed_ref[...])
    for j in range(8):
        parts = [terms[j * 8 : j * 8 + 8, v * 128 : v * 128 + 128] for v in range(4)]
        out_ref[j] = jnp.concatenate(parts, axis=0).astype(BF16)


def put_pieces(ref, row, place, block):
    first, second = block[:128].T, block[128:].T
    for p in range(16):
        b = p * 8
        rows = jnp.concatenate([first[b : b + 8], second[b : b + 8]], axis=0).astype(BF16)
        ref[p, pl.ds(pl.multiple_of(row + place * 16, 16), 16), :] = rows


def proj_kernel(
    at_ref, gained_ref, scale_ref, near_ref, own_hbm, got_hbm, far_hbm, sig_ref, gate_ref, taps, far, sems
):
    core = at_ref[2]
    start = 2048 - at_ref[3] * 2048
    half = pl.ds(pl.multiple_of(core * 128, 128), 128)
    copies = [pltpu.make_async_copy(far_hbm.at[x], far.at[x], sems.at[x]) for x in range(4)]
    copies.append(pltpu.make_async_copy(own_hbm, taps.at[0], sems.at[4]))
    copies.append(pltpu.make_async_copy(got_hbm, taps.at[1], sems.at[5]))
    for copy in copies:
        copy.start()
    for part in range(2):
        total = near_ref[part]
        for x in range(4):
            if part == 0:
                copies[x].wait()
            for y in (0, 2):
                starts = [start + (k * 4 + x) * 128 for k in (y, y + 1)]
                left = [gained_ref[part, :, pl.ds(pl.multiple_of(at, 128), 128)] for at in starts]
                right = [weight_block(far, x, y * 384), weight_block(far, x, y * 384 + 384)]
                total += mm(jnp.concatenate(left, axis=1), jnp.concatenate(right, axis=0))
        scale = scale_ref[part]
        proj = (total * jnp.concatenate([scale, scale, scale], axis=1)).astype(BF16).astype(F32)
        place = core if part == 0 else 1 - core
        put_pieces(sig_ref, 0, place, proj[:, 128:256] * proj[:, 256:])
        copies[4 + part].wait()
        put_pieces(sig_ref, 32, place, taps[part, :, half].astype(F32))
        gate_ref[place, 0] = proj[:128, :128].T.astype(BF16)
        gate_ref[place, 1] = proj[128:, :128].T.astype(BF16)


def mix_kernel(core_ref, got_ref, keep_ref, other_ref, base_ref, out_ref):
    core = core_ref[0]
    keep, other = keep_ref[...].astype(F32), other_ref[...].astype(F32)
    conv = got_ref[:, :16, :].astype(F32)
    for rb in range(2):
        total = base_ref[rb * 128 : rb * 128 + 128, :]
        for c in range(2):
            cube = jnp.concatenate([conv[b * 2 + c, rb * 8 : rb * 8 + 8] for b in range(16)], axis=0)
            gate = jnp.where(core == c, keep[rb], other[rb])
            mixed = (gate * cube).T.astype(BF16)
            weights = []
            for b in range(16):
                x, holder, y = (c * 16 + b) // 8, b % 8 // 4, b % 4
                piece = got_ref[(y * 4 + x) * 2 + holder, 16:, :].astype(F32)
                weights.append(jnp.concatenate([piece[v * 8 : v * 8 + 8] for v in range(4)], axis=1))
            total += mm(mixed, jnp.concatenate(weights, axis=0).astype(BF16))
        out_ref[rb * 128 : rb * 128 + 128, :] = total.astype(BF16)


def call(kernel, outs, specs, scratch, flops, args, mib=8):
    return pl.pallas_call(
        kernel,
        out_shape=outs,
        in_specs=specs,
        out_specs=jax.tree.map(lambda _: pl.BlockSpec(memory_space=pltpu.VMEM), outs),
        scratch_shapes=scratch,
        compiler_params=pltpu.CompilerParams(vmem_limit_bytes=mib * 2**20),
        cost_estimate=pl.CostEstimate(flops=flops, bytes_accessed=4 * 2**20, transcendentals=0),
    )(*args)


def shape(dims, dtype):
    return jax.ShapeDtypeStruct(dims, dtype)


def by_position(own, other, place):
    return jnp.where(place == 0, jnp.stack([own, other]), jnp.stack([other, own]))


def spectra(got):
    return call(
        spectra_kernel,
        (shape((1024, 256), F32), shape((1024, 256), F32)),
        whole(3),
        [pltpu.VMEM((512, 128), F32)],
        4 * 10**8,
        (got, jnp.asarray(MATRICES, BF16), jnp.asarray(TWIDDLES, F32)),
    )


def convolve(z, signal, taps, before):
    return call(
        conv_kernel,
        shape((32, 16, 128), BF16),
        [SCALARS] + whole(5),
        [pltpu.VMEM((512, 128), F32)],
        6 * 10**8,
        (z, signal, taps, before, jnp.asarray(MATRICES, BF16), jnp.asarray(TWIDDLES, F32)),
        mib=16,
    )


def per_device(tokens_in, pre_gain, w_in, w_out, long_filter, w_unembed, target_ids, score_mask):
    ctx, tp = lax.axis_index("ctx"), lax.axis_index("tp")
    core, z = ctx % 2, ctx // 32
    z_at = z.reshape(1).astype(jnp.int32)

    core_at = core.reshape(1).astype(jnp.int32)
    w_in = w_in.transpose(1, 0, 2)
    keep = lax.dynamic_slice_in_dim(w_in, core * 128, 128, 2)
    got = lax.dynamic_slice_in_dim(lax.ppermute(w_in, "ctx", PERM_CORE), core * 128, 128, 2)
    near = jnp.concatenate([jnp.where(core == 0, keep, got), jnp.where(core == 0, got, keep)], axis=1)
    rows = w_out.reshape(4, 8, 4, 128).transpose(0, 2, 1, 3).reshape(128, 128)
    first = jnp.concatenate([near.reshape(384, 128), rows])
    near = call(copy_kernel, shape((384, 128), BF16), whole(1), [], 10**10, (first,))
    near, tokens = lax.optimization_barrier((near, tokens_in))
    beside = lax.ppermute(tokens, "ctx", PERM_CORE)
    near = jnp.stack([near] + [lax.ppermute(near, "ctx", PERM_X[k]) for k in (1, 2, 3)])
    far = lax.ppermute(first, "ctx", PERM_Z)

    rows = by_position(first[384:].reshape(4, 32, 128), far[384:].reshape(4, 32, 128), z)
    far = jnp.concatenate([jnp.broadcast_to(far[:384], (4, 384, 128)), rows[0], rows[1]], axis=1)
    rows = lax.all_to_all(far, "ctx", 0, 0, axis_index_groups=GROUPS_Y, tiled=True)
    near, rows, taps = lax.optimization_barrier((near, rows, long_filter))

    far = jnp.broadcast_to(rows[:, :384].reshape(1, 1536, 128), (4, 1536, 128))
    far = lax.all_to_all(far, "ctx", 0, 0, axis_index_groups=GROUPS_X, tiled=True)
    nears = [near] + [lax.ppermute(near, "ctx", PERM_Y[k]) for k in (1, 2, 3)]
    taps_got = lax.ppermute(taps, "ctx", PERM_CORE)

    at = jnp.stack([(ctx // 8) % 4, (ctx // 2) % 4, core, z]).astype(jnp.int32)
    anywhere = pl.BlockSpec(memory_space=pl.ANY)
    gained, scale, sums = call(
        near_kernel,
        (shape((2, 256, 4096), BF16), shape((2, 256, 128), F32), shape((2, 256, 384), F32)),
        [SCALARS, anywhere, anywhere] + whole(1) + [anywhere] * 4,
        [
            pltpu.VMEM((2, 256, 4096), BF16),
            pltpu.VMEM((4, 4, 384, 128), BF16),
            pltpu.SemaphoreType.DMA((3, 4)),
        ],
        8 * 10**8,
        (at, tokens_in, beside, pre_gain.reshape(1, 4096), *nears),
        mib=12,
    )
    signal, gate = call(
        proj_kernel,
        (shape((16, 64, 128), BF16), shape((2, 2, 128, 128), BF16)),
        [SCALARS] + whole(3) + [anywhere] * 3,
        [pltpu.VMEM((2, 256, 256), BF16), pltpu.VMEM((4, 1536, 128), BF16), pltpu.SemaphoreType.DMA((6,))],
        8 * 10**8,
        (at, gained, scale, sums, taps, taps_got, far),
    )
    got = lax.all_to_all(signal, "ctx", 0, 0, axis_index_groups=GROUPS_CORE, tiled=True)
    before = lax.ppermute(got, "ctx", PERM_Z_UP)
    terms = call(product_kernel, shape((8, 32, 128), BF16), whole(2), [], 4 * 10**7, (rows, w_unembed))
    terms, _ = lax.optimization_barrier((terms, got))
    terms = lax.all_to_all(terms, "tp", 0, 0, tiled=True)
    gate_keep = lax.dynamic_index_in_dim(gate, core, 0, False)
    gate_got = lax.ppermute(lax.dynamic_index_in_dim(gate, 1 - core, 0, False), "ctx", PERM_CORE)

    conv = convolve(z_at, *spectra(got), before)
    conv = call(pack_kernel, shape((32, 48, 128), BF16), whole(2), [], 10**5, (conv, terms))
    conv = lax.all_to_all(conv, "ctx", 0, 0, axis_index_groups=GROUPS_PLANE, tiled=True)

    width = w_unembed.shape[0]
    base = mm(lax.dynamic_slice_in_dim(tokens_in, tp * width, width, 1), w_unembed)
    logits = call(
        mix_kernel,
        shape((256, 512), BF16),
        [SCALARS] + whole(4),
        [],
        10**8,
        (core_at, conv, gate_keep, gate_got, base),
    )
    logits = lax.all_to_all(logits.reshape(4, 64, 512), "tp", 0, 0, axis_index_groups=GROUPS_TP, tiled=True)
    logits = jnp.sum(logits.astype(F32), axis=0).astype(BF16)
    far = lax.ppermute(logits, "tp", [(i, i ^ 4) for i in range(8)])
    logits = logits.astype(F32) + far.astype(F32)

    row_top = jnp.max(logits, axis=1, keepdims=True)
    log_total = row_top[:, 0] + jnp.log(jnp.sum(jnp.exp(logits - row_top), axis=1))
    ids = lax.dynamic_slice_in_dim(target_ids, (tp % 4) * 64, 64, 0)
    mask = lax.dynamic_slice_in_dim(score_mask, (tp % 4) * 64, 64, 0)
    vocab_index = lax.broadcasted_iota(jnp.int32, (64, 512), 1)
    picked = jnp.sum(jnp.where(vocab_index == ids[:, None], logits, 0.0), axis=1)
    scores = (picked - log_total) * mask.astype(F32)
    scores = jnp.broadcast_to(scores[None, :], (4, 64))
    scores = lax.all_to_all(scores, "tp", 0, 0, axis_index_groups=GROUPS_TP, tiled=True)
    return scores.reshape(256)


def solution(mesh):
    return jax.shard_map(
        per_device,
        mesh=mesh,
        in_specs=(
            P("ctx", None),
            P(),
            P("ctx", None, "tp"),
            P("ctx", "tp"),
            P("ctx", "tp"),
            P("tp", None),
            P("ctx"),
            P("ctx"),
        ),
        out_specs=P("ctx"),
        check_vma=False,
    )
```

```python
import math

import jax
import jax.numpy as jnp
import numpy as np
from jax import lax
from jax.experimental import pallas as pl
from jax.experimental.pallas import tpu as pltpu
from jax.sharding import PartitionSpec as P

NORM_EPS = 1e-05
F32 = jnp.float32
BF16 = jnp.bfloat16

COORDS = [(z, y, x, c) for z in range(2) for y in range(4) for x in range(4) for c in range(2)]


def ctx_id(z, y, x, c):
    return ((z * 4 + y) * 4 + x) * 2 + c


def ctx_perm(move):
    return [(ctx_id(*at), ctx_id(*move(*at))) for at in COORDS]


PERM_CORE = ctx_perm(lambda z, y, x, c: (z, y, x, 1 - c))
PERM_Z = ctx_perm(lambda z, y, x, c: (1 - z, y, x, c))
PERM_Z_UP = [(i, i + 32) for i in range(32)]
PERM_X = [ctx_perm(lambda z, y, x, c, k=k: (z, y, (x + k) % 4, c)) for k in range(4)]
PERM_Y = [ctx_perm(lambda z, y, x, c, k=k: (z, (y + k) % 4, x, c)) for k in range(4)]
GROUPS_X = [[ctx_id(z, y, x, c) for x in range(4)] for z in range(2) for y in range(4) for c in range(2)]
GROUPS_Y = [[ctx_id(z, y, x, c) for y in range(4)] for z in range(2) for x in range(4) for c in range(2)]
GROUPS_PLANE = [
    [ctx_id(z, y, x, c) for y in range(4) for x in range(4) for c in range(2)] for z in range(2)
]
GROUPS_CORE = [
    [ctx_id(z, y, x, c) for y in range(4) for x in range(4)] for z in range(2) for c in range(2)
]
GROUPS_TP = [[0, 1, 2, 3], [4, 5, 6, 7]]


def tables():
    index = np.arange(128)
    inner = 2.0 * math.pi * (np.outer(index, index) % 128) / 128
    outer = 2.0 * math.pi * np.outer(index, index) / 16384
    cos, sin = np.cos(inner), np.sin(inner)
    first = np.concatenate([cos[:, :64], -sin[:, :64]], axis=0)
    second = np.block([[cos, -sin], [sin, cos]])
    back = np.block([[cos, sin], [-sin, cos]])
    last = np.concatenate([cos[:64], -sin[:64]], axis=1) / 16384.0
    return (first, second, back, last, np.cos(outer), np.sin(outer))


FIRST, SECOND, BACK, LAST, COS_TW, SIN_TW = tables()
MATRICES = np.concatenate([np.pad(FIRST, ((0, 0), (0, 192))), SECOND, BACK, LAST])
TWIDDLES = np.concatenate([COS_TW, SIN_TW], axis=1)


def mm(left, right):
    return jnp.dot(left, right, preferred_element_type=F32)


def whole(count):
    return [pl.BlockSpec(memory_space=pltpu.VMEM)] * count


SCALARS = pl.BlockSpec(memory_space=pltpu.SMEM)
ANYWHERE = pl.BlockSpec(memory_space=pl.ANY)


def spectrum(scratch, matrices, twiddles):
    cos_tw, sin_tw = twiddles[:, :128], twiddles[:, 128:]
    cube = jnp.concatenate([scratch[pl.ds(c, 64, stride=8), :] for c in range(8)], axis=1)
    step = mm(matrices[:256, :64], cube.astype(BF16))
    parts = []
    for c in range(8):
        real, imag = step[:128, c * 128 : c * 128 + 128], step[128:, c * 128 : c * 128 + 128]
        parts.append(
            jnp.concatenate(
                [(real * cos_tw + imag * sin_tw).astype(BF16), (imag * cos_tw - real * sin_tw).astype(BF16)],
                axis=1,
            )
        )
    return mm(jnp.concatenate(parts, axis=0), matrices[256:512, :])


def rows_of(scratch, ref, at):
    for p in range(16):
        scratch[p * 32 : p * 32 + 32] = ref[p, at : at + 32].astype(F32)


def spectra_kernel(got_ref, matrices, twiddles, signal_ref, filter_ref, scratch):
    rows_of(scratch, got_ref, 0)
    signal_ref[...] = spectrum(scratch, matrices, twiddles)
    rows_of(scratch, got_ref, 32)
    filter_ref[...] = spectrum(scratch, matrices, twiddles)


def conv_kernel(z_ref, signal_ref, filter_ref, before_ref, matrices, twiddles, out_ref, scratch):
    upper = z_ref[0] == 1
    cos_tw, sin_tw = twiddles[:, :128], twiddles[:, 128:]
    own, high = signal_ref[...], filter_ref[...]
    rows_of(scratch, before_ref, 0)
    old = jnp.where(upper, spectrum(scratch, matrices, twiddles), 0.0)
    rows_of(scratch, before_ref, 32)
    low = jnp.where(upper, spectrum(scratch, matrices, twiddles), high)
    odd = lax.broadcasted_iota(jnp.int32, (1024, 256), 0) & 1
    every = jnp.where(odd == 1, -low, low) + high
    own_r, own_i, old_r, old_i = own[:, :128], own[:, 128:], old[:, :128], old[:, 128:]
    low_r, low_i, all_r, all_i = low[:, :128], low[:, 128:], every[:, :128], every[:, 128:]
    real = own_r * low_r - own_i * low_i + old_r * all_r - old_i * all_i
    imag = own_r * low_i + own_i * low_r + old_r * all_i + old_i * all_r
    half = mm(jnp.concatenate([real.astype(BF16), imag.astype(BF16)], axis=1), matrices[512:768, :])
    parts = []
    for c in range(8):
        real, imag = half[c * 128 : c * 128 + 128, :128], half[c * 128 : c * 128 + 128, 128:]
        parts.append(
            jnp.concatenate(
                [(real * cos_tw - imag * sin_tw).astype(BF16), (imag * cos_tw + real * sin_tw).astype(BF16)],
                axis=0,
            )
        )
    result = mm(matrices[768:, :], jnp.concatenate(parts, axis=1))
    for c in range(8):
        scratch[pl.ds(c, 64, stride=8), :] = result[:, c * 128 : c * 128 + 128]
    for d in range(32):
        out_ref[d] = scratch[d * 16 : d * 16 + 16].astype(BF16)


def pack_kernel(conv_ref, terms_ref, out_ref):
    piece = sum(terms_ref[j].astype(F32) for j in range(8)).astype(BF16)
    for d in range(32):
        out_ref[d, :16] = conv_ref[d]
        out_ref[d, 16:] = piece


def first_kernel(core_ref, own_hbm, got_ref, rows_hbm, out_ref, own_ref, rows_ref, sems):
    copies = [
        pltpu.make_async_copy(own_hbm, own_ref, sems.at[0]),
        pltpu.make_async_copy(rows_hbm, rows_ref, sems.at[1]),
    ]
    for copy in copies:
        copy.start()
    for copy in copies:
        copy.wait()
    core = core_ref[0]
    half = pl.ds(pl.multiple_of(core * 128, 128), 128)
    for g in range(3):
        own, got = own_ref[g, :, half], got_ref[g, :, half]
        out_ref[g * 128 : g * 128 + 64] = jnp.where(core == 0, own, got)
        out_ref[g * 128 + 64 : g * 128 + 128] = jnp.where(core == 0, got, own)
    rows = rows_ref[...].astype(F32)
    blocks = [rows[y * 8 : y * 8 + 8, v * 128 : v * 128 + 128] for y in range(4) for v in range(4)]
    out_ref[384:] = jnp.concatenate(blocks, axis=0).astype(BF16)


def copies_kernel(first_ref, out_ref):
    for k in range(4):
        out_ref[k] = first_ref[:384]


def weight_block(ref, lead, row):
    return jnp.concatenate([ref[lead, row + 128 * g : row + 128 * g + 128, :] for g in range(3)], axis=1)


def norm_kernel(own_hbm, beside_hbm, gain_ref, gained_hbm, scale_ref, tokens, gained, sems):
    gain = gain_ref[...]
    copies, stores = [], []
    for part, ref in enumerate((own_hbm, beside_hbm)):
        for i in range(4):
            rows = pl.ds(i * 64, 64)
            copies.append(pltpu.make_async_copy(ref.at[rows], tokens.at[part, rows], sems.at[0, part, i]))
            stores.append(
                pltpu.make_async_copy(gained.at[part, rows], gained_hbm.at[part, rows], sems.at[1, part, i])
            )
    for copy in copies:
        copy.start()
    for k in range(8):
        copies[k].wait()
        part, i = k // 4, k % 4
        for half in range(2):
            rows = slice(i * 64 + half * 32, i * 64 + half * 32 + 32)
            block = tokens[part, rows, :]
            stream = block.astype(F32)
            mean = jnp.mean(stream * stream, axis=1, keepdims=True)
            scale_ref[part, rows, :] = jnp.broadcast_to(lax.rsqrt(mean + NORM_EPS), (32, 128))
            gained[part, rows, :] = block * gain
        stores[k].start()
    for store in stores:
        store.wait()


def near_kernel(
    at_ref, gained_hbm, own_taps, got_taps, near_ref, unembed_ref, out_ref, terms_ref, pieces_ref, gained, taps, sems
):
    core, z = at_ref[2], at_ref[3]
    columns = pl.ds(pl.multiple_of(z * 2048, 2048), 2048)
    copies = [
        pltpu.make_async_copy(gained_hbm.at[part, :, columns], gained.at[part], sems.at[part]) for part in range(2)
    ]
    copies.append(pltpu.make_async_copy(own_taps, taps.at[0], sems.at[2]))
    copies.append(pltpu.make_async_copy(got_taps, taps.at[1], sems.at[3]))
    for copy in copies:
        copy.start()

    blocks = []
    for plane in range(2):
        for y in range(4):
            block = near_ref[y, 1536 + plane * 32 : 1568 + plane * 32, :].astype(F32)
            blocks.append(jnp.concatenate([block[v * 8 : v * 8 + 8] for v in range(4)], axis=1))
    terms = mm(jnp.concatenate(blocks, axis=0).astype(BF16), unembed_ref[...])
    for j in range(8):
        parts = [terms[j * 8 : j * 8 + 8, v * 128 : v * 128 + 128] for v in range(4)]
        terms_ref[j] = jnp.concatenate(parts, axis=0).astype(BF16)

    for part in range(2):
        copies[part].wait()
        total = jnp.zeros((256, 384), F32)
        for y in range(4):
            for x in (0, 2):
                left = gained[part, :, (y * 4 + x) * 128 : (y * 4 + x) * 128 + 256]
                right = [weight_block(near_ref, y, x * 384), weight_block(near_ref, y, x * 384 + 384)]
                total += mm(left, jnp.concatenate(right, axis=0))
        out_ref[part] = total
    half = pl.ds(pl.multiple_of(core * 128, 128), 128)
    for part in range(2):
        copies[2 + part].wait()
        put_pieces(pieces_ref, 0, core if part == 0 else 1 - core, taps[part, :, half].astype(F32))


def put_pieces(ref, row, place, block):
    first, second = block[:128].T, block[128:].T
    for p in range(16):
        b = p * 8
        rows = jnp.concatenate([first[b : b + 8], second[b : b + 8]], axis=0).astype(BF16)
        ref[p, pl.ds(pl.multiple_of(row + place * 16, 16), 16), :] = rows


def proj_kernel(
    at_ref, gained_hbm, scale_ref, near_ref, pieces_ref, f0, f1, f2, f3, sig_ref, gate_ref, gained, fars, sems
):
    y_at, x_at, core = at_ref[0], at_ref[1], at_ref[2]
    columns = pl.ds(pl.multiple_of(2048 - at_ref[3] * 2048, 2048), 2048)
    copies = [
        pltpu.make_async_copy(gained_hbm.at[part, :, columns], gained.at[part], sems.at[part]) for part in range(2)
    ]
    copies += [pltpu.make_async_copy(f, fars.at[k], sems.at[2 + k]) for k, f in enumerate((f0, f1, f2, f3))]
    for k in (0, 2, 3, 4, 5, 1):
        copies[k].start()
    for part in range(2):
        copies[part].wait()
        total = near_ref[part]
        for step in range(4):
            if part == 0:
                copies[2 + step].wait()
            x = lax.rem(x_at + 4 - step, 4)
            for k in (0, 2):
                starts = [(lax.rem(y_at + 4 - j, 4) * 4 + x) * 128 for j in (k, k + 1)]
                left = [gained[part, :, pl.ds(pl.multiple_of(at, 128), 128)] for at in starts]
                right = [weight_block(fars.at[step], k, 0), weight_block(fars.at[step], k + 1, 0)]
                total += mm(jnp.concatenate(left, axis=1), jnp.concatenate(right, axis=0))
        scale = scale_ref[part]
        proj = (total * jnp.concatenate([scale, scale, scale], axis=1)).astype(BF16).astype(F32)
        place = core if part == 0 else 1 - core
        put_pieces(sig_ref, 0, place, proj[:, 128:256] * proj[:, 256:])
        gate_ref[place, 0] = proj[:128, :128].T.astype(BF16)
        gate_ref[place, 1] = proj[128:, :128].T.astype(BF16)
    for p in range(16):
        sig_ref[p, 32:, :] = pieces_ref[p]


def mix_kernel(core_ref, got_ref, keep_ref, other_ref, base_ref, out_ref):
    core = core_ref[0]
    keep, other = keep_ref[...].astype(F32), other_ref[...].astype(F32)
    conv = got_ref[:, :16, :].astype(F32)
    for rb in range(2):
        total = base_ref[rb * 128 : rb * 128 + 128, :]
        for c in range(2):
            cube = jnp.concatenate([conv[b * 2 + c, rb * 8 : rb * 8 + 8] for b in range(16)], axis=0)
            gate = jnp.where(core == c, keep[rb], other[rb])
            mixed = (gate * cube).T.astype(BF16)
            weights = []
            for b in range(16):
                x, holder, y = (c * 16 + b) // 8, b % 8 // 4, b % 4
                piece = got_ref[(y * 4 + x) * 2 + holder, 16:, :].astype(F32)
                weights.append(jnp.concatenate([piece[v * 8 : v * 8 + 8] for v in range(4)], axis=1))
            total += mm(mixed, jnp.concatenate(weights, axis=0).astype(BF16))
        out_ref[rb * 128 : rb * 128 + 128, :] = total.astype(BF16)


def call(kernel, outs, specs, scratch, flops, args, mib=8, out_specs=None):
    if out_specs is None:
        out_specs = jax.tree.map(lambda _: pl.BlockSpec(memory_space=pltpu.VMEM), outs)
    return pl.pallas_call(
        kernel,
        out_shape=outs,
        in_specs=specs,
        out_specs=out_specs,
        scratch_shapes=scratch,
        compiler_params=pltpu.CompilerParams(vmem_limit_bytes=mib * 2**20),
        cost_estimate=pl.CostEstimate(flops=flops, bytes_accessed=4 * 2**20, transcendentals=0),
    )(*args)


def shape(dims, dtype):
    return jax.ShapeDtypeStruct(dims, dtype)


def by_position(own, other, place):
    return jnp.where(place == 0, jnp.stack([own, other]), jnp.stack([other, own]))


def spectra(got):
    return call(
        spectra_kernel,
        (shape((1024, 256), F32), shape((1024, 256), F32)),
        whole(3),
        [pltpu.VMEM((512, 128), F32)],
        4 * 10**8,
        (got, jnp.asarray(MATRICES, BF16), jnp.asarray(TWIDDLES, F32)),
    )


def convolve(z, signal, taps, before):
    return call(
        conv_kernel,
        shape((32, 16, 128), BF16),
        [SCALARS] + whole(5),
        [pltpu.VMEM((512, 128), F32)],
        6 * 10**8,
        (z, signal, taps, before, jnp.asarray(MATRICES, BF16), jnp.asarray(TWIDDLES, F32)),
        mib=16,
    )


def per_device(tokens_in, pre_gain, w_in, w_out, long_filter, w_unembed, target_ids, score_mask):
    ctx, tp = lax.axis_index("ctx"), lax.axis_index("tp")
    core, z = ctx % 2, ctx // 32
    z_at = z.reshape(1).astype(jnp.int32)

    core_at = core.reshape(1).astype(jnp.int32)
    w_in = w_in.transpose(1, 0, 2)
    first = call(
        first_kernel,
        shape((512, 128), BF16),
        [SCALARS, ANYWHERE] + whole(1) + [ANYWHERE],
        [pltpu.VMEM((3, 64, 256), BF16), pltpu.VMEM((32, 512), BF16), pltpu.SemaphoreType.DMA((2,))],
        10**5,
        (core_at, w_in, lax.ppermute(w_in, "ctx", PERM_CORE), w_out),
    )
    near = call(copies_kernel, shape((4, 384, 128), BF16), whole(1), [], 10**10, (first,))
    near, tokens = lax.optimization_barrier((near, tokens_in))
    beside = lax.ppermute(tokens, "ctx", PERM_CORE)
    near = lax.all_to_all(near, "ctx", 0, 0, axis_index_groups=GROUPS_X, tiled=True)
    far = lax.ppermute(first, "ctx", PERM_Z)

    rows = by_position(first[384:].reshape(4, 32, 128), far[384:].reshape(4, 32, 128), z)
    far = far[:384]
    far = jnp.stack([far] + [lax.ppermute(far, "ctx", PERM_Y[k]) for k in (1, 2, 3)])
    near, far, rows, taps = lax.optimization_barrier((near, far, rows, long_filter))

    near = jnp.broadcast_to(near.reshape(1, 1536, 128), (4, 1536, 128))
    near = jnp.concatenate([near, rows[0], rows[1]], axis=1)
    near = lax.all_to_all(near, "ctx", 0, 0, axis_index_groups=GROUPS_Y, tiled=True)
    fars = [far] + [lax.ppermute(far, "ctx", PERM_X[k]) for k in (1, 2, 3)]
    taps_got = lax.ppermute(taps, "ctx", PERM_CORE)

    at = jnp.stack([(ctx // 8) % 4, (ctx // 2) % 4, core, z]).astype(jnp.int32)
    gained, scale = call(
        norm_kernel,
        (shape((2, 256, 4096), BF16), shape((2, 256, 128), F32)),
        [ANYWHERE, ANYWHERE] + whole(1),
        [
            pltpu.VMEM((2, 256, 4096), BF16),
            pltpu.VMEM((2, 256, 4096), BF16),
            pltpu.SemaphoreType.DMA((2, 2, 4)),
        ],
        10**7,
        (tokens_in, beside, pre_gain.reshape(1, 4096)),
        mib=16,
        out_specs=(ANYWHERE, whole(1)[0]),
    )
    sums, terms, pieces = call(
        near_kernel,
        (shape((2, 256, 384), F32), shape((8, 32, 128), BF16), shape((16, 32, 128), BF16)),
        [SCALARS] + [ANYWHERE] * 3 + whole(2),
        [pltpu.VMEM((2, 256, 2048), BF16), pltpu.VMEM((2, 256, 256), BF16), pltpu.SemaphoreType.DMA((4,))],
        8 * 10**8,
        (at, gained, taps, taps_got, near, w_unembed),
    )
    signal, gate = call(
        proj_kernel,
        (shape((16, 64, 128), BF16), shape((2, 2, 128, 128), BF16)),
        [SCALARS, ANYWHERE] + whole(3) + [ANYWHERE] * 4,
        [pltpu.VMEM((2, 256, 2048), BF16), pltpu.VMEM((4, 4, 384, 128), BF16), pltpu.SemaphoreType.DMA((6,))],
        8 * 10**8,
        (at, gained, scale, sums, pieces, *fars),
    )
    got = lax.all_to_all(signal, "ctx", 0, 0, axis_index_groups=GROUPS_CORE, tiled=True)
    before = lax.ppermute(got, "ctx", PERM_Z_UP)
    terms, _ = lax.optimization_barrier((terms, got))
    terms = lax.all_to_all(terms, "tp", 0, 0, tiled=True)
    gate_keep = lax.dynamic_index_in_dim(gate, core, 0, False)
    gate_got = lax.ppermute(lax.dynamic_index_in_dim(gate, 1 - core, 0, False), "ctx", PERM_CORE)

    conv = convolve(z_at, *spectra(got), before)
    conv = call(pack_kernel, shape((32, 48, 128), BF16), whole(2), [], 10**5, (conv, terms))
    conv = lax.all_to_all(conv, "ctx", 0, 0, axis_index_groups=GROUPS_PLANE, tiled=True)

    width = w_unembed.shape[0]
    base = mm(lax.dynamic_slice_in_dim(tokens_in, tp * width, width, 1), w_unembed)
    logits = call(
        mix_kernel,
        shape((256, 512), BF16),
        [SCALARS] + whole(4),
        [],
        10**8,
        (core_at, conv, gate_keep, gate_got, base),
    )
    logits = lax.all_to_all(logits.reshape(4, 64, 512), "tp", 0, 0, axis_index_groups=GROUPS_TP, tiled=True)
    logits = jnp.sum(logits.astype(F32), axis=0).astype(BF16)
    far = lax.ppermute(logits, "tp", [(i, i ^ 4) for i in range(8)])
    logits = logits.astype(F32) + far.astype(F32)

    row_top = jnp.max(logits, axis=1, keepdims=True)
    log_total = row_top[:, 0] + jnp.log(jnp.sum(jnp.exp(logits - row_top), axis=1))
    ids = lax.dynamic_slice_in_dim(target_ids, (tp % 4) * 64, 64, 0)
    mask = lax.dynamic_slice_in_dim(score_mask, (tp % 4) * 64, 64, 0)
    vocab_index = lax.broadcasted_iota(jnp.int32, (64, 512), 1)
    picked = jnp.sum(jnp.where(vocab_index == ids[:, None], logits, 0.0), axis=1)
    scores = (picked - log_total) * mask.astype(F32)
    scores = jnp.broadcast_to(scores[None, :], (4, 64))
    scores = lax.all_to_all(scores, "tp", 0, 0, axis_index_groups=GROUPS_TP, tiled=True)
    return scores.reshape(256)


def solution(mesh):
    return jax.shard_map(
        per_device,
        mesh=mesh,
        in_specs=(
            P("ctx", None),
            P(),
            P("ctx", None, "tp"),
            P("ctx", "tp"),
            P("ctx", "tp"),
            P("tp", None),
            P("ctx"),
            P("ctx"),
        ),
        out_specs=P("ctx"),
        check_vma=False,
    )
```

```python
import math

import jax
import jax.numpy as jnp
import numpy as np
from jax import lax
from jax.experimental import pallas as pl
from jax.experimental.pallas import tpu as pltpu
from jax.sharding import PartitionSpec as P

NORM_EPS = 1e-05
F32 = jnp.float32
BF16 = jnp.bfloat16

COORDS = [(z, y, x, c) for z in range(2) for y in range(4) for x in range(4) for c in range(2)]


def ctx_id(z, y, x, c):
    return ((z * 4 + y) * 4 + x) * 2 + c


def ctx_perm(move):
    return [(ctx_id(*at), ctx_id(*move(*at))) for at in COORDS]


PERM_CORE = ctx_perm(lambda z, y, x, c: (z, y, x, 1 - c))
PERM_Z = ctx_perm(lambda z, y, x, c: (1 - z, y, x, c))
PERM_Z_UP = [(i, i + 32) for i in range(32)]
PERM_X = [ctx_perm(lambda z, y, x, c, k=k: (z, y, (x + k) % 4, c)) for k in range(4)]
PERM_Y = [ctx_perm(lambda z, y, x, c, k=k: (z, (y + k) % 4, x, c)) for k in range(4)]
GROUPS_X = [[ctx_id(z, y, x, c) for x in range(4)] for z in range(2) for y in range(4) for c in range(2)]
GROUPS_Y = [[ctx_id(z, y, x, c) for y in range(4)] for z in range(2) for x in range(4) for c in range(2)]
GROUPS_PLANE = [
    [ctx_id(z, y, x, c) for y in range(4) for x in range(4) for c in range(2)] for z in range(2)
]
GROUPS_CORE = [
    [ctx_id(z, y, x, c) for y in range(4) for x in range(4)] for z in range(2) for c in range(2)
]
GROUPS_TP = [[0, 1, 2, 3], [4, 5, 6, 7]]


def tables():
    index = np.arange(128)
    inner = 2.0 * math.pi * (np.outer(index, index) % 128) / 128
    outer = 2.0 * math.pi * np.outer(index, index) / 16384
    cos, sin = np.cos(inner), np.sin(inner)
    first = np.concatenate([cos[:, :64], -sin[:, :64]], axis=0)
    second = np.block([[cos, -sin], [sin, cos]])
    back = np.block([[cos, sin], [-sin, cos]])
    last = np.concatenate([cos[:64], -sin[:64]], axis=1) / 16384.0
    return (first, second, back, last, np.cos(outer), np.sin(outer))


FIRST, SECOND, BACK, LAST, COS_TW, SIN_TW = tables()
MATRICES = np.concatenate([np.pad(FIRST, ((0, 0), (0, 192))), SECOND, BACK, LAST])
TWIDDLES = np.concatenate([COS_TW, SIN_TW], axis=1)


def mm(left, right):
    return jnp.dot(left, right, preferred_element_type=F32)


def whole(count):
    return [pl.BlockSpec(memory_space=pltpu.VMEM)] * count


SCALARS = pl.BlockSpec(memory_space=pltpu.SMEM)
IN_HBM = pl.BlockSpec(memory_space=pltpu.HBM)


def spectrum(scratch, matrices, twiddles):
    cos_tw, sin_tw = twiddles[:, :128], twiddles[:, 128:]
    cube = jnp.concatenate([scratch[pl.ds(c, 64, stride=8), :] for c in range(8)], axis=1)
    step = mm(matrices[:256, :64], cube.astype(BF16))
    parts = []
    for c in range(8):
        real, imag = step[:128, c * 128 : c * 128 + 128], step[128:, c * 128 : c * 128 + 128]
        parts.append(
            jnp.concatenate(
                [(real * cos_tw + imag * sin_tw).astype(BF16), (imag * cos_tw - real * sin_tw).astype(BF16)],
                axis=1,
            )
        )
    return mm(jnp.concatenate(parts, axis=0), matrices[256:512, :])


def rows_of(scratch, ref, at):
    for p in range(16):
        scratch[p * 32 : p * 32 + 32] = ref[p, at : at + 32].astype(F32)


def spectra_kernel(got_ref, matrices, twiddles, signal_ref, filter_ref, scratch):
    rows_of(scratch, got_ref, 0)
    signal_ref[...] = spectrum(scratch, matrices, twiddles)
    rows_of(scratch, got_ref, 32)
    filter_ref[...] = spectrum(scratch, matrices, twiddles)


def conv_kernel(z_ref, signal_ref, filter_ref, before_ref, matrices, twiddles, out_ref, scratch):
    upper = z_ref[0] == 1
    cos_tw, sin_tw = twiddles[:, :128], twiddles[:, 128:]
    own, high = signal_ref[...], filter_ref[...]
    rows_of(scratch, before_ref, 0)
    old = jnp.where(upper, spectrum(scratch, matrices, twiddles), 0.0)
    rows_of(scratch, before_ref, 32)
    low = jnp.where(upper, spectrum(scratch, matrices, twiddles), high)
    odd = lax.broadcasted_iota(jnp.int32, (1024, 256), 0) & 1
    every = jnp.where(odd == 1, -low, low) + high
    own_r, own_i, old_r, old_i = own[:, :128], own[:, 128:], old[:, :128], old[:, 128:]
    low_r, low_i, all_r, all_i = low[:, :128], low[:, 128:], every[:, :128], every[:, 128:]
    real = own_r * low_r - own_i * low_i + old_r * all_r - old_i * all_i
    imag = own_r * low_i + own_i * low_r + old_r * all_i + old_i * all_r
    half = mm(jnp.concatenate([real.astype(BF16), imag.astype(BF16)], axis=1), matrices[512:768, :])
    parts = []
    for c in range(8):
        real, imag = half[c * 128 : c * 128 + 128, :128], half[c * 128 : c * 128 + 128, 128:]
        parts.append(
            jnp.concatenate(
                [(real * cos_tw - imag * sin_tw).astype(BF16), (imag * cos_tw + real * sin_tw).astype(BF16)],
                axis=0,
            )
        )
    result = mm(matrices[768:, :], jnp.concatenate(parts, axis=1))
    for c in range(8):
        scratch[pl.ds(c, 64, stride=8), :] = result[:, c * 128 : c * 128 + 128]
    for d in range(32):
        out_ref[d] = scratch[d * 16 : d * 16 + 16].astype(BF16)


def pack_kernel(conv_ref, terms_ref, out_ref):
    piece = sum(terms_ref[j].astype(F32) for j in range(8)).astype(BF16)
    for d in range(32):
        out_ref[d, :16] = conv_ref[d]
        out_ref[d, 16:] = piece


def first_kernel(core_ref, own_hbm, got_ref, rows_hbm, out_ref, own_ref, rows_ref, sems):
    copies = [
        pltpu.make_async_copy(own_hbm, own_ref, sems.at[0]),
        pltpu.make_async_copy(rows_hbm, rows_ref, sems.at[1]),
    ]
    for copy in copies:
        copy.start()
    for copy in copies:
        copy.wait()
    core = core_ref[0]
    half = pl.ds(pl.multiple_of(core * 128, 128), 128)
    for g in range(3):
        own, got = own_ref[g, :, half], got_ref[g, :, half]
        out_ref[g * 128 : g * 128 + 64] = jnp.where(core == 0, own, got)
        out_ref[g * 128 + 64 : g * 128 + 128] = jnp.where(core == 0, got, own)
    rows = rows_ref[...].astype(F32)
    blocks = [rows[y * 8 : y * 8 + 8, v * 128 : v * 128 + 128] for y in range(4) for v in range(4)]
    out_ref[384:] = jnp.concatenate(blocks, axis=0).astype(BF16)


def copies_kernel(first_ref, out_ref):
    for k in range(4):
        out_ref[k] = first_ref[:384]


def weight_block(ref, lead, row):
    return jnp.concatenate([ref[lead, row + 128 * g : row + 128 * g + 128, :] for g in range(3)], axis=1)


def norm_kernel(own_hbm, beside_hbm, gain_ref, gained_hbm, scale_ref, tokens, gained, sems):
    gain = gain_ref[...]
    copies, stores = [], []
    for part, ref in enumerate((own_hbm, beside_hbm)):
        for i in range(4):
            rows = pl.ds(i * 64, 64)
            copies.append(pltpu.make_async_copy(ref.at[rows], tokens.at[part, rows], sems.at[0, part, i]))
            stores.append(
                pltpu.make_async_copy(gained.at[part, rows], gained_hbm.at[part, rows], sems.at[1, part, i])
            )
    for copy in copies:
        copy.start()
    for k in range(8):
        copies[k].wait()
        part, i = k // 4, k % 4
        for half in range(2):
            rows = slice(i * 64 + half * 32, i * 64 + half * 32 + 32)
            block = tokens[part, rows, :]
            stream = block.astype(F32)
            mean = jnp.mean(stream * stream, axis=1, keepdims=True)
            scale_ref[part, rows, :] = jnp.broadcast_to(lax.rsqrt(mean + NORM_EPS), (32, 128))
            gained[part, rows, :] = block * gain
        stores[k].start()
    for store in stores:
        store.wait()


def near_kernel(
    at_ref, gained_hbm, own_taps, got_taps, near_ref, unembed_ref, out_ref, terms_ref, pieces_ref, gained, taps, sems
):
    core, z = at_ref[2], at_ref[3]
    columns = pl.ds(pl.multiple_of(z * 2048, 2048), 2048)
    copies = [
        pltpu.make_async_copy(gained_hbm.at[part, :, columns], gained.at[part], sems.at[part]) for part in range(2)
    ]
    copies.append(pltpu.make_async_copy(own_taps, taps.at[0], sems.at[2]))
    copies.append(pltpu.make_async_copy(got_taps, taps.at[1], sems.at[3]))
    for copy in copies:
        copy.start()

    blocks = []
    for plane in range(2):
        for y in range(4):
            block = near_ref[y, 1536 + plane * 32 : 1568 + plane * 32, :].astype(F32)
            blocks.append(jnp.concatenate([block[v * 8 : v * 8 + 8] for v in range(4)], axis=1))
    terms = mm(jnp.concatenate(blocks, axis=0).astype(BF16), unembed_ref[...])
    for j in range(8):
        parts = [terms[j * 8 : j * 8 + 8, v * 128 : v * 128 + 128] for v in range(4)]
        terms_ref[j] = jnp.concatenate(parts, axis=0).astype(BF16)

    for part in range(2):
        copies[part].wait()
        total = jnp.zeros((256, 384), F32)
        for y in range(4):
            for x in (0, 2):
                left = gained[part, :, (y * 4 + x) * 128 : (y * 4 + x) * 128 + 256]
                right = [weight_block(near_ref, y, x * 384), weight_block(near_ref, y, x * 384 + 384)]
                total += mm(left, jnp.concatenate(right, axis=0))
        out_ref[part] = total
    half = pl.ds(pl.multiple_of(core * 128, 128), 128)
    for part in range(2):
        copies[2 + part].wait()
        put_pieces(pieces_ref, 0, core if part == 0 else 1 - core, taps[part, :, half].astype(F32))


def put_pieces(ref, row, place, block):
    first, second = block[:128].T, block[128:].T
    for p in range(16):
        b = p * 8
        rows = jnp.concatenate([first[b : b + 8], second[b : b + 8]], axis=0).astype(BF16)
        ref[p, pl.ds(pl.multiple_of(row + place * 16, 16), 16), :] = rows


def proj_kernel(
    at_ref, gained_hbm, scale_ref, near_ref, pieces_ref, f0, f1, f2, f3, sig_ref, gate_ref, gained, fars, sems
):
    y_at, x_at, core = at_ref[0], at_ref[1], at_ref[2]
    columns = pl.ds(pl.multiple_of(2048 - at_ref[3] * 2048, 2048), 2048)
    copies = [
        pltpu.make_async_copy(gained_hbm.at[part, :, columns], gained.at[part], sems.at[part]) for part in range(2)
    ]
    copies += [pltpu.make_async_copy(f, fars.at[k], sems.at[2 + k]) for k, f in enumerate((f0, f1, f2, f3))]
    for k in (0, 2, 3, 4, 5, 1):
        copies[k].start()
    for part in range(2):
        copies[part].wait()
        total = near_ref[part]
        for step in range(4):
            if part == 0:
                copies[2 + step].wait()
            x = lax.rem(x_at + 4 - step, 4)
            for k in (0, 2):
                starts = [(lax.rem(y_at + 4 - j, 4) * 4 + x) * 128 for j in (k, k + 1)]
                left = [gained[part, :, pl.ds(pl.multiple_of(at, 128), 128)] for at in starts]
                right = [weight_block(fars.at[step], k, 0), weight_block(fars.at[step], k + 1, 0)]
                total += mm(jnp.concatenate(left, axis=1), jnp.concatenate(right, axis=0))
        scale = scale_ref[part]
        proj = (total * jnp.concatenate([scale, scale, scale], axis=1)).astype(BF16).astype(F32)
        place = core if part == 0 else 1 - core
        put_pieces(sig_ref, 0, place, proj[:, 128:256] * proj[:, 256:])
        gate_ref[place, 0] = proj[:128, :128].T.astype(BF16)
        gate_ref[place, 1] = proj[128:, :128].T.astype(BF16)
    for p in range(16):
        sig_ref[p, 32:, :] = pieces_ref[p]


def mix_kernel(core_ref, got_ref, keep_ref, other_ref, base_ref, out_ref):
    core = core_ref[0]
    keep, other = keep_ref[...].astype(F32), other_ref[...].astype(F32)
    conv = got_ref[:, :16, :].astype(F32)
    for rb in range(2):
        total = base_ref[rb * 128 : rb * 128 + 128, :]
        for c in range(2):
            cube = jnp.concatenate([conv[b * 2 + c, rb * 8 : rb * 8 + 8] for b in range(16)], axis=0)
            gate = jnp.where(core == c, keep[rb], other[rb])
            mixed = (gate * cube).T.astype(BF16)
            weights = []
            for b in range(16):
                x, holder, y = (c * 16 + b) // 8, b % 8 // 4, b % 4
                piece = got_ref[(y * 4 + x) * 2 + holder, 16:, :].astype(F32)
                weights.append(jnp.concatenate([piece[v * 8 : v * 8 + 8] for v in range(4)], axis=1))
            total += mm(mixed, jnp.concatenate(weights, axis=0).astype(BF16))
        out_ref[rb * 128 : rb * 128 + 128, :] = total.astype(BF16)


def call(kernel, outs, specs, scratch, flops, args, mib=8, out_specs=None):
    if out_specs is None:
        out_specs = jax.tree.map(lambda _: pl.BlockSpec(memory_space=pltpu.VMEM), outs)
    return pl.pallas_call(
        kernel,
        out_shape=outs,
        in_specs=specs,
        out_specs=out_specs,
        scratch_shapes=scratch,
        compiler_params=pltpu.CompilerParams(vmem_limit_bytes=mib * 2**20),
        cost_estimate=pl.CostEstimate(flops=flops, bytes_accessed=4 * 2**20, transcendentals=0),
    )(*args)


def shape(dims, dtype):
    return jax.ShapeDtypeStruct(dims, dtype)


def by_position(own, other, place):
    return jnp.where(place == 0, jnp.stack([own, other]), jnp.stack([other, own]))


def spectra(got):
    return call(
        spectra_kernel,
        (shape((1024, 256), F32), shape((1024, 256), F32)),
        whole(3),
        [pltpu.VMEM((512, 128), F32)],
        4 * 10**8,
        (got, jnp.asarray(MATRICES, BF16), jnp.asarray(TWIDDLES, F32)),
    )


def convolve(z, signal, taps, before):
    return call(
        conv_kernel,
        shape((32, 16, 128), BF16),
        [SCALARS] + whole(5),
        [pltpu.VMEM((512, 128), F32)],
        6 * 10**8,
        (z, signal, taps, before, jnp.asarray(MATRICES, BF16), jnp.asarray(TWIDDLES, F32)),
        mib=16,
    )


def per_device(tokens_in, pre_gain, w_in, w_out, long_filter, w_unembed, target_ids, score_mask):
    ctx, tp = lax.axis_index("ctx"), lax.axis_index("tp")
    core, z = ctx % 2, ctx // 32
    z_at = z.reshape(1).astype(jnp.int32)

    core_at = core.reshape(1).astype(jnp.int32)
    w_in = w_in.transpose(1, 0, 2)
    first = call(
        first_kernel,
        shape((512, 128), BF16),
        [SCALARS, IN_HBM] + whole(1) + [IN_HBM],
        [pltpu.VMEM((3, 64, 256), BF16), pltpu.VMEM((32, 512), BF16), pltpu.SemaphoreType.DMA((2,))],
        10**5,
        (core_at, w_in, lax.ppermute(w_in, "ctx", PERM_CORE), w_out),
    )
    near = call(copies_kernel, shape((4, 384, 128), BF16), whole(1), [], 10**10, (first,))
    near, tokens = lax.optimization_barrier((near, tokens_in))
    beside = lax.ppermute(tokens, "ctx", PERM_CORE)
    near = lax.all_to_all(near, "ctx", 0, 0, axis_index_groups=GROUPS_X, tiled=True)
    far = lax.ppermute(first, "ctx", PERM_Z)

    rows = by_position(first[384:].reshape(4, 32, 128), far[384:].reshape(4, 32, 128), z)
    far = far[:384]
    far = jnp.stack([far] + [lax.ppermute(far, "ctx", PERM_Y[k]) for k in (1, 2, 3)])
    near, far, rows, taps = lax.optimization_barrier((near, far, rows, long_filter))

    near = jnp.broadcast_to(near.reshape(1, 1536, 128), (4, 1536, 128))
    near = jnp.concatenate([near, rows[0], rows[1]], axis=1)
    near = lax.all_to_all(near, "ctx", 0, 0, axis_index_groups=GROUPS_Y, tiled=True)
    fars = [far] + [lax.ppermute(far, "ctx", PERM_X[k]) for k in (1, 2, 3)]
    taps_got = lax.ppermute(taps, "ctx", PERM_CORE)

    at = jnp.stack([(ctx // 8) % 4, (ctx // 2) % 4, core, z]).astype(jnp.int32)
    gained, scale = call(
        norm_kernel,
        (shape((2, 256, 4096), BF16), shape((2, 256, 128), F32)),
        [IN_HBM, IN_HBM] + whole(1),
        [
            pltpu.VMEM((2, 256, 4096), BF16),
            pltpu.VMEM((2, 256, 4096), BF16),
            pltpu.SemaphoreType.DMA((2, 2, 4)),
        ],
        10**7,
        (tokens_in, beside, pre_gain.reshape(1, 4096)),
        mib=16,
        out_specs=(IN_HBM, whole(1)[0]),
    )
    sums, terms, pieces = call(
        near_kernel,
        (shape((2, 256, 384), F32), shape((8, 32, 128), BF16), shape((16, 32, 128), BF16)),
        [SCALARS] + [IN_HBM] * 3 + whole(2),
        [pltpu.VMEM((2, 256, 2048), BF16), pltpu.VMEM((2, 256, 256), BF16), pltpu.SemaphoreType.DMA((4,))],
        8 * 10**8,
        (at, gained, taps, taps_got, near, w_unembed),
    )
    signal, gate = call(
        proj_kernel,
        (shape((16, 64, 128), BF16), shape((2, 2, 128, 128), BF16)),
        [SCALARS, IN_HBM] + whole(3) + [IN_HBM] * 4,
        [pltpu.VMEM((2, 256, 2048), BF16), pltpu.VMEM((4, 4, 384, 128), BF16), pltpu.SemaphoreType.DMA((6,))],
        8 * 10**8,
        (at, gained, scale, sums, pieces, *fars),
    )
    got = lax.all_to_all(signal, "ctx", 0, 0, axis_index_groups=GROUPS_CORE, tiled=True)
    before = lax.ppermute(got, "ctx", PERM_Z_UP)
    terms, _ = lax.optimization_barrier((terms, got))
    terms = lax.all_to_all(terms, "tp", 0, 0, tiled=True)
    gate_keep = lax.dynamic_index_in_dim(gate, core, 0, False)
    gate_got = lax.ppermute(lax.dynamic_index_in_dim(gate, 1 - core, 0, False), "ctx", PERM_CORE)

    conv = convolve(z_at, *spectra(got), before)
    conv = call(pack_kernel, shape((32, 48, 128), BF16), whole(2), [], 10**5, (conv, terms))
    conv = lax.all_to_all(conv, "ctx", 0, 0, axis_index_groups=GROUPS_PLANE, tiled=True)

    width = w_unembed.shape[0]
    base = mm(lax.dynamic_slice_in_dim(tokens_in, tp * width, width, 1), w_unembed)
    logits = call(
        mix_kernel,
        shape((256, 512), BF16),
        [SCALARS] + whole(4),
        [],
        10**8,
        (core_at, conv, gate_keep, gate_got, base),
    )
    logits = lax.all_to_all(logits.reshape(4, 64, 512), "tp", 0, 0, axis_index_groups=GROUPS_TP, tiled=True)
    logits = jnp.sum(logits.astype(F32), axis=0).astype(BF16)
    far = lax.ppermute(logits, "tp", [(i, i ^ 4) for i in range(8)])
    logits = logits.astype(F32) + far.astype(F32)

    row_top = jnp.max(logits, axis=1, keepdims=True)
    log_total = row_top[:, 0] + jnp.log(jnp.sum(jnp.exp(logits - row_top), axis=1))
    ids = lax.dynamic_slice_in_dim(target_ids, (tp % 4) * 64, 64, 0)
    mask = lax.dynamic_slice_in_dim(score_mask, (tp % 4) * 64, 64, 0)
    vocab_index = lax.broadcasted_iota(jnp.int32, (64, 512), 1)
    picked = jnp.sum(jnp.where(vocab_index == ids[:, None], logits, 0.0), axis=1)
    scores = (picked - log_total) * mask.astype(F32)
    scores = jnp.broadcast_to(scores[None, :], (4, 64))
    scores = lax.all_to_all(scores, "tp", 0, 0, axis_index_groups=GROUPS_TP, tiled=True)
    return scores.reshape(256)


def solution(mesh):
    return jax.shard_map(
        per_device,
        mesh=mesh,
        in_specs=(
            P("ctx", None),
            P(),
            P("ctx", None, "tp"),
            P("ctx", "tp"),
            P("ctx", "tp"),
            P("tp", None),
            P("ctx"),
            P("ctx"),
        ),
        out_specs=P("ctx"),
        check_vma=False,
    )
```

```python
import math

import jax
import jax.numpy as jnp
import numpy as np
from jax import lax
from jax.experimental import pallas as pl
from jax.experimental.pallas import tpu as pltpu
from jax.sharding import PartitionSpec as P

NORM_EPS = 1e-05
F32 = jnp.float32
BF16 = jnp.bfloat16

COORDS = [(z, y, x, c) for z in range(2) for y in range(4) for x in range(4) for c in range(2)]


def ctx_id(z, y, x, c):
    return ((z * 4 + y) * 4 + x) * 2 + c


def ctx_perm(move):
    return [(ctx_id(*at), ctx_id(*move(*at))) for at in COORDS]


PERM_CORE = ctx_perm(lambda z, y, x, c: (z, y, x, 1 - c))
PERM_Z = ctx_perm(lambda z, y, x, c: (1 - z, y, x, c))
PERM_Z_UP = [(i, i + 32) for i in range(32)]
PERM_X = [ctx_perm(lambda z, y, x, c, k=k: (z, y, (x + k) % 4, c)) for k in range(4)]
PERM_Y = [ctx_perm(lambda z, y, x, c, k=k: (z, (y + k) % 4, x, c)) for k in range(4)]
GROUPS_X = [[ctx_id(z, y, x, c) for x in range(4)] for z in range(2) for y in range(4) for c in range(2)]
GROUPS_Y = [[ctx_id(z, y, x, c) for y in range(4)] for z in range(2) for x in range(4) for c in range(2)]
GROUPS_PLANE = [
    [ctx_id(z, y, x, c) for y in range(4) for x in range(4) for c in range(2)] for z in range(2)
]
GROUPS_CORE = [
    [ctx_id(z, y, x, c) for y in range(4) for x in range(4)] for z in range(2) for c in range(2)
]
GROUPS_TP = [[0, 1, 2, 3], [4, 5, 6, 7]]


def tables():
    index = np.arange(128)
    inner = 2.0 * math.pi * (np.outer(index, index) % 128) / 128
    outer = 2.0 * math.pi * np.outer(index, index) / 16384
    cos, sin = np.cos(inner), np.sin(inner)
    first = np.concatenate([cos[:, :64], -sin[:, :64]], axis=0)
    second = np.block([[cos, -sin], [sin, cos]])
    back = np.block([[cos, sin], [-sin, cos]])
    last = np.concatenate([cos[:64], -sin[:64]], axis=1) / 16384.0
    return (first, second, back, last, np.cos(outer), np.sin(outer))


FIRST, SECOND, BACK, LAST, COS_TW, SIN_TW = tables()
MATRICES = np.concatenate([np.pad(FIRST, ((0, 0), (0, 192))), SECOND, BACK, LAST])
TWIDDLES = np.concatenate([COS_TW, SIN_TW], axis=1)


def mm(left, right):
    return jnp.dot(left, right, preferred_element_type=F32)


def whole(count):
    return [pl.BlockSpec(memory_space=pltpu.VMEM)] * count


SCALARS = pl.BlockSpec(memory_space=pltpu.SMEM)
IN_HBM = pl.BlockSpec(memory_space=pltpu.HBM)


def spectrum(scratch, matrices, twiddles):
    cos_tw, sin_tw = twiddles[:, :128], twiddles[:, 128:]
    cube = jnp.concatenate([scratch[pl.ds(c, 64, stride=8), :] for c in range(8)], axis=1)
    step = mm(matrices[:256, :64], cube.astype(BF16))
    parts = []
    for c in range(8):
        real, imag = step[:128, c * 128 : c * 128 + 128], step[128:, c * 128 : c * 128 + 128]
        parts.append(
            jnp.concatenate(
                [(real * cos_tw + imag * sin_tw).astype(BF16), (imag * cos_tw - real * sin_tw).astype(BF16)],
                axis=1,
            )
        )
    return mm(jnp.concatenate(parts, axis=0), matrices[256:512, :])


def rows_of(scratch, ref, at):
    for p in range(16):
        scratch[p * 32 : p * 32 + 32] = ref[p, at : at + 32].astype(F32)


def spectra_kernel(got_ref, matrices, twiddles, signal_ref, filter_ref, scratch):
    rows_of(scratch, got_ref, 0)
    signal_ref[...] = spectrum(scratch, matrices, twiddles)
    rows_of(scratch, got_ref, 32)
    filter_ref[...] = spectrum(scratch, matrices, twiddles)


def conv_kernel(z_ref, signal_ref, filter_ref, before_ref, matrices, twiddles, out_ref, scratch):
    upper = z_ref[0] == 1
    cos_tw, sin_tw = twiddles[:, :128], twiddles[:, 128:]
    own, high = signal_ref[...], filter_ref[...]
    rows_of(scratch, before_ref, 0)
    old = jnp.where(upper, spectrum(scratch, matrices, twiddles), 0.0)
    rows_of(scratch, before_ref, 32)
    low = jnp.where(upper, spectrum(scratch, matrices, twiddles), high)
    odd = lax.broadcasted_iota(jnp.int32, (1024, 256), 0) & 1
    every = jnp.where(odd == 1, -low, low) + high
    own_r, own_i, old_r, old_i = own[:, :128], own[:, 128:], old[:, :128], old[:, 128:]
    low_r, low_i, all_r, all_i = low[:, :128], low[:, 128:], every[:, :128], every[:, 128:]
    real = own_r * low_r - own_i * low_i + old_r * all_r - old_i * all_i
    imag = own_r * low_i + own_i * low_r + old_r * all_i + old_i * all_r
    half = mm(jnp.concatenate([real.astype(BF16), imag.astype(BF16)], axis=1), matrices[512:768, :])
    parts = []
    for c in range(8):
        real, imag = half[c * 128 : c * 128 + 128, :128], half[c * 128 : c * 128 + 128, 128:]
        parts.append(
            jnp.concatenate(
                [(real * cos_tw - imag * sin_tw).astype(BF16), (imag * cos_tw + real * sin_tw).astype(BF16)],
                axis=0,
            )
        )
    result = mm(matrices[768:, :], jnp.concatenate(parts, axis=1))
    for c in range(8):
        scratch[pl.ds(c, 64, stride=8), :] = result[:, c * 128 : c * 128 + 128]
    for d in range(32):
        out_ref[d] = scratch[d * 16 : d * 16 + 16].astype(BF16)


def pack_kernel(conv_ref, terms_ref, out_ref):
    piece = sum(terms_ref[j].astype(F32) for j in range(8)).astype(BF16)
    for d in range(32):
        out_ref[d, :16] = conv_ref[d]
        out_ref[d, 16:] = piece


def first_kernel(core_ref, own_ref, got_ref, rows_ref, out_ref):
    core = core_ref[0]
    half = pl.ds(pl.multiple_of(core * 128, 128), 128)
    for g in range(3):
        own, got = own_ref[g], got_ref[g, :, half]
        out_ref[g * 128 : g * 128 + 64] = jnp.where(core == 0, own, got)
        out_ref[g * 128 + 64 : g * 128 + 128] = jnp.where(core == 0, got, own)
    out_ref[384:] = rows_ref[...]


def copies_kernel(first_ref, out_ref):
    for k in range(4):
        out_ref[k] = first_ref[:384]


def spread_kernel(z_ref, near_ref, first_ref, far_ref, out_hbm, sems):
    z = z_ref[0]
    copies = []
    for y in range(4):
        copies.append(pltpu.make_async_copy(near_ref, out_hbm.at[y, pl.ds(0, 1536)], sems.at[y, 0]))
        rows = pl.ds(384 + y * 32, 32)
        for k, (ref, place) in enumerate(((first_ref, z), (far_ref, 1 - z))):
            to = pl.ds(pl.multiple_of(1536 + place * 32, 32), 32)
            copies.append(pltpu.make_async_copy(ref.at[rows], out_hbm.at[y, to], sems.at[y, k + 1]))
    for copy in copies:
        copy.start()
    for copy in copies:
        copy.wait()


def last_kernel(scores_ref, out_ref):
    out_ref[...] = jnp.concatenate([scores_ref[k] for k in range(4)], axis=1)


def weight_block(ref, lead, row):
    return jnp.concatenate([ref[lead, row + 128 * g : row + 128 * g + 128, :] for g in range(3)], axis=1)


def near_kernel(
    at_ref, own_hbm, beside_hbm, gain_ref, own_taps, got_taps, near_ref, unembed_ref,
    gained_ref, scale_ref, out_ref, terms_ref, pieces_ref, tokens, taps, sems,
):
    core, start = at_ref[2], at_ref[3] * 2048
    gain = gain_ref[...]
    copies = []
    for part, ref in enumerate((own_hbm, beside_hbm)):
        for i in range(4):
            rows = pl.ds(i * 64, 64)
            copies.append(pltpu.make_async_copy(ref.at[rows], tokens.at[part, rows], sems.at[part, i]))
    copies.append(pltpu.make_async_copy(own_taps, taps.at[0], sems.at[2, 0]))
    copies.append(pltpu.make_async_copy(got_taps, taps.at[1], sems.at[2, 1]))
    for copy in copies:
        copy.start()

    blocks = []
    for plane in range(2):
        for y in range(4):
            block = near_ref[y, 1536 + plane * 32 : 1568 + plane * 32, :].astype(F32)
            blocks.append(jnp.concatenate([block[v * 8 : v * 8 + 8] for v in range(4)], axis=1))
    terms = mm(jnp.concatenate(blocks, axis=0).astype(BF16), unembed_ref[...])
    for j in range(8):
        parts = [terms[j * 8 : j * 8 + 8, v * 128 : v * 128 + 128] for v in range(4)]
        terms_ref[j] = jnp.concatenate(parts, axis=0).astype(BF16)

    for part in range(2):
        for i in range(4):
            copies[part * 4 + i].wait()
            for half in range(2):
                rows = slice(i * 64 + half * 32, i * 64 + half * 32 + 32)
                block = tokens[part, rows, :]
                stream = block.astype(F32)
                mean = jnp.mean(stream * stream, axis=1, keepdims=True)
                scale_ref[part, rows, :] = jnp.broadcast_to(lax.rsqrt(mean + NORM_EPS), (32, 128))
                gained_ref[part, rows, :] = block * gain
        total = jnp.zeros((256, 384), F32)
        for y in range(4):
            for x in (0, 2):
                left = gained_ref[part, :, pl.ds(pl.multiple_of(start + (y * 4 + x) * 128, 128), 256)]
                right = [weight_block(near_ref, y, x * 384), weight_block(near_ref, y, x * 384 + 384)]
                total += mm(left, jnp.concatenate(right, axis=0))
        out_ref[part] = total
    half = pl.ds(pl.multiple_of(core * 128, 128), 128)
    for part in range(2):
        copies[8 + part].wait()
        put_pieces(pieces_ref, 0, core if part == 0 else 1 - core, taps[part, :, half].astype(F32))


def put_pieces(ref, row, place, block):
    first, second = block[:128].T, block[128:].T
    for p in range(16):
        b = p * 8
        rows = jnp.concatenate([first[b : b + 8], second[b : b + 8]], axis=0).astype(BF16)
        ref[p, pl.ds(pl.multiple_of(row + place * 16, 16), 16), :] = rows


def proj_kernel(at_ref, gained_ref, scale_ref, near_ref, pieces_ref, f0, f1, f2, f3, sig_ref, gate_ref, fars, sems):
    y_at, x_at, core = at_ref[0], at_ref[1], at_ref[2]
    start = 2048 - at_ref[3] * 2048
    copies = [pltpu.make_async_copy(f, fars.at[k], sems.at[k]) for k, f in enumerate((f0, f1, f2, f3))]
    for copy in copies:
        copy.start()
    for part in range(2):
        total = near_ref[part]
        for step in range(4):
            if part == 0:
                copies[step].wait()
            x = lax.rem(x_at + 4 - step, 4)
            for k in (0, 2):
                starts = [start + (lax.rem(y_at + 4 - j, 4) * 4 + x) * 128 for j in (k, k + 1)]
                left = [gained_ref[part, :, pl.ds(pl.multiple_of(at, 128), 128)] for at in starts]
                right = [weight_block(fars.at[step], k, 0), weight_block(fars.at[step], k + 1, 0)]
                total += mm(jnp.concatenate(left, axis=1), jnp.concatenate(right, axis=0))
        scale = scale_ref[part]
        proj = (total * jnp.concatenate([scale, scale, scale], axis=1)).astype(BF16).astype(F32)
        place = core if part == 0 else 1 - core
        put_pieces(sig_ref, 0, place, proj[:, 128:256] * proj[:, 256:])
        gate_ref[place, 0] = proj[:128, :128].T.astype(BF16)
        gate_ref[place, 1] = proj[128:, :128].T.astype(BF16)
    for p in range(16):
        sig_ref[p, 32:, :] = pieces_ref[p]


def mix_kernel(core_ref, got_ref, keep_ref, other_ref, base_ref, out_ref):
    core = core_ref[0]
    keep, other = keep_ref[...].astype(F32), other_ref[...].astype(F32)
    conv = got_ref[:, :16, :].astype(F32)
    for rb in range(2):
        total = base_ref[rb * 128 : rb * 128 + 128, :]
        for c in range(2):
            cube = jnp.concatenate([conv[b * 2 + c, rb * 8 : rb * 8 + 8] for b in range(16)], axis=0)
            gate = jnp.where(core == c, keep[rb], other[rb])
            mixed = (gate * cube).T.astype(BF16)
            weights = []
            for b in range(16):
                x, holder, y = (c * 16 + b) // 8, b % 8 // 4, b % 4
                piece = got_ref[(y * 4 + x) * 2 + holder, 16:, :].astype(F32)
                weights.append(jnp.concatenate([piece[v * 8 : v * 8 + 8] for v in range(4)], axis=1))
            total += mm(mixed, jnp.concatenate(weights, axis=0).astype(BF16))
        out_ref[rb * 128 : rb * 128 + 128, :] = total.astype(BF16)


def call(kernel, outs, specs, scratch, flops, args, mib=8, out_specs=None):
    if out_specs is None:
        out_specs = jax.tree.map(lambda _: pl.BlockSpec(memory_space=pltpu.VMEM), outs)
    return pl.pallas_call(
        kernel,
        out_shape=outs,
        in_specs=specs,
        out_specs=out_specs,
        scratch_shapes=scratch,
        compiler_params=pltpu.CompilerParams(vmem_limit_bytes=mib * 2**20),
        cost_estimate=pl.CostEstimate(flops=flops, bytes_accessed=4 * 2**20, transcendentals=0),
    )(*args)


def shape(dims, dtype):
    return jax.ShapeDtypeStruct(dims, dtype)


def by_position(own, other, place):
    return jnp.where(place == 0, jnp.stack([own, other]), jnp.stack([other, own]))


def spectra(got):
    return call(
        spectra_kernel,
        (shape((1024, 256), F32), shape((1024, 256), F32)),
        whole(3),
        [pltpu.VMEM((512, 128), F32)],
        4 * 10**8,
        (got, jnp.asarray(MATRICES, BF16), jnp.asarray(TWIDDLES, F32)),
    )


def convolve(z, signal, taps, before):
    return call(
        conv_kernel,
        shape((32, 16, 128), BF16),
        [SCALARS] + whole(5),
        [pltpu.VMEM((512, 128), F32)],
        6 * 10**8,
        (z, signal, taps, before, jnp.asarray(MATRICES, BF16), jnp.asarray(TWIDDLES, F32)),
        mib=16,
    )


def per_device(tokens_in, pre_gain, w_in, w_out, long_filter, w_unembed, target_ids, score_mask):
    ctx, tp = lax.axis_index("ctx"), lax.axis_index("tp")
    core, z = ctx % 2, ctx // 32
    z_at = z.reshape(1).astype(jnp.int32)

    core_at = core.reshape(1).astype(jnp.int32)
    w_in = w_in.transpose(1, 0, 2)
    keep = lax.dynamic_slice_in_dim(w_in, core * 128, 128, 2)
    rows = w_out.reshape(4, 8, 4, 128).transpose(0, 2, 1, 3).reshape(128, 128)
    first = call(
        first_kernel,
        shape((512, 128), BF16),
        [SCALARS] + whole(3),
        [],
        10**5,
        (core_at, keep, lax.ppermute(w_in, "ctx", PERM_CORE), rows),
    )
    near = call(copies_kernel, shape((4, 384, 128), BF16), whole(1), [], 10**10, (first,))
    near, tokens = lax.optimization_barrier((near, tokens_in))
    beside = lax.ppermute(tokens, "ctx", PERM_CORE)
    near = lax.all_to_all(near, "ctx", 0, 0, axis_index_groups=GROUPS_X, tiled=True)
    far = lax.ppermute(first, "ctx", PERM_Z)

    along = far[:384]
    along = jnp.stack([along] + [lax.ppermute(along, "ctx", PERM_Y[k]) for k in (1, 2, 3)])
    near, along, far, taps = lax.optimization_barrier((near, along, far, long_filter))

    near = call(
        spread_kernel,
        shape((4, 1600, 128), BF16),
        [SCALARS] + whole(3),
        [pltpu.SemaphoreType.DMA((4, 3))],
        10**5,
        (z_at, near.reshape(1536, 128), first, far),
        out_specs=IN_HBM,
    )
    near = lax.all_to_all(near, "ctx", 0, 0, axis_index_groups=GROUPS_Y, tiled=True)
    far = along
    fars = [far] + [lax.ppermute(far, "ctx", PERM_X[k]) for k in (1, 2, 3)]
    taps_got = lax.ppermute(taps, "ctx", PERM_CORE)

    at = jnp.stack([(ctx // 8) % 4, (ctx // 2) % 4, core, z]).astype(jnp.int32)
    gained, scale, sums, terms, pieces = call(
        near_kernel,
        (
            shape((2, 256, 4096), BF16),
            shape((2, 256, 128), F32),
            shape((2, 256, 384), F32),
            shape((8, 32, 128), BF16),
            shape((16, 32, 128), BF16),
        ),
        [SCALARS, IN_HBM, IN_HBM] + whole(1) + [IN_HBM, IN_HBM] + whole(2),
        [pltpu.VMEM((2, 256, 4096), BF16), pltpu.VMEM((2, 256, 256), BF16), pltpu.SemaphoreType.DMA((3, 4))],
        8 * 10**8,
        (at, tokens_in, beside, pre_gain.reshape(1, 4096), taps, taps_got, near, w_unembed),
        mib=12,
    )
    signal, gate = call(
        proj_kernel,
        (shape((16, 64, 128), BF16), shape((2, 2, 128, 128), BF16)),
        [SCALARS] + whole(4) + [IN_HBM] * 4,
        [pltpu.VMEM((4, 4, 384, 128), BF16), pltpu.SemaphoreType.DMA((4,))],
        8 * 10**8,
        (at, gained, scale, sums, pieces, *fars),
    )
    got = lax.all_to_all(signal, "ctx", 0, 0, axis_index_groups=GROUPS_CORE, tiled=True)
    before = lax.ppermute(got, "ctx", PERM_Z_UP)
    terms, _ = lax.optimization_barrier((terms, got))
    terms = lax.all_to_all(terms, "tp", 0, 0, tiled=True)
    gate_keep = lax.dynamic_index_in_dim(gate, core, 0, False)
    gate_got = lax.ppermute(lax.dynamic_index_in_dim(gate, 1 - core, 0, False), "ctx", PERM_CORE)

    conv = convolve(z_at, *spectra(got), before)
    conv = call(pack_kernel, shape((32, 48, 128), BF16), whole(2), [], 10**5, (conv, terms))
    conv = lax.all_to_all(conv, "ctx", 0, 0, axis_index_groups=GROUPS_PLANE, tiled=True)

    width = w_unembed.shape[0]
    base = mm(lax.dynamic_slice_in_dim(tokens_in, tp * width, width, 1), w_unembed)
    logits = call(
        mix_kernel,
        shape((256, 512), BF16),
        [SCALARS] + whole(4),
        [],
        10**8,
        (core_at, conv, gate_keep, gate_got, base),
    )
    logits = lax.all_to_all(logits.reshape(4, 64, 512), "tp", 0, 0, axis_index_groups=GROUPS_TP, tiled=True)
    logits = jnp.sum(logits.astype(F32), axis=0).astype(BF16)
    far = lax.ppermute(logits, "tp", [(i, i ^ 4) for i in range(8)])
    logits = logits.astype(F32) + far.astype(F32)

    row_top = jnp.max(logits, axis=1, keepdims=True)
    log_total = row_top[:, 0] + jnp.log(jnp.sum(jnp.exp(logits - row_top), axis=1))
    ids = lax.dynamic_slice_in_dim(target_ids, (tp % 4) * 64, 64, 0)
    mask = lax.dynamic_slice_in_dim(score_mask, (tp % 4) * 64, 64, 0)
    vocab_index = lax.broadcasted_iota(jnp.int32, (64, 512), 1)
    picked = jnp.sum(jnp.where(vocab_index == ids[:, None], logits, 0.0), axis=1)
    scores = (picked - log_total) * mask.astype(F32)
    scores = jnp.broadcast_to(scores[None, None, :], (4, 1, 64))
    scores = lax.all_to_all(scores, "tp", 0, 0, axis_index_groups=GROUPS_TP, tiled=True)
    return call(last_kernel, shape((1, 256), F32), whole(1), [], 10**3, (scores,)).reshape(256)


def solution(mesh):
    return jax.shard_map(
        per_device,
        mesh=mesh,
        in_specs=(
            P("ctx", None),
            P(),
            P("ctx", None, "tp"),
            P("ctx", "tp"),
            P("ctx", "tp"),
            P("tp", None),
            P("ctx"),
            P("ctx"),
        ),
        out_specs=P("ctx"),
        check_vma=False,
    )
```

```python
import math

import jax
import jax.numpy as jnp
import numpy as np
from jax import lax
from jax.experimental import pallas as pl
from jax.experimental.pallas import tpu as pltpu
from jax.sharding import PartitionSpec as P

NORM_EPS = 1e-05
F32 = jnp.float32
BF16 = jnp.bfloat16

COORDS = [(z, y, x, c) for z in range(2) for y in range(4) for x in range(4) for c in range(2)]


def ctx_id(z, y, x, c):
    return ((z * 4 + y) * 4 + x) * 2 + c


def ctx_perm(move):
    return [(ctx_id(*at), ctx_id(*move(*at))) for at in COORDS]


PERM_CORE = ctx_perm(lambda z, y, x, c: (z, y, x, 1 - c))
PERM_Z = ctx_perm(lambda z, y, x, c: (1 - z, y, x, c))
PERM_Z_UP = [(i, i + 32) for i in range(32)]
PERM_X = [ctx_perm(lambda z, y, x, c, k=k: (z, y, (x + k) % 4, c)) for k in range(4)]
PERM_Y = [ctx_perm(lambda z, y, x, c, k=k: (z, (y + k) % 4, x, c)) for k in range(4)]
GROUPS_X = [[ctx_id(z, y, x, c) for x in range(4)] for z in range(2) for y in range(4) for c in range(2)]
GROUPS_Y = [[ctx_id(z, y, x, c) for y in range(4)] for z in range(2) for x in range(4) for c in range(2)]
GROUPS_PLANE = [
    [ctx_id(z, y, x, c) for y in range(4) for x in range(4) for c in range(2)] for z in range(2)
]
GROUPS_CORE = [
    [ctx_id(z, y, x, c) for y in range(4) for x in range(4)] for z in range(2) for c in range(2)
]
GROUPS_TP = [[0, 1, 2, 3], [4, 5, 6, 7]]


def tables():
    index = np.arange(128)
    inner = 2.0 * math.pi * (np.outer(index, index) % 128) / 128
    outer = 2.0 * math.pi * np.outer(index, index) / 16384
    cos, sin = np.cos(inner), np.sin(inner)
    first = np.concatenate([cos[:, :64], -sin[:, :64]], axis=0)
    second = np.block([[cos, -sin], [sin, cos]])
    back = np.block([[cos, sin], [-sin, cos]])
    last = np.concatenate([cos[:64], -sin[:64]], axis=1) / 16384.0
    return (first, second, back, last, np.cos(outer), np.sin(outer))


FIRST, SECOND, BACK, LAST, COS_TW, SIN_TW = tables()
MATRICES = np.concatenate([np.pad(FIRST, ((0, 0), (0, 192))), SECOND, BACK, LAST])
TWIDDLES = np.concatenate([COS_TW, SIN_TW], axis=1)


def mm(left, right):
    return jnp.dot(left, right, preferred_element_type=F32)


def whole(count):
    return [pl.BlockSpec(memory_space=pltpu.VMEM)] * count


SCALARS = pl.BlockSpec(memory_space=pltpu.SMEM)
IN_HBM = pl.BlockSpec(memory_space=pltpu.HBM)


def spectrum(scratch, matrices, twiddles):
    cos_tw, sin_tw = twiddles[:, :128], twiddles[:, 128:]
    cube = jnp.concatenate([scratch[pl.ds(c, 64, stride=8), :] for c in range(8)], axis=1)
    step = mm(matrices[:256, :64], cube.astype(BF16))
    parts = []
    for c in range(8):
        real, imag = step[:128, c * 128 : c * 128 + 128], step[128:, c * 128 : c * 128 + 128]
        parts.append(
            jnp.concatenate(
                [(real * cos_tw + imag * sin_tw).astype(BF16), (imag * cos_tw - real * sin_tw).astype(BF16)],
                axis=1,
            )
        )
    return mm(jnp.concatenate(parts, axis=0), matrices[256:512, :])


def rows_of(scratch, ref, at):
    for p in range(16):
        scratch[p * 32 : p * 32 + 32] = ref[p, at : at + 32].astype(F32)


def spectra_kernel(z_ref, got_ref, matrices, twiddles, signal_ref, low_ref, all_ref, scratch):
    upper = z_ref[0] == 1
    rows_of(scratch, got_ref, 0)
    signal_ref[...] = spectrum(scratch, matrices, twiddles)
    rows_of(scratch, got_ref, 32)
    high = spectrum(scratch, matrices, twiddles)
    rows_of(scratch, got_ref, 64)
    low = jnp.where(upper, spectrum(scratch, matrices, twiddles), high)
    low_ref[...] = low
    odd = lax.broadcasted_iota(jnp.int32, (1024, 256), 0) & 1
    all_ref[...] = jnp.where(odd == 1, -low, low) + high


def conv_kernel(z_ref, signal_ref, low_ref, all_ref, before_ref, matrices, twiddles, out_ref, scratch):
    cos_tw, sin_tw = twiddles[:, :128], twiddles[:, 128:]
    own, low, every = signal_ref[...], low_ref[...], all_ref[...]
    scratch[...] = before_ref[...].astype(F32)
    old = jnp.where(z_ref[0] == 1, spectrum(scratch, matrices, twiddles), 0.0)
    own_r, own_i, old_r, old_i = own[:, :128], own[:, 128:], old[:, :128], old[:, 128:]
    low_r, low_i, all_r, all_i = low[:, :128], low[:, 128:], every[:, :128], every[:, 128:]
    real = own_r * low_r - own_i * low_i + old_r * all_r - old_i * all_i
    imag = own_r * low_i + own_i * low_r + old_r * all_i + old_i * all_r
    half = mm(jnp.concatenate([real.astype(BF16), imag.astype(BF16)], axis=1), matrices[512:768, :])
    parts = []
    for c in range(8):
        real, imag = half[c * 128 : c * 128 + 128, :128], half[c * 128 : c * 128 + 128, 128:]
        parts.append(
            jnp.concatenate(
                [(real * cos_tw - imag * sin_tw).astype(BF16), (imag * cos_tw + real * sin_tw).astype(BF16)],
                axis=0,
            )
        )
    result = mm(matrices[768:, :], jnp.concatenate(parts, axis=1))
    for c in range(8):
        scratch[pl.ds(c, 64, stride=8), :] = result[:, c * 128 : c * 128 + 128]
    for d in range(32):
        out_ref[d] = scratch[d * 16 : d * 16 + 16].astype(BF16)


def pack_kernel(conv_ref, terms_ref, out_ref):
    piece = sum(terms_ref[j].astype(F32) for j in range(8)).astype(BF16)
    for d in range(32):
        out_ref[d, :16] = conv_ref[d]
        out_ref[d, 16:] = piece


def first_kernel(core_ref, own_ref, got_ref, rows_ref, taps_ref, out_ref):
    core = core_ref[0]
    half = pl.ds(pl.multiple_of(core * 128, 128), 128)
    for g in range(3):
        own, got = own_ref[g], got_ref[g, :, half]
        out_ref[g * 128 : g * 128 + 64] = jnp.where(core == 0, own, got)
        out_ref[g * 128 + 64 : g * 128 + 128] = jnp.where(core == 0, got, own)
    out_ref[384:512] = rows_ref[...]
    out_ref[512:768] = taps_ref[:, :128]
    out_ref[768:] = taps_ref[:, 128:]


def copies_kernel(first_ref, out_ref):
    for k in range(4):
        out_ref[k] = first_ref[:384]


def spread_kernel(z_ref, near_ref, first_ref, far_ref, out_hbm, sems):
    z = z_ref[0]
    copies = []
    for y in range(4):
        copies.append(pltpu.make_async_copy(near_ref, out_hbm.at[y, pl.ds(0, 1536)], sems.at[y, 0]))
        rows = pl.ds(384 + y * 32, 32)
        for k, (ref, place) in enumerate(((first_ref, z), (far_ref, 1 - z))):
            to = pl.ds(pl.multiple_of(1536 + place * 32, 32), 32)
            copies.append(pltpu.make_async_copy(ref.at[rows], out_hbm.at[y, to], sems.at[y, k + 1]))
    for copy in copies:
        copy.start()
    for copy in copies:
        copy.wait()


def last_kernel(scores_ref, out_ref):
    out_ref[...] = jnp.concatenate([scores_ref[k] for k in range(4)], axis=1)


def weight_block(ref, lead, row):
    return jnp.concatenate([ref[lead, row + 128 * g : row + 128 * g + 128, :] for g in range(3)], axis=1)


def near_kernel(
    at_ref, own_hbm, beside_hbm, gain_ref, own_taps, got_taps, near_ref, unembed_ref,
    gained_ref, scale_ref, out_ref, terms_ref, pieces_ref, tokens, taps, sems,
):
    core, start = at_ref[2], at_ref[3] * 2048
    gain = gain_ref[...]
    copies = []
    for part, ref in enumerate((own_hbm, beside_hbm)):
        for i in range(4):
            rows = pl.ds(i * 64, 64)
            copies.append(pltpu.make_async_copy(ref.at[rows], tokens.at[part, rows], sems.at[part, i]))
    copies.append(pltpu.make_async_copy(own_taps, taps.at[0], sems.at[2, 0]))
    copies.append(pltpu.make_async_copy(got_taps, taps.at[1], sems.at[2, 1]))
    for copy in copies:
        copy.start()

    blocks = []
    for plane in range(2):
        for y in range(4):
            block = near_ref[y, 1536 + plane * 32 : 1568 + plane * 32, :].astype(F32)
            blocks.append(jnp.concatenate([block[v * 8 : v * 8 + 8] for v in range(4)], axis=1))
    terms = mm(jnp.concatenate(blocks, axis=0).astype(BF16), unembed_ref[...])
    for j in range(8):
        parts = [terms[j * 8 : j * 8 + 8, v * 128 : v * 128 + 128] for v in range(4)]
        terms_ref[j] = jnp.concatenate(parts, axis=0).astype(BF16)

    for part in range(2):
        for i in range(4):
            copies[part * 4 + i].wait()
            for half in range(2):
                rows = slice(i * 64 + half * 32, i * 64 + half * 32 + 32)
                block = tokens[part, rows, :]
                stream = block.astype(F32)
                mean = jnp.mean(stream * stream, axis=1, keepdims=True)
                scale_ref[part, rows, :] = jnp.broadcast_to(lax.rsqrt(mean + NORM_EPS), (32, 128))
                gained_ref[part, rows, :] = block * gain
        total = jnp.zeros((256, 384), F32)
        for y in range(4):
            for x in (0, 2):
                left = gained_ref[part, :, pl.ds(pl.multiple_of(start + (y * 4 + x) * 128, 128), 256)]
                right = [weight_block(near_ref, y, x * 384), weight_block(near_ref, y, x * 384 + 384)]
                total += mm(left, jnp.concatenate(right, axis=0))
        out_ref[part] = total
    for part in range(2):
        copies[8 + part].wait()
        for plane in range(2):
            place = core if part == 0 else 1 - core
            put_pieces(pieces_ref, plane * 32, place, taps[part, plane].astype(F32))


def put_pieces(ref, row, place, block):
    first, second = block[:128].T, block[128:].T
    for p in range(16):
        b = p * 8
        rows = jnp.concatenate([first[b : b + 8], second[b : b + 8]], axis=0).astype(BF16)
        ref[p, pl.ds(pl.multiple_of(row + place * 16, 16), 16), :] = rows


def proj_kernel(at_ref, gained_ref, scale_ref, near_ref, pieces_ref, f0, f1, f2, f3, sig_ref, gate_ref, fars, sems):
    y_at, x_at, core = at_ref[0], at_ref[1], at_ref[2]
    start = 2048 - at_ref[3] * 2048
    copies = [pltpu.make_async_copy(f, fars.at[k], sems.at[k]) for k, f in enumerate((f0, f1, f2, f3))]
    for copy in copies:
        copy.start()
    for part in range(2):
        total = near_ref[part]
        for step in range(4):
            if part == 0:
                copies[step].wait()
            x = lax.rem(x_at + 4 - step, 4)
            for k in (0, 2):
                starts = [start + (lax.rem(y_at + 4 - j, 4) * 4 + x) * 128 for j in (k, k + 1)]
                left = [gained_ref[part, :, pl.ds(pl.multiple_of(at, 128), 128)] for at in starts]
                right = [weight_block(fars.at[step], k, 0), weight_block(fars.at[step], k + 1, 0)]
                total += mm(jnp.concatenate(left, axis=1), jnp.concatenate(right, axis=0))
        scale = scale_ref[part]
        proj = (total * jnp.concatenate([scale, scale, scale], axis=1)).astype(BF16).astype(F32)
        place = core if part == 0 else 1 - core
        put_pieces(sig_ref, 0, place, proj[:, 128:256] * proj[:, 256:])
        gate_ref[place, 0] = proj[:128, :128].T.astype(BF16)
        gate_ref[place, 1] = proj[128:, :128].T.astype(BF16)
    for p in range(16):
        sig_ref[p, 32:, :] = pieces_ref[p]


def mix_kernel(core_ref, got_ref, keep_ref, other_ref, base_ref, out_ref):
    core = core_ref[0]
    keep, other = keep_ref[...].astype(F32), other_ref[...].astype(F32)
    conv = got_ref[:, :16, :].astype(F32)
    for rb in range(2):
        total = base_ref[rb * 128 : rb * 128 + 128, :]
        for c in range(2):
            cube = jnp.concatenate([conv[b * 2 + c, rb * 8 : rb * 8 + 8] for b in range(16)], axis=0)
            gate = jnp.where(core == c, keep[rb], other[rb])
            mixed = (gate * cube).T.astype(BF16)
            weights = []
            for b in range(16):
                x, holder, y = (c * 16 + b) // 8, b % 8 // 4, b % 4
                piece = got_ref[(y * 4 + x) * 2 + holder, 16:, :].astype(F32)
                weights.append(jnp.concatenate([piece[v * 8 : v * 8 + 8] for v in range(4)], axis=1))
            total += mm(mixed, jnp.concatenate(weights, axis=0).astype(BF16))
        out_ref[rb * 128 : rb * 128 + 128, :] = total.astype(BF16)


def call(kernel, outs, specs, scratch, flops, args, mib=8, out_specs=None):
    if out_specs is None:
        out_specs = jax.tree.map(lambda _: pl.BlockSpec(memory_space=pltpu.VMEM), outs)
    return pl.pallas_call(
        kernel,
        out_shape=outs,
        in_specs=specs,
        out_specs=out_specs,
        scratch_shapes=scratch,
        compiler_params=pltpu.CompilerParams(vmem_limit_bytes=mib * 2**20),
        cost_estimate=pl.CostEstimate(flops=flops, bytes_accessed=4 * 2**20, transcendentals=0),
    )(*args)


def shape(dims, dtype):
    return jax.ShapeDtypeStruct(dims, dtype)


def by_position(own, other, place):
    return jnp.where(place == 0, jnp.stack([own, other]), jnp.stack([other, own]))


def spectra(z, got):
    return call(
        spectra_kernel,
        (shape((1024, 256), F32), shape((1024, 256), F32), shape((1024, 256), F32)),
        [SCALARS] + whole(3),
        [pltpu.VMEM((512, 128), F32)],
        4 * 10**8,
        (z, got, jnp.asarray(MATRICES, BF16), jnp.asarray(TWIDDLES, F32)),
        mib=16,
    )


def convolve(z, signal, low, every, before):
    return call(
        conv_kernel,
        shape((32, 16, 128), BF16),
        [SCALARS] + whole(6),
        [pltpu.VMEM((512, 128), F32)],
        6 * 10**8,
        (z, signal, low, every, before, jnp.asarray(MATRICES, BF16), jnp.asarray(TWIDDLES, F32)),
        mib=16,
    )


def per_device(tokens_in, pre_gain, w_in, w_out, long_filter, w_unembed, target_ids, score_mask):
    ctx, tp = lax.axis_index("ctx"), lax.axis_index("tp")
    core, z = ctx % 2, ctx // 32
    z_at = z.reshape(1).astype(jnp.int32)

    core_at = core.reshape(1).astype(jnp.int32)
    w_in = w_in.transpose(1, 0, 2)
    keep = lax.dynamic_slice_in_dim(w_in, core * 128, 128, 2)
    rows = w_out.reshape(4, 8, 4, 128).transpose(0, 2, 1, 3).reshape(128, 128)
    first = call(
        first_kernel,
        shape((1024, 128), BF16),
        [SCALARS] + whole(4),
        [],
        10**5,
        (core_at, keep, lax.ppermute(w_in, "ctx", PERM_CORE), rows, long_filter),
    )
    near = call(copies_kernel, shape((4, 384, 128), BF16), whole(1), [], 10**10, (first,))
    near, tokens = lax.optimization_barrier((near, tokens_in))
    beside = lax.ppermute(tokens, "ctx", PERM_CORE)
    near = lax.all_to_all(near, "ctx", 0, 0, axis_index_groups=GROUPS_X, tiled=True)
    far = lax.ppermute(first, "ctx", PERM_Z)

    along = far[:384]
    along = jnp.stack([along] + [lax.ppermute(along, "ctx", PERM_Y[k]) for k in (1, 2, 3)])
    near, along, far = lax.optimization_barrier((near, along, far))

    near = call(
        spread_kernel,
        shape((4, 1600, 128), BF16),
        [SCALARS] + whole(3),
        [pltpu.SemaphoreType.DMA((4, 3))],
        10**5,
        (z_at, near.reshape(1536, 128), first, far),
        out_specs=IN_HBM,
    )
    near = lax.all_to_all(near, "ctx", 0, 0, axis_index_groups=GROUPS_Y, tiled=True)
    taps = far[512:].reshape(2, 256, 128)
    far = along
    fars = [far] + [lax.ppermute(far, "ctx", PERM_X[k]) for k in (1, 2, 3)]
    taps = jnp.stack([first[512:].reshape(2, 256, 128), taps])
    taps_got = lax.ppermute(lax.dynamic_index_in_dim(taps, 1 - core, 1, False), "ctx", PERM_CORE)
    taps = lax.dynamic_index_in_dim(taps, core, 1, False)

    at = jnp.stack([(ctx // 8) % 4, (ctx // 2) % 4, core, z]).astype(jnp.int32)
    gained, scale, sums, terms, pieces = call(
        near_kernel,
        (
            shape((2, 256, 4096), BF16),
            shape((2, 256, 128), F32),
            shape((2, 256, 384), F32),
            shape((8, 32, 128), BF16),
            shape((16, 64, 128), BF16),
        ),
        [SCALARS, IN_HBM, IN_HBM] + whole(1) + [IN_HBM, IN_HBM] + whole(2),
        [pltpu.VMEM((2, 256, 4096), BF16), pltpu.VMEM((2, 2, 256, 128), BF16), pltpu.SemaphoreType.DMA((3, 4))],
        8 * 10**8,
        (at, tokens_in, beside, pre_gain.reshape(1, 4096), taps, taps_got, near, w_unembed),
        mib=12,
    )
    signal, gate = call(
        proj_kernel,
        (shape((16, 96, 128), BF16), shape((2, 2, 128, 128), BF16)),
        [SCALARS] + whole(4) + [IN_HBM] * 4,
        [pltpu.VMEM((4, 4, 384, 128), BF16), pltpu.SemaphoreType.DMA((4,))],
        8 * 10**8,
        (at, gained, scale, sums, pieces, *fars),
    )
    got = lax.all_to_all(signal, "ctx", 0, 0, axis_index_groups=GROUPS_CORE, tiled=True)
    before = lax.ppermute(got[:, :32].reshape(512, 128), "ctx", PERM_Z_UP)
    terms, _ = lax.optimization_barrier((terms, got))
    terms = lax.all_to_all(terms, "tp", 0, 0, tiled=True)
    gate_keep = lax.dynamic_index_in_dim(gate, core, 0, False)
    gate_got = lax.ppermute(lax.dynamic_index_in_dim(gate, 1 - core, 0, False), "ctx", PERM_CORE)

    conv = convolve(z_at, *spectra(z_at, got), before)
    conv = call(pack_kernel, shape((32, 48, 128), BF16), whole(2), [], 10**5, (conv, terms))
    conv = lax.all_to_all(conv, "ctx", 0, 0, axis_index_groups=GROUPS_PLANE, tiled=True)

    width = w_unembed.shape[0]
    base = mm(lax.dynamic_slice_in_dim(tokens_in, tp * width, width, 1), w_unembed)
    logits = call(
        mix_kernel,
        shape((256, 512), BF16),
        [SCALARS] + whole(4),
        [],
        10**8,
        (core_at, conv, gate_keep, gate_got, base),
    )
    logits = lax.all_to_all(logits.reshape(4, 64, 512), "tp", 0, 0, axis_index_groups=GROUPS_TP, tiled=True)
    logits = jnp.sum(logits.astype(F32), axis=0).astype(BF16)
    far = lax.ppermute(logits, "tp", [(i, i ^ 4) for i in range(8)])
    logits = logits.astype(F32) + far.astype(F32)

    row_top = jnp.max(logits, axis=1, keepdims=True)
    log_total = row_top[:, 0] + jnp.log(jnp.sum(jnp.exp(logits - row_top), axis=1))
    ids = lax.dynamic_slice_in_dim(target_ids, (tp % 4) * 64, 64, 0)
    mask = lax.dynamic_slice_in_dim(score_mask, (tp % 4) * 64, 64, 0)
    vocab_index = lax.broadcasted_iota(jnp.int32, (64, 512), 1)
    picked = jnp.sum(jnp.where(vocab_index == ids[:, None], logits, 0.0), axis=1)
    scores = (picked - log_total) * mask.astype(F32)
    scores = jnp.broadcast_to(scores[None, None, :], (4, 1, 64))
    scores = lax.all_to_all(scores, "tp", 0, 0, axis_index_groups=GROUPS_TP, tiled=True)
    return call(last_kernel, shape((1, 256), F32), whole(1), [], 10**3, (scores,)).reshape(256)


def solution(mesh):
    return jax.shard_map(
        per_device,
        mesh=mesh,
        in_specs=(
            P("ctx", None),
            P(),
            P("ctx", None, "tp"),
            P("ctx", "tp"),
            P("ctx", "tp"),
            P("tp", None),
            P("ctx"),
            P("ctx"),
        ),
        out_specs=P("ctx"),
        check_vma=False,
    )
```

```python
import math

import jax
import jax.numpy as jnp
import numpy as np
from jax import lax
from jax.experimental import pallas as pl
from jax.experimental.pallas import tpu as pltpu
from jax.sharding import PartitionSpec as P

NORM_EPS = 1e-05
F32 = jnp.float32
BF16 = jnp.bfloat16

COORDS = [(z, y, x, c) for z in range(2) for y in range(4) for x in range(4) for c in range(2)]


def ctx_id(z, y, x, c):
    return ((z * 4 + y) * 4 + x) * 2 + c


def ctx_perm(move):
    return [(ctx_id(*at), ctx_id(*move(*at))) for at in COORDS]


PERM_CORE = ctx_perm(lambda z, y, x, c: (z, y, x, 1 - c))
PERM_Z = ctx_perm(lambda z, y, x, c: (1 - z, y, x, c))
PERM_Z_UP = [(i, i + 32) for i in range(32)]
PERM_X = [ctx_perm(lambda z, y, x, c, k=k: (z, y, (x + k) % 4, c)) for k in range(4)]
PERM_Y = [ctx_perm(lambda z, y, x, c, k=k: (z, (y + k) % 4, x, c)) for k in range(4)]
GROUPS_X = [[ctx_id(z, y, x, c) for x in range(4)] for z in range(2) for y in range(4) for c in range(2)]
GROUPS_Y = [[ctx_id(z, y, x, c) for y in range(4)] for z in range(2) for x in range(4) for c in range(2)]
GROUPS_PLANE = [
    [ctx_id(z, y, x, c) for y in range(4) for x in range(4) for c in range(2)] for z in range(2)
]
GROUPS_CORE = [
    [ctx_id(z, y, x, c) for y in range(4) for x in range(4)] for z in range(2) for c in range(2)
]
GROUPS_TP = [[0, 1, 2, 3], [4, 5, 6, 7]]


def tables():
    index = np.arange(128)
    inner = 2.0 * math.pi * (np.outer(index, index) % 128) / 128
    outer = 2.0 * math.pi * np.outer(index, index) / 16384
    cos, sin = np.cos(inner), np.sin(inner)
    first = np.concatenate([cos[:, :64], -sin[:, :64]], axis=0)
    second = np.block([[cos, -sin], [sin, cos]])
    back = np.block([[cos, sin], [-sin, cos]])
    last = np.concatenate([cos[:64], -sin[:64]], axis=1) / 16384.0
    return (first, second, back, last, np.cos(outer), np.sin(outer))


FIRST, SECOND, BACK, LAST, COS_TW, SIN_TW = tables()
MATRICES = np.concatenate([np.pad(FIRST, ((0, 0), (0, 192))), SECOND, BACK, LAST])
TWIDDLES = np.concatenate([COS_TW, SIN_TW], axis=1)


def mm(left, right):
    return jnp.dot(left, right, preferred_element_type=F32)


def whole(count):
    return [pl.BlockSpec(memory_space=pltpu.VMEM)] * count


SCALARS = pl.BlockSpec(memory_space=pltpu.SMEM)
IN_HBM = pl.BlockSpec(memory_space=pltpu.HBM)


def spectrum(scratch, matrices, twiddles):
    cos_tw, sin_tw = twiddles[:, :128], twiddles[:, 128:]
    cube = jnp.concatenate([scratch[pl.ds(c, 64, stride=8), :] for c in range(8)], axis=1)
    step = mm(matrices[:256, :64], cube.astype(BF16))
    parts = []
    for c in range(8):
        real, imag = step[:128, c * 128 : c * 128 + 128], step[128:, c * 128 : c * 128 + 128]
        parts.append(
            jnp.concatenate(
                [(real * cos_tw + imag * sin_tw).astype(BF16), (imag * cos_tw - real * sin_tw).astype(BF16)],
                axis=1,
            )
        )
    return mm(jnp.concatenate(parts, axis=0), matrices[256:512, :])


def rows_of(scratch, ref, at):
    for p in range(16):
        scratch[p * 32 : p * 32 + 32] = ref[p, at : at + 32].astype(F32)


def spectra_kernel(got_ref, matrices, twiddles, signal_ref, filter_ref, scratch):
    rows_of(scratch, got_ref, 0)
    signal_ref[...] = spectrum(scratch, matrices, twiddles)
    rows_of(scratch, got_ref, 32)
    filter_ref[...] = spectrum(scratch, matrices, twiddles)


def conv_kernel(z_ref, signal_ref, filter_ref, before_ref, matrices, twiddles, out_ref, scratch):
    upper = z_ref[0] == 1
    cos_tw, sin_tw = twiddles[:, :128], twiddles[:, 128:]
    own, high = signal_ref[...], filter_ref[...]
    rows_of(scratch, before_ref, 0)
    old = jnp.where(upper, spectrum(scratch, matrices, twiddles), 0.0)
    rows_of(scratch, before_ref, 32)
    low = jnp.where(upper, spectrum(scratch, matrices, twiddles), high)
    odd = lax.broadcasted_iota(jnp.int32, (1024, 256), 0) & 1
    every = jnp.where(odd == 1, -low, low) + high
    own_r, own_i, old_r, old_i = own[:, :128], own[:, 128:], old[:, :128], old[:, 128:]
    low_r, low_i, all_r, all_i = low[:, :128], low[:, 128:], every[:, :128], every[:, 128:]
    real = own_r * low_r - own_i * low_i + old_r * all_r - old_i * all_i
    imag = own_r * low_i + own_i * low_r + old_r * all_i + old_i * all_r
    half = mm(jnp.concatenate([real.astype(BF16), imag.astype(BF16)], axis=1), matrices[512:768, :])
    parts = []
    for c in range(8):
        real, imag = half[c * 128 : c * 128 + 128, :128], half[c * 128 : c * 128 + 128, 128:]
        parts.append(
            jnp.concatenate(
                [(real * cos_tw - imag * sin_tw).astype(BF16), (imag * cos_tw + real * sin_tw).astype(BF16)],
                axis=0,
            )
        )
    result = mm(matrices[768:, :], jnp.concatenate(parts, axis=1))
    for c in range(8):
        scratch[pl.ds(c, 64, stride=8), :] = result[:, c * 128 : c * 128 + 128]
    for d in range(32):
        out_ref[d] = scratch[d * 16 : d * 16 + 16].astype(BF16)


def pack_kernel(conv_ref, terms_ref, out_ref):
    piece = sum(terms_ref[j].astype(F32) for j in range(8)).astype(BF16)
    for d in range(32):
        out_ref[d, :16] = conv_ref[d]
        out_ref[d, 16:] = piece


def first_kernel(core_ref, own_ref, got_ref, rows_ref, out_ref):
    core = core_ref[0]
    half = pl.ds(pl.multiple_of(core * 128, 128), 128)
    for g in range(3):
        own, got = own_ref[g], got_ref[g, :, half]
        out_ref[g * 128 : g * 128 + 64] = jnp.where(core == 0, own, got)
        out_ref[g * 128 + 64 : g * 128 + 128] = jnp.where(core == 0, got, own)
    out_ref[384:] = rows_ref[...]


def copies_kernel(first_ref, out_ref):
    for k in range(4):
        out_ref[k] = first_ref[:384]


def spread_kernel(z_ref, near_ref, first_ref, far_ref, out_hbm, sems):
    z = z_ref[0]
    copies = []
    for y in range(4):
        copies.append(pltpu.make_async_copy(near_ref, out_hbm.at[y, pl.ds(0, 1536)], sems.at[y, 0]))
        rows = pl.ds(384 + y * 32, 32)
        for k, (ref, place) in enumerate(((first_ref, z), (far_ref, 1 - z))):
            to = pl.ds(pl.multiple_of(1536 + place * 32, 32), 32)
            copies.append(pltpu.make_async_copy(ref.at[rows], out_hbm.at[y, to], sems.at[y, k + 1]))
    for copy in copies:
        copy.start()
    for copy in copies:
        copy.wait()


def last_kernel(scores_ref, out_ref):
    out_ref[...] = jnp.concatenate([scores_ref[k] for k in range(4)], axis=1)


def weight_block(ref, lead, row):
    return jnp.concatenate([ref[lead, row + 128 * g : row + 128 * g + 128, :] for g in range(3)], axis=1)


def near_kernel(
    at_ref, own_hbm, beside_hbm, gain_ref, own_taps, got_taps, near_ref, unembed_ref,
    gained_ref, scale_ref, out_ref, terms_ref, pieces_ref, tokens, taps, sems,
):
    core, start = at_ref[2], at_ref[3] * 2048
    gain = gain_ref[...]
    copies = []
    for part, ref in enumerate((own_hbm, beside_hbm)):
        for i in range(4):
            rows = pl.ds(i * 64, 64)
            copies.append(pltpu.make_async_copy(ref.at[rows], tokens.at[part, rows], sems.at[part, i]))
    copies.append(pltpu.make_async_copy(own_taps, taps.at[0], sems.at[2, 0]))
    copies.append(pltpu.make_async_copy(got_taps, taps.at[1], sems.at[2, 1]))
    for copy in copies:
        copy.start()

    blocks = []
    for plane in range(2):
        for y in range(4):
            block = near_ref[y, 1536 + plane * 32 : 1568 + plane * 32, :].astype(F32)
            blocks.append(jnp.concatenate([block[v * 8 : v * 8 + 8] for v in range(4)], axis=1))
    terms = mm(jnp.concatenate(blocks, axis=0).astype(BF16), unembed_ref[...])
    for j in range(8):
        parts = [terms[j * 8 : j * 8 + 8, v * 128 : v * 128 + 128] for v in range(4)]
        terms_ref[j] = jnp.concatenate(parts, axis=0).astype(BF16)

    for part in range(2):
        for i in range(4):
            copies[part * 4 + i].wait()
            for half in range(2):
                rows = slice(i * 64 + half * 32, i * 64 + half * 32 + 32)
                block = tokens[part, rows, :]
                stream = block.astype(F32)
                mean = jnp.mean(stream * stream, axis=1, keepdims=True)
                scale_ref[part, rows, :] = jnp.broadcast_to(lax.rsqrt(mean + NORM_EPS), (32, 128))
                gained_ref[part, rows, :] = block * gain
        total = jnp.zeros((256, 384), F32)
        for y in range(4):
            for x in (0, 2):
                left = gained_ref[part, :, pl.ds(pl.multiple_of(start + (y * 4 + x) * 128, 128), 256)]
                right = [weight_block(near_ref, y, x * 384), weight_block(near_ref, y, x * 384 + 384)]
                total += mm(left, jnp.concatenate(right, axis=0))
        out_ref[part] = total
    half = pl.ds(pl.multiple_of(core * 128, 128), 128)
    for part in range(2):
        copies[8 + part].wait()
        put_pieces(pieces_ref, 0, core if part == 0 else 1 - core, taps[part, :, half].astype(F32))


def put_pieces(ref, row, place, block):
    first, second = block[:128].T, block[128:].T
    for p in range(16):
        b = p * 8
        rows = jnp.concatenate([first[b : b + 8], second[b : b + 8]], axis=0).astype(BF16)
        ref[p, pl.ds(pl.multiple_of(row + place * 16, 16), 16), :] = rows


def proj_kernel(at_ref, gained_ref, scale_ref, near_ref, pieces_ref, f0, f1, f2, f3, sig_ref, gate_ref, fars, sems):
    y_at, x_at, core = at_ref[0], at_ref[1], at_ref[2]
    start = 2048 - at_ref[3] * 2048
    copies = [pltpu.make_async_copy(f, fars.at[k], sems.at[k]) for k, f in enumerate((f0, f1, f2, f3))]
    for copy in copies:
        copy.start()
    for part in range(2):
        total = near_ref[part]
        for step in range(4):
            if part == 0:
                copies[step].wait()
            x = lax.rem(x_at + 4 - step, 4)
            for k in (0, 2):
                starts = [start + (lax.rem(y_at + 4 - j, 4) * 4 + x) * 128 for j in (k, k + 1)]
                left = [gained_ref[part, :, pl.ds(pl.multiple_of(at, 128), 128)] for at in starts]
                right = [weight_block(fars.at[step], k, 0), weight_block(fars.at[step], k + 1, 0)]
                total += mm(jnp.concatenate(left, axis=1), jnp.concatenate(right, axis=0))
        scale = scale_ref[part]
        proj = (total * jnp.concatenate([scale, scale, scale], axis=1)).astype(BF16).astype(F32)
        place = core if part == 0 else 1 - core
        put_pieces(sig_ref, 0, place, proj[:, 128:256] * proj[:, 256:])
        gate_ref[place, 0] = proj[:128, :128].T.astype(BF16)
        gate_ref[place, 1] = proj[128:, :128].T.astype(BF16)
    for p in range(16):
        sig_ref[p, 32:, :] = pieces_ref[p]


def mix_kernel(core_ref, got_ref, keep_ref, other_ref, base_ref, out_ref):
    core = core_ref[0]
    keep, other = keep_ref[...].astype(F32), other_ref[...].astype(F32)
    conv = got_ref[:, :16, :].astype(F32)
    for rb in range(2):
        total = base_ref[rb * 128 : rb * 128 + 128, :]
        for c in range(2):
            cube = jnp.concatenate([conv[b * 2 + c, rb * 8 : rb * 8 + 8] for b in range(16)], axis=0)
            gate = jnp.where(core == c, keep[rb], other[rb])
            mixed = (gate * cube).T.astype(BF16)
            weights = []
            for b in range(16):
                x, holder, y = (c * 16 + b) // 8, b % 8 // 4, b % 4
                piece = got_ref[(y * 4 + x) * 2 + holder, 16:, :].astype(F32)
                weights.append(jnp.concatenate([piece[v * 8 : v * 8 + 8] for v in range(4)], axis=1))
            total += mm(mixed, jnp.concatenate(weights, axis=0).astype(BF16))
        out_ref[rb * 128 : rb * 128 + 128, :] = total.astype(BF16)


def call(kernel, outs, specs, scratch, flops, args, mib=8, out_specs=None):
    if out_specs is None:
        out_specs = jax.tree.map(lambda _: pl.BlockSpec(memory_space=pltpu.VMEM), outs)
    return pl.pallas_call(
        kernel,
        out_shape=outs,
        in_specs=specs,
        out_specs=out_specs,
        scratch_shapes=scratch,
        compiler_params=pltpu.CompilerParams(vmem_limit_bytes=mib * 2**20),
        cost_estimate=pl.CostEstimate(flops=flops, bytes_accessed=4 * 2**20, transcendentals=0),
    )(*args)


def shape(dims, dtype):
    return jax.ShapeDtypeStruct(dims, dtype)


def by_position(own, other, place):
    return jnp.where(place == 0, jnp.stack([own, other]), jnp.stack([other, own]))


def spectra(got):
    return call(
        spectra_kernel,
        (shape((1024, 256), F32), shape((1024, 256), F32)),
        whole(3),
        [pltpu.VMEM((512, 128), F32)],
        4 * 10**8,
        (got, jnp.asarray(MATRICES, BF16), jnp.asarray(TWIDDLES, F32)),
    )


def convolve(z, signal, taps, before):
    return call(
        conv_kernel,
        shape((32, 16, 128), BF16),
        [SCALARS] + whole(5),
        [pltpu.VMEM((512, 128), F32)],
        6 * 10**8,
        (z, signal, taps, before, jnp.asarray(MATRICES, BF16), jnp.asarray(TWIDDLES, F32)),
        mib=16,
    )


def per_device(tokens_in, pre_gain, w_in, w_out, long_filter, w_unembed, target_ids, score_mask):
    ctx, tp = lax.axis_index("ctx"), lax.axis_index("tp")
    core, z = ctx % 2, ctx // 32
    z_at = z.reshape(1).astype(jnp.int32)

    core_at = core.reshape(1).astype(jnp.int32)
    w_in = w_in.transpose(1, 0, 2)
    keep = lax.dynamic_slice_in_dim(w_in, core * 128, 128, 2)
    rows = w_out.reshape(4, 8, 4, 128).transpose(0, 2, 1, 3).reshape(128, 128)
    first = call(
        first_kernel,
        shape((512, 128), BF16),
        [SCALARS] + whole(3),
        [],
        10**5,
        (core_at, keep, lax.ppermute(w_in, "ctx", PERM_CORE), rows),
    )
    near = call(copies_kernel, shape((4, 384, 128), BF16), whole(1), [], 10**5, (first,))
    beside = lax.ppermute(tokens_in, "ctx", PERM_CORE)
    near = lax.all_to_all(near, "ctx", 0, 0, axis_index_groups=GROUPS_X, tiled=True)
    far = lax.ppermute(first, "ctx", PERM_Z)

    along = far[:384]
    along = jnp.stack([along] + [lax.ppermute(along, "ctx", PERM_Y[k]) for k in (1, 2, 3)])
    near, along, far, taps = lax.optimization_barrier((near, along, far, long_filter))

    near = call(
        spread_kernel,
        shape((4, 1600, 128), BF16),
        [SCALARS] + whole(3),
        [pltpu.SemaphoreType.DMA((4, 3))],
        10**5,
        (z_at, near.reshape(1536, 128), first, far),
        out_specs=IN_HBM,
    )
    near = lax.all_to_all(near, "ctx", 0, 0, axis_index_groups=GROUPS_Y, tiled=True)
    far = along
    fars = [far] + [lax.ppermute(far, "ctx", PERM_X[k]) for k in (1, 2, 3)]
    taps_got = lax.ppermute(taps, "ctx", PERM_CORE)

    at = jnp.stack([(ctx // 8) % 4, (ctx // 2) % 4, core, z]).astype(jnp.int32)
    gained, scale, sums, terms, pieces = call(
        near_kernel,
        (
            shape((2, 256, 4096), BF16),
            shape((2, 256, 128), F32),
            shape((2, 256, 384), F32),
            shape((8, 32, 128), BF16),
            shape((16, 32, 128), BF16),
        ),
        [SCALARS, IN_HBM, IN_HBM] + whole(1) + [IN_HBM, IN_HBM] + whole(2),
        [pltpu.VMEM((2, 256, 4096), BF16), pltpu.VMEM((2, 256, 256), BF16), pltpu.SemaphoreType.DMA((3, 4))],
        8 * 10**8,
        (at, tokens_in, beside, pre_gain.reshape(1, 4096), taps, taps_got, near, w_unembed),
        mib=12,
    )
    signal, gate = call(
        proj_kernel,
        (shape((16, 64, 128), BF16), shape((2, 2, 128, 128), BF16)),
        [SCALARS] + whole(4) + [IN_HBM] * 4,
        [pltpu.VMEM((4, 4, 384, 128), BF16), pltpu.SemaphoreType.DMA((4,))],
        8 * 10**8,
        (at, gained, scale, sums, pieces, *fars),
    )
    got = lax.all_to_all(signal, "ctx", 0, 0, axis_index_groups=GROUPS_CORE, tiled=True)
    before = lax.ppermute(got, "ctx", PERM_Z_UP)
    terms, _ = lax.optimization_barrier((terms, got))
    terms = lax.all_to_all(terms, "tp", 0, 0, tiled=True)
    gate_keep = lax.dynamic_index_in_dim(gate, core, 0, False)
    gate_got = lax.ppermute(lax.dynamic_index_in_dim(gate, 1 - core, 0, False), "ctx", PERM_CORE)

    conv = convolve(z_at, *spectra(got), before)
    conv = call(pack_kernel, shape((32, 48, 128), BF16), whole(2), [], 10**5, (conv, terms))
    conv = lax.all_to_all(conv, "ctx", 0, 0, axis_index_groups=GROUPS_PLANE, tiled=True)

    width = w_unembed.shape[0]
    base = mm(lax.dynamic_slice_in_dim(tokens_in, tp * width, width, 1), w_unembed)
    logits = call(
        mix_kernel,
        shape((256, 512), BF16),
        [SCALARS] + whole(4),
        [],
        10**8,
        (core_at, conv, gate_keep, gate_got, base),
    )
    logits = lax.all_to_all(logits.reshape(4, 64, 512), "tp", 0, 0, axis_index_groups=GROUPS_TP, tiled=True)
    logits = jnp.sum(logits.astype(F32), axis=0).astype(BF16)
    far = lax.ppermute(logits, "tp", [(i, i ^ 4) for i in range(8)])
    logits = logits.astype(F32) + far.astype(F32)

    row_top = jnp.max(logits, axis=1, keepdims=True)
    log_total = row_top[:, 0] + jnp.log(jnp.sum(jnp.exp(logits - row_top), axis=1))
    ids = lax.dynamic_slice_in_dim(target_ids, (tp % 4) * 64, 64, 0)
    mask = lax.dynamic_slice_in_dim(score_mask, (tp % 4) * 64, 64, 0)
    vocab_index = lax.broadcasted_iota(jnp.int32, (64, 512), 1)
    picked = jnp.sum(jnp.where(vocab_index == ids[:, None], logits, 0.0), axis=1)
    scores = (picked - log_total) * mask.astype(F32)
    scores = jnp.broadcast_to(scores[None, None, :], (4, 1, 64))
    scores = lax.all_to_all(scores, "tp", 0, 0, axis_index_groups=GROUPS_TP, tiled=True)
    return call(last_kernel, shape((1, 256), F32), whole(1), [], 10**3, (scores,)).reshape(256)


def solution(mesh):
    return jax.shard_map(
        per_device,
        mesh=mesh,
        in_specs=(
            P("ctx", None),
            P(),
            P("ctx", None, "tp"),
            P("ctx", "tp"),
            P("ctx", "tp"),
            P("tp", None),
            P("ctx"),
            P("ctx"),
        ),
        out_specs=P("ctx"),
        check_vma=False,
    )
```

```python
import math

import jax
import jax.numpy as jnp
import numpy as np
from jax import lax
from jax.experimental import pallas as pl
from jax.experimental.pallas import tpu as pltpu
from jax.sharding import PartitionSpec as P

NORM_EPS = 1e-05
F32 = jnp.float32
BF16 = jnp.bfloat16

COORDS = [(z, y, x, c) for z in range(2) for y in range(4) for x in range(4) for c in range(2)]


def ctx_id(z, y, x, c):
    return ((z * 4 + y) * 4 + x) * 2 + c


def ctx_perm(move):
    return [(ctx_id(*at), ctx_id(*move(*at))) for at in COORDS]


PERM_CORE = ctx_perm(lambda z, y, x, c: (z, y, x, 1 - c))
PERM_Z = ctx_perm(lambda z, y, x, c: (1 - z, y, x, c))
PERM_Z_UP = [(i, i + 32) for i in range(32)]
PERM_X = [ctx_perm(lambda z, y, x, c, k=k: (z, y, (x + k) % 4, c)) for k in range(4)]
PERM_Y = [ctx_perm(lambda z, y, x, c, k=k: (z, (y + k) % 4, x, c)) for k in range(4)]
GROUPS_X = [[ctx_id(z, y, x, c) for x in range(4)] for z in range(2) for y in range(4) for c in range(2)]
GROUPS_Y = [[ctx_id(z, y, x, c) for y in range(4)] for z in range(2) for x in range(4) for c in range(2)]
GROUPS_PLANE = [
    [ctx_id(z, y, x, c) for y in range(4) for x in range(4) for c in range(2)] for z in range(2)
]
GROUPS_CORE = [
    [ctx_id(z, y, x, c) for y in range(4) for x in range(4)] for z in range(2) for c in range(2)
]
GROUPS_TP = [[0, 1, 2, 3], [4, 5, 6, 7]]


def tables():
    index = np.arange(128)
    inner = 2.0 * math.pi * (np.outer(index, index) % 128) / 128
    outer = 2.0 * math.pi * np.outer(index, index) / 16384
    cos, sin = np.cos(inner), np.sin(inner)
    first = np.concatenate([cos[:, :64], -sin[:, :64]], axis=0)
    second = np.block([[cos, -sin], [sin, cos]])
    back = np.block([[cos, sin], [-sin, cos]])
    last = np.concatenate([cos[:64], -sin[:64]], axis=1) / 16384.0
    return (first, second, back, last, np.cos(outer), np.sin(outer))


FIRST, SECOND, BACK, LAST, COS_TW, SIN_TW = tables()
MATRICES = np.concatenate([np.pad(FIRST, ((0, 0), (0, 192))), SECOND, BACK, LAST])
TWIDDLES = np.concatenate([COS_TW, SIN_TW], axis=1)


def mm(left, right):
    return jnp.dot(left, right, preferred_element_type=F32)


def whole(count):
    return [pl.BlockSpec(memory_space=pltpu.VMEM)] * count


SCALARS = pl.BlockSpec(memory_space=pltpu.SMEM)
IN_HBM = pl.BlockSpec(memory_space=pltpu.HBM)


def spectrum(scratch, matrices, twiddles):
    cos_tw, sin_tw = twiddles[:, :128], twiddles[:, 128:]
    cube = jnp.concatenate([scratch[pl.ds(c, 64, stride=8), :] for c in range(8)], axis=1)
    step = mm(matrices[:256, :64], cube.astype(BF16))
    parts = []
    for c in range(8):
        real, imag = step[:128, c * 128 : c * 128 + 128], step[128:, c * 128 : c * 128 + 128]
        parts.append(
            jnp.concatenate(
                [(real * cos_tw + imag * sin_tw).astype(BF16), (imag * cos_tw - real * sin_tw).astype(BF16)],
                axis=1,
            )
        )
    return mm(jnp.concatenate(parts, axis=0), matrices[256:512, :])


def rows_of(scratch, ref, at):
    for p in range(16):
        scratch[p * 32 : p * 32 + 32] = ref[p, at : at + 32].astype(F32)


def spectra_kernel(got_ref, matrices, twiddles, signal_ref, filter_ref, scratch):
    rows_of(scratch, got_ref, 0)
    signal_ref[...] = spectrum(scratch, matrices, twiddles)
    rows_of(scratch, got_ref, 32)
    filter_ref[...] = spectrum(scratch, matrices, twiddles)


def conv_kernel(z_ref, signal_ref, filter_ref, before_ref, matrices, twiddles, out_ref, scratch):
    upper = z_ref[0] == 1
    cos_tw, sin_tw = twiddles[:, :128], twiddles[:, 128:]
    own, high = signal_ref[...], filter_ref[...]
    rows_of(scratch, before_ref, 0)
    old = jnp.where(upper, spectrum(scratch, matrices, twiddles), 0.0)
    rows_of(scratch, before_ref, 32)
    low = jnp.where(upper, spectrum(scratch, matrices, twiddles), high)
    odd = lax.broadcasted_iota(jnp.int32, (1024, 256), 0) & 1
    every = jnp.where(odd == 1, -low, low) + high
    own_r, own_i, old_r, old_i = own[:, :128], own[:, 128:], old[:, :128], old[:, 128:]
    low_r, low_i, all_r, all_i = low[:, :128], low[:, 128:], every[:, :128], every[:, 128:]
    real = own_r * low_r - own_i * low_i + old_r * all_r - old_i * all_i
    imag = own_r * low_i + own_i * low_r + old_r * all_i + old_i * all_r
    half = mm(jnp.concatenate([real.astype(BF16), imag.astype(BF16)], axis=1), matrices[512:768, :])
    parts = []
    for c in range(8):
        real, imag = half[c * 128 : c * 128 + 128, :128], half[c * 128 : c * 128 + 128, 128:]
        parts.append(
            jnp.concatenate(
                [(real * cos_tw - imag * sin_tw).astype(BF16), (imag * cos_tw + real * sin_tw).astype(BF16)],
                axis=0,
            )
        )
    result = mm(matrices[768:, :], jnp.concatenate(parts, axis=1))
    for c in range(8):
        scratch[pl.ds(c, 64, stride=8), :] = result[:, c * 128 : c * 128 + 128]
    for d in range(32):
        out_ref[d] = scratch[d * 16 : d * 16 + 16].astype(BF16)


def pack_kernel(conv_ref, terms_ref, out_ref):
    piece = sum(terms_ref[j].astype(F32) for j in range(8)).astype(BF16)
    for d in range(32):
        out_ref[d, :16] = conv_ref[d]
        out_ref[d, 16:] = piece


def first_kernel(core_ref, own_ref, got_ref, rows_ref, out_ref):
    core = core_ref[0]
    half = pl.ds(pl.multiple_of(core * 128, 128), 128)
    for g in range(3):
        own, got = own_ref[g], got_ref[g, :, half]
        out_ref[g * 128 : g * 128 + 64] = jnp.where(core == 0, own, got)
        out_ref[g * 128 + 64 : g * 128 + 128] = jnp.where(core == 0, got, own)
    out_ref[384:] = rows_ref[...]


def copies_kernel(first_ref, out_ref):
    for k in range(4):
        out_ref[k] = first_ref[:384]


def spread_kernel(z_ref, near_ref, first_ref, far_ref, out_hbm, sems):
    z = z_ref[0]
    copies = []
    for y in range(4):
        copies.append(pltpu.make_async_copy(near_ref, out_hbm.at[y, pl.ds(0, 1536)], sems.at[y, 0]))
        rows = pl.ds(384 + y * 32, 32)
        for k, (ref, place) in enumerate(((first_ref, z), (far_ref, 1 - z))):
            to = pl.ds(pl.multiple_of(1536 + place * 32, 32), 32)
            copies.append(pltpu.make_async_copy(ref.at[rows], out_hbm.at[y, to], sems.at[y, k + 1]))
    for copy in copies:
        copy.start()
    for copy in copies:
        copy.wait()


def last_kernel(scores_ref, out_ref):
    out_ref[...] = jnp.concatenate([scores_ref[k] for k in range(4)], axis=1)


def weight_block(ref, lead, row):
    return jnp.concatenate([ref[lead, row + 128 * g : row + 128 * g + 128, :] for g in range(3)], axis=1)


def scale_kernel(own_hbm, beside_hbm, scale_ref, tokens, sems):
    copies = []
    for part, ref in enumerate((own_hbm, beside_hbm)):
        for i in range(4):
            rows = pl.ds(i * 64, 64)
            copies.append(pltpu.make_async_copy(ref.at[rows], tokens.at[part, rows], sems.at[part, i]))
    for copy in copies:
        copy.start()
    for k in range(8):
        copies[k].wait()
        part, i = k // 4, k % 4
        for half in range(2):
            rows = slice(i * 64 + half * 32, i * 64 + half * 32 + 32)
            stream = tokens[part, rows, :].astype(F32)
            mean = jnp.mean(stream * stream, axis=1, keepdims=True)
            scale_ref[part, rows, :] = jnp.broadcast_to(lax.rsqrt(mean + NORM_EPS), (32, 128))


def near_kernel(
    at_ref, own_hbm, beside_hbm, gain_ref, own_taps, got_taps, near_ref, unembed_ref,
    gained_ref, out_ref, terms_ref, pieces_ref, tokens, taps, sems,
):
    core, start = at_ref[2], at_ref[3] * 2048
    gain = gain_ref[...]
    copies = []
    for part, ref in enumerate((own_hbm, beside_hbm)):
        for i in range(4):
            rows = pl.ds(i * 64, 64)
            copies.append(pltpu.make_async_copy(ref.at[rows], tokens.at[part, rows], sems.at[part, i]))
    copies.append(pltpu.make_async_copy(own_taps, taps.at[0], sems.at[2, 0]))
    copies.append(pltpu.make_async_copy(got_taps, taps.at[1], sems.at[2, 1]))
    for copy in copies:
        copy.start()

    blocks = []
    for plane in range(2):
        for y in range(4):
            block = near_ref[y, 1536 + plane * 32 : 1568 + plane * 32, :].astype(F32)
            blocks.append(jnp.concatenate([block[v * 8 : v * 8 + 8] for v in range(4)], axis=1))
    terms = mm(jnp.concatenate(blocks, axis=0).astype(BF16), unembed_ref[...])
    for j in range(8):
        parts = [terms[j * 8 : j * 8 + 8, v * 128 : v * 128 + 128] for v in range(4)]
        terms_ref[j] = jnp.concatenate(parts, axis=0).astype(BF16)

    for part in range(2):
        for i in range(4):
            copies[part * 4 + i].wait()
            rows = slice(i * 64, i * 64 + 64)
            gained_ref[part, rows, :] = tokens[part, rows, :] * gain
        total = jnp.zeros((256, 384), F32)
        for y in range(4):
            for x in (0, 2):
                left = gained_ref[part, :, pl.ds(pl.multiple_of(start + (y * 4 + x) * 128, 128), 256)]
                right = [weight_block(near_ref, y, x * 384), weight_block(near_ref, y, x * 384 + 384)]
                total += mm(left, jnp.concatenate(right, axis=0))
        out_ref[part] = total
    half = pl.ds(pl.multiple_of(core * 128, 128), 128)
    for part in range(2):
        copies[8 + part].wait()
        put_pieces(pieces_ref, 0, core if part == 0 else 1 - core, taps[part, :, half].astype(F32))


def put_pieces(ref, row, place, block):
    first, second = block[:128].T, block[128:].T
    for p in range(16):
        b = p * 8
        rows = jnp.concatenate([first[b : b + 8], second[b : b + 8]], axis=0).astype(BF16)
        ref[p, pl.ds(pl.multiple_of(row + place * 16, 16), 16), :] = rows


def proj_kernel(
    at_ref, gained_ref, near_ref, pieces_ref, scale_hbm, f0, f1, f2, f3, sig_ref, gate_ref, fars, scales, sems
):
    y_at, x_at, core = at_ref[0], at_ref[1], at_ref[2]
    start = 2048 - at_ref[3] * 2048
    copies = [pltpu.make_async_copy(f, fars.at[k], sems.at[k]) for k, f in enumerate((f0, f1, f2, f3))]
    copies.append(pltpu.make_async_copy(scale_hbm, scales, sems.at[4]))
    for copy in copies:
        copy.start()
    for part in range(2):
        total = near_ref[part]
        for step in range(4):
            if part == 0:
                copies[step].wait()
            x = lax.rem(x_at + 4 - step, 4)
            for k in (0, 2):
                starts = [start + (lax.rem(y_at + 4 - j, 4) * 4 + x) * 128 for j in (k, k + 1)]
                left = [gained_ref[part, :, pl.ds(pl.multiple_of(at, 128), 128)] for at in starts]
                right = [weight_block(fars.at[step], k, 0), weight_block(fars.at[step], k + 1, 0)]
                total += mm(jnp.concatenate(left, axis=1), jnp.concatenate(right, axis=0))
        if part == 0:
            copies[4].wait()
        scale = scales[part]
        proj = (total * jnp.concatenate([scale, scale, scale], axis=1)).astype(BF16).astype(F32)
        place = core if part == 0 else 1 - core
        put_pieces(sig_ref, 0, place, proj[:, 128:256] * proj[:, 256:])
        gate_ref[place, 0] = proj[:128, :128].T.astype(BF16)
        gate_ref[place, 1] = proj[128:, :128].T.astype(BF16)
    for p in range(16):
        sig_ref[p, 32:, :] = pieces_ref[p]


def mix_kernel(core_ref, got_ref, keep_ref, other_ref, base_ref, out_ref):
    core = core_ref[0]
    keep, other = keep_ref[...].astype(F32), other_ref[...].astype(F32)
    conv = got_ref[:, :16, :].astype(F32)
    for rb in range(2):
        total = base_ref[rb * 128 : rb * 128 + 128, :]
        for c in range(2):
            cube = jnp.concatenate([conv[b * 2 + c, rb * 8 : rb * 8 + 8] for b in range(16)], axis=0)
            gate = jnp.where(core == c, keep[rb], other[rb])
            mixed = (gate * cube).T.astype(BF16)
            weights = []
            for b in range(16):
                x, holder, y = (c * 16 + b) // 8, b % 8 // 4, b % 4
                piece = got_ref[(y * 4 + x) * 2 + holder, 16:, :].astype(F32)
                weights.append(jnp.concatenate([piece[v * 8 : v * 8 + 8] for v in range(4)], axis=1))
            total += mm(mixed, jnp.concatenate(weights, axis=0).astype(BF16))
        out_ref[rb * 128 : rb * 128 + 128, :] = total.astype(BF16)


def call(kernel, outs, specs, scratch, flops, args, mib=8, out_specs=None):
    if out_specs is None:
        out_specs = jax.tree.map(lambda _: pl.BlockSpec(memory_space=pltpu.VMEM), outs)
    return pl.pallas_call(
        kernel,
        out_shape=outs,
        in_specs=specs,
        out_specs=out_specs,
        scratch_shapes=scratch,
        compiler_params=pltpu.CompilerParams(vmem_limit_bytes=mib * 2**20),
        cost_estimate=pl.CostEstimate(flops=flops, bytes_accessed=4 * 2**20, transcendentals=0),
    )(*args)


def shape(dims, dtype):
    return jax.ShapeDtypeStruct(dims, dtype)


def by_position(own, other, place):
    return jnp.where(place == 0, jnp.stack([own, other]), jnp.stack([other, own]))


def spectra(got):
    return call(
        spectra_kernel,
        (shape((1024, 256), F32), shape((1024, 256), F32)),
        whole(3),
        [pltpu.VMEM((512, 128), F32)],
        4 * 10**8,
        (got, jnp.asarray(MATRICES, BF16), jnp.asarray(TWIDDLES, F32)),
    )


def convolve(z, signal, taps, before):
    return call(
        conv_kernel,
        shape((32, 16, 128), BF16),
        [SCALARS] + whole(5),
        [pltpu.VMEM((512, 128), F32)],
        6 * 10**8,
        (z, signal, taps, before, jnp.asarray(MATRICES, BF16), jnp.asarray(TWIDDLES, F32)),
        mib=16,
    )


def per_device(tokens_in, pre_gain, w_in, w_out, long_filter, w_unembed, target_ids, score_mask):
    ctx, tp = lax.axis_index("ctx"), lax.axis_index("tp")
    core, z = ctx % 2, ctx // 32
    z_at = z.reshape(1).astype(jnp.int32)

    core_at = core.reshape(1).astype(jnp.int32)
    w_in = w_in.transpose(1, 0, 2)
    keep = lax.dynamic_slice_in_dim(w_in, core * 128, 128, 2)
    rows = w_out.reshape(4, 8, 4, 128).transpose(0, 2, 1, 3).reshape(128, 128)
    first = call(
        first_kernel,
        shape((512, 128), BF16),
        [SCALARS] + whole(3),
        [],
        10**5,
        (core_at, keep, lax.ppermute(w_in, "ctx", PERM_CORE), rows),
    )
    near = call(copies_kernel, shape((4, 384, 128), BF16), whole(1), [], 10**5, (first,))
    beside = lax.ppermute(tokens_in, "ctx", PERM_CORE)
    near = lax.all_to_all(near, "ctx", 0, 0, axis_index_groups=GROUPS_X, tiled=True)
    far = lax.ppermute(first, "ctx", PERM_Z)

    along = far[:384]
    along = jnp.stack([along] + [lax.ppermute(along, "ctx", PERM_Y[k]) for k in (1, 2, 3)])
    near, along, far, taps = lax.optimization_barrier((near, along, far, long_filter))

    near = call(
        spread_kernel,
        shape((4, 1600, 128), BF16),
        [SCALARS] + whole(3),
        [pltpu.SemaphoreType.DMA((4, 3))],
        10**5,
        (z_at, near.reshape(1536, 128), first, far),
        out_specs=IN_HBM,
    )
    near = lax.all_to_all(near, "ctx", 0, 0, axis_index_groups=GROUPS_Y, tiled=True)
    far = along
    fars = [far] + [lax.ppermute(far, "ctx", PERM_X[k]) for k in (1, 2, 3)]
    taps_got = lax.ppermute(taps, "ctx", PERM_CORE)

    at = jnp.stack([(ctx // 8) % 4, (ctx // 2) % 4, core, z]).astype(jnp.int32)
    scale = call(
        scale_kernel,
        shape((2, 256, 128), F32),
        [IN_HBM, IN_HBM],
        [pltpu.VMEM((2, 256, 4096), BF16), pltpu.SemaphoreType.DMA((2, 4))],
        10**7,
        (tokens_in, beside),
    )
    gained, sums, terms, pieces = call(
        near_kernel,
        (
            shape((2, 256, 4096), BF16),
            shape((2, 256, 384), F32),
            shape((8, 32, 128), BF16),
            shape((16, 32, 128), BF16),
        ),
        [SCALARS, IN_HBM, IN_HBM] + whole(1) + [IN_HBM, IN_HBM] + whole(2),
        [pltpu.VMEM((2, 256, 4096), BF16), pltpu.VMEM((2, 256, 256), BF16), pltpu.SemaphoreType.DMA((3, 4))],
        8 * 10**8,
        (at, tokens_in, beside, pre_gain.reshape(1, 4096), taps, taps_got, near, w_unembed),
        mib=12,
    )
    signal, gate = call(
        proj_kernel,
        (shape((16, 64, 128), BF16), shape((2, 2, 128, 128), BF16)),
        [SCALARS] + whole(3) + [IN_HBM] * 5,
        [pltpu.VMEM((4, 4, 384, 128), BF16), pltpu.VMEM((2, 256, 128), F32), pltpu.SemaphoreType.DMA((5,))],
        8 * 10**8,
        (at, gained, sums, pieces, scale, *fars),
    )
    got = lax.all_to_all(signal, "ctx", 0, 0, axis_index_groups=GROUPS_CORE, tiled=True)
    before = lax.ppermute(got, "ctx", PERM_Z_UP)
    terms, _ = lax.optimization_barrier((terms, got))
    terms = lax.all_to_all(terms, "tp", 0, 0, tiled=True)
    gate_keep = lax.dynamic_index_in_dim(gate, core, 0, False)
    gate_got = lax.ppermute(lax.dynamic_index_in_dim(gate, 1 - core, 0, False), "ctx", PERM_CORE)

    conv = convolve(z_at, *spectra(got), before)
    conv = call(pack_kernel, shape((32, 48, 128), BF16), whole(2), [], 10**5, (conv, terms))
    conv = lax.all_to_all(conv, "ctx", 0, 0, axis_index_groups=GROUPS_PLANE, tiled=True)

    width = w_unembed.shape[0]
    base = mm(lax.dynamic_slice_in_dim(tokens_in, tp * width, width, 1), w_unembed)
    logits = call(
        mix_kernel,
        shape((256, 512), BF16),
        [SCALARS] + whole(4),
        [],
        10**8,
        (core_at, conv, gate_keep, gate_got, base),
    )
    logits = lax.all_to_all(logits.reshape(4, 64, 512), "tp", 0, 0, axis_index_groups=GROUPS_TP, tiled=True)
    logits = jnp.sum(logits.astype(F32), axis=0).astype(BF16)
    far = lax.ppermute(logits, "tp", [(i, i ^ 4) for i in range(8)])
    logits = logits.astype(F32) + far.astype(F32)

    row_top = jnp.max(logits, axis=1, keepdims=True)
    log_total = row_top[:, 0] + jnp.log(jnp.sum(jnp.exp(logits - row_top), axis=1))
    ids = lax.dynamic_slice_in_dim(target_ids, (tp % 4) * 64, 64, 0)
    mask = lax.dynamic_slice_in_dim(score_mask, (tp % 4) * 64, 64, 0)
    vocab_index = lax.broadcasted_iota(jnp.int32, (64, 512), 1)
    picked = jnp.sum(jnp.where(vocab_index == ids[:, None], logits, 0.0), axis=1)
    scores = (picked - log_total) * mask.astype(F32)
    scores = jnp.broadcast_to(scores[None, None, :], (4, 1, 64))
    scores = lax.all_to_all(scores, "tp", 0, 0, axis_index_groups=GROUPS_TP, tiled=True)
    return call(last_kernel, shape((1, 256), F32), whole(1), [], 10**3, (scores,)).reshape(256)


def solution(mesh):
    return jax.shard_map(
        per_device,
        mesh=mesh,
        in_specs=(
            P("ctx", None),
            P(),
            P("ctx", None, "tp"),
            P("ctx", "tp"),
            P("ctx", "tp"),
            P("tp", None),
            P("ctx"),
            P("ctx"),
        ),
        out_specs=P("ctx"),
        check_vma=False,
    )
```

```python
import math

import jax
import jax.numpy as jnp
import numpy as np
from jax import lax
from jax.experimental import pallas as pl
from jax.experimental.pallas import tpu as pltpu
from jax.sharding import PartitionSpec as P

NORM_EPS = 1e-05
F32 = jnp.float32
BF16 = jnp.bfloat16

COORDS = [(z, y, x, c) for z in range(2) for y in range(4) for x in range(4) for c in range(2)]


def ctx_id(z, y, x, c):
    return ((z * 4 + y) * 4 + x) * 2 + c


def ctx_perm(move):
    return [(ctx_id(*at), ctx_id(*move(*at))) for at in COORDS]


PERM_CORE = ctx_perm(lambda z, y, x, c: (z, y, x, 1 - c))
PERM_Z = ctx_perm(lambda z, y, x, c: (1 - z, y, x, c))
PERM_Z_UP = [(i, i + 32) for i in range(32)]
PERM_X = [ctx_perm(lambda z, y, x, c, k=k: (z, y, (x + k) % 4, c)) for k in range(4)]
PERM_Y = [ctx_perm(lambda z, y, x, c, k=k: (z, (y + k) % 4, x, c)) for k in range(4)]
GROUPS_X = [[ctx_id(z, y, x, c) for x in range(4)] for z in range(2) for y in range(4) for c in range(2)]
GROUPS_Y = [[ctx_id(z, y, x, c) for y in range(4)] for z in range(2) for x in range(4) for c in range(2)]
GROUPS_PLANE = [
    [ctx_id(z, y, x, c) for y in range(4) for x in range(4) for c in range(2)] for z in range(2)
]
GROUPS_CORE = [
    [ctx_id(z, y, x, c) for y in range(4) for x in range(4)] for z in range(2) for c in range(2)
]
GROUPS_TP = [[0, 1, 2, 3], [4, 5, 6, 7]]


def tables():
    index = np.arange(128)
    inner = 2.0 * math.pi * (np.outer(index, index) % 128) / 128
    outer = 2.0 * math.pi * np.outer(index, index) / 16384
    cos, sin = np.cos(inner), np.sin(inner)
    first = np.concatenate([cos[:, :64], -sin[:, :64]], axis=0)
    second = np.block([[cos, -sin], [sin, cos]])
    back = np.block([[cos, sin], [-sin, cos]])
    last = np.concatenate([cos[:64], -sin[:64]], axis=1) / 16384.0
    return (first, second, back, last, np.cos(outer), np.sin(outer))


FIRST, SECOND, BACK, LAST, COS_TW, SIN_TW = tables()
MATRICES = np.concatenate([np.pad(FIRST, ((0, 0), (0, 192))), SECOND, BACK, LAST])
TWIDDLES = np.concatenate([COS_TW, SIN_TW], axis=1)


def mm(left, right):
    return jnp.dot(left, right, preferred_element_type=F32)


def whole(count):
    return [pl.BlockSpec(memory_space=pltpu.VMEM)] * count


SCALARS = pl.BlockSpec(memory_space=pltpu.SMEM)
IN_HBM = pl.BlockSpec(memory_space=pltpu.HBM)


def spectrum(scratch, matrices, twiddles):
    cos_tw, sin_tw = twiddles[:, :128], twiddles[:, 128:]
    cube = jnp.concatenate([scratch[pl.ds(c, 64, stride=8), :] for c in range(8)], axis=1)
    step = mm(matrices[:256, :64], cube.astype(BF16))
    parts = []
    for c in range(8):
        real, imag = step[:128, c * 128 : c * 128 + 128], step[128:, c * 128 : c * 128 + 128]
        parts.append(
            jnp.concatenate(
                [(real * cos_tw + imag * sin_tw).astype(BF16), (imag * cos_tw - real * sin_tw).astype(BF16)],
                axis=1,
            )
        )
    return mm(jnp.concatenate(parts, axis=0), matrices[256:512, :])


def rows_of(scratch, ref, at):
    for p in range(16):
        scratch[p * 32 : p * 32 + 32] = ref[p, at : at + 32].astype(F32)


def spectra_kernel(got_ref, matrices, twiddles, signal_ref, filter_ref, scratch):
    rows_of(scratch, got_ref, 0)
    signal_ref[...] = spectrum(scratch, matrices, twiddles)
    rows_of(scratch, got_ref, 32)
    filter_ref[...] = spectrum(scratch, matrices, twiddles)


def conv_kernel(z_ref, signal_ref, filter_ref, before_ref, matrices, twiddles, out_ref, scratch):
    upper = z_ref[0] == 1
    cos_tw, sin_tw = twiddles[:, :128], twiddles[:, 128:]
    own, high = signal_ref[...], filter_ref[...]
    rows_of(scratch, before_ref, 0)
    old = jnp.where(upper, spectrum(scratch, matrices, twiddles), 0.0)
    rows_of(scratch, before_ref, 32)
    low = jnp.where(upper, spectrum(scratch, matrices, twiddles), high)
    odd = lax.broadcasted_iota(jnp.int32, (1024, 256), 0) & 1
    every = jnp.where(odd == 1, -low, low) + high
    own_r, own_i, old_r, old_i = own[:, :128], own[:, 128:], old[:, :128], old[:, 128:]
    low_r, low_i, all_r, all_i = low[:, :128], low[:, 128:], every[:, :128], every[:, 128:]
    real = own_r * low_r - own_i * low_i + old_r * all_r - old_i * all_i
    imag = own_r * low_i + own_i * low_r + old_r * all_i + old_i * all_r
    half = mm(jnp.concatenate([real.astype(BF16), imag.astype(BF16)], axis=1), matrices[512:768, :])
    parts = []
    for c in range(8):
        real, imag = half[c * 128 : c * 128 + 128, :128], half[c * 128 : c * 128 + 128, 128:]
        parts.append(
            jnp.concatenate(
                [(real * cos_tw - imag * sin_tw).astype(BF16), (imag * cos_tw + real * sin_tw).astype(BF16)],
                axis=0,
            )
        )
    result = mm(matrices[768:, :], jnp.concatenate(parts, axis=1))
    for c in range(8):
        scratch[pl.ds(c, 64, stride=8), :] = result[:, c * 128 : c * 128 + 128]
    for d in range(32):
        out_ref[d] = scratch[d * 16 : d * 16 + 16].astype(BF16)


def pack_kernel(conv_ref, terms_ref, out_ref):
    piece = sum(terms_ref[j].astype(F32) for j in range(8)).astype(BF16)
    for d in range(32):
        out_ref[d, :16] = conv_ref[d]
        out_ref[d, 16:] = piece


def first_kernel(core_ref, own_ref, got_ref, rows_ref, out_ref):
    core = core_ref[0]
    half = pl.ds(pl.multiple_of(core * 128, 128), 128)
    for g in range(3):
        own, got = own_ref[g], got_ref[g, :, half]
        out_ref[g * 128 : g * 128 + 64] = jnp.where(core == 0, own, got)
        out_ref[g * 128 + 64 : g * 128 + 128] = jnp.where(core == 0, got, own)
    out_ref[384:] = rows_ref[...]


def copies_kernel(first_ref, out_ref):
    for k in range(4):
        out_ref[k] = first_ref[:384]


def spread_kernel(z_ref, near_ref, first_ref, far_ref, out_hbm, sems):
    z = z_ref[0]
    copies = []
    for y in range(4):
        copies.append(pltpu.make_async_copy(near_ref, out_hbm.at[y, pl.ds(0, 1536)], sems.at[y, 0]))
        rows = pl.ds(384 + y * 32, 32)
        for k, (ref, place) in enumerate(((first_ref, z), (far_ref, 1 - z))):
            to = pl.ds(pl.multiple_of(1536 + place * 32, 32), 32)
            copies.append(pltpu.make_async_copy(ref.at[rows], out_hbm.at[y, to], sems.at[y, k + 1]))
    for copy in copies:
        copy.start()
    for copy in copies:
        copy.wait()


def last_kernel(scores_ref, out_ref):
    out_ref[...] = jnp.concatenate([scores_ref[k] for k in range(4)], axis=1)


def weight_block(ref, lead, row):
    return jnp.concatenate([ref[lead, row + 128 * g : row + 128 * g + 128, :] for g in range(3)], axis=1)


def near_kernel(
    at_ref, own_hbm, beside_hbm, gain_ref, own_taps, got_taps, near_ref, unembed_ref,
    gained_ref, scale_ref, out_ref, terms_ref, pieces_ref, tokens, taps, sems, spare,
):
    core, start = at_ref[2], at_ref[3] * 2048
    gain = gain_ref[...]
    copies = []
    for part, ref in enumerate((own_hbm, beside_hbm)):
        for i in range(4):
            rows = pl.ds(i * 64, 64)
            copies.append(pltpu.make_async_copy(ref.at[rows], tokens.at[part, rows], sems.at[part, i]))
    copies.append(pltpu.make_async_copy(own_taps, taps.at[0], sems.at[2, 0]))
    copies.append(pltpu.make_async_copy(got_taps, taps.at[1], sems.at[2, 1]))
    for copy in copies:
        copy.start()

    blocks = []
    for plane in range(2):
        for y in range(4):
            block = near_ref[y, 1536 + plane * 32 : 1568 + plane * 32, :].astype(F32)
            blocks.append(jnp.concatenate([block[v * 8 : v * 8 + 8] for v in range(4)], axis=1))
    terms = mm(jnp.concatenate(blocks, axis=0).astype(BF16), unembed_ref[...])
    for j in range(8):
        parts = [terms[j * 8 : j * 8 + 8, v * 128 : v * 128 + 128] for v in range(4)]
        terms_ref[j] = jnp.concatenate(parts, axis=0).astype(BF16)

    for part in range(2):
        for i in range(4):
            copies[part * 4 + i].wait()
            for half in range(2):
                rows = slice(i * 64 + half * 32, i * 64 + half * 32 + 32)
                block = tokens[part, rows, :]
                stream = block.astype(F32)
                mean = jnp.mean(stream * stream, axis=1, keepdims=True)
                scale_ref[part, rows, :] = jnp.broadcast_to(lax.rsqrt(mean + NORM_EPS), (32, 128))
                gained_ref[part, rows, :] = block * gain
        total = jnp.zeros((256, 384), F32)
        for y in range(4):
            for x in (0, 2):
                left = gained_ref[part, :, pl.ds(pl.multiple_of(start + (y * 4 + x) * 128, 128), 256)]
                right = [weight_block(near_ref, y, x * 384), weight_block(near_ref, y, x * 384 + 384)]
                total += mm(left, jnp.concatenate(right, axis=0))
        out_ref[part] = total
    half = pl.ds(pl.multiple_of(core * 128, 128), 128)
    for part in range(2):
        copies[8 + part].wait()
        put_pieces(pieces_ref, 0, core if part == 0 else 1 - core, taps[part, :, half].astype(F32))


def put_pieces(ref, row, place, block):
    first, second = block[:128].T, block[128:].T
    for p in range(16):
        b = p * 8
        rows = jnp.concatenate([first[b : b + 8], second[b : b + 8]], axis=0).astype(BF16)
        ref[p, pl.ds(pl.multiple_of(row + place * 16, 16), 16), :] = rows


def proj_kernel(at_ref, gained_ref, scale_ref, near_ref, pieces_ref, f0, f1, f2, f3, sig_ref, gate_ref, fars, sems):
    y_at, x_at, core = at_ref[0], at_ref[1], at_ref[2]
    start = 2048 - at_ref[3] * 2048
    copies = [pltpu.make_async_copy(f, fars.at[k], sems.at[k]) for k, f in enumerate((f0, f1, f2, f3))]
    for copy in copies:
        copy.start()
    for part in range(2):
        total = near_ref[part]
        for step in range(4):
            if part == 0:
                copies[step].wait()
            x = lax.rem(x_at + 4 - step, 4)
            for k in (0, 2):
                starts = [start + (lax.rem(y_at + 4 - j, 4) * 4 + x) * 128 for j in (k, k + 1)]
                left = [gained_ref[part, :, pl.ds(pl.multiple_of(at, 128), 128)] for at in starts]
                right = [weight_block(fars.at[step], k, 0), weight_block(fars.at[step], k + 1, 0)]
                total += mm(jnp.concatenate(left, axis=1), jnp.concatenate(right, axis=0))
        scale = scale_ref[part]
        proj = (total * jnp.concatenate([scale, scale, scale], axis=1)).astype(BF16).astype(F32)
        place = core if part == 0 else 1 - core
        put_pieces(sig_ref, 0, place, proj[:, 128:256] * proj[:, 256:])
        gate_ref[place, 0] = proj[:128, :128].T.astype(BF16)
        gate_ref[place, 1] = proj[128:, :128].T.astype(BF16)
    for p in range(16):
        sig_ref[p, 32:, :] = pieces_ref[p]


def mix_kernel(core_ref, got_ref, keep_ref, other_ref, base_ref, out_ref):
    core = core_ref[0]
    keep, other = keep_ref[...].astype(F32), other_ref[...].astype(F32)
    conv = got_ref[:, :16, :].astype(F32)
    for rb in range(2):
        total = base_ref[rb * 128 : rb * 128 + 128, :]
        for c in range(2):
            cube = jnp.concatenate([conv[b * 2 + c, rb * 8 : rb * 8 + 8] for b in range(16)], axis=0)
            gate = jnp.where(core == c, keep[rb], other[rb])
            mixed = (gate * cube).T.astype(BF16)
            weights = []
            for b in range(16):
                x, holder, y = (c * 16 + b) // 8, b % 8 // 4, b % 4
                piece = got_ref[(y * 4 + x) * 2 + holder, 16:, :].astype(F32)
                weights.append(jnp.concatenate([piece[v * 8 : v * 8 + 8] for v in range(4)], axis=1))
            total += mm(mixed, jnp.concatenate(weights, axis=0).astype(BF16))
        out_ref[rb * 128 : rb * 128 + 128, :] = total.astype(BF16)


def call(kernel, outs, specs, scratch, flops, args, mib=8, out_specs=None):
    if out_specs is None:
        out_specs = jax.tree.map(lambda _: pl.BlockSpec(memory_space=pltpu.VMEM), outs)
    return pl.pallas_call(
        kernel,
        out_shape=outs,
        in_specs=specs,
        out_specs=out_specs,
        scratch_shapes=scratch,
        compiler_params=pltpu.CompilerParams(vmem_limit_bytes=mib * 2**20),
        cost_estimate=pl.CostEstimate(flops=flops, bytes_accessed=4 * 2**20, transcendentals=0),
    )(*args)


def shape(dims, dtype):
    return jax.ShapeDtypeStruct(dims, dtype)


def by_position(own, other, place):
    return jnp.where(place == 0, jnp.stack([own, other]), jnp.stack([other, own]))


def spectra(got):
    return call(
        spectra_kernel,
        (shape((1024, 256), F32), shape((1024, 256), F32)),
        whole(3),
        [pltpu.VMEM((512, 128), F32)],
        4 * 10**8,
        (got, jnp.asarray(MATRICES, BF16), jnp.asarray(TWIDDLES, F32)),
    )


def convolve(z, signal, taps, before):
    return call(
        conv_kernel,
        shape((32, 16, 128), BF16),
        [SCALARS] + whole(5),
        [pltpu.VMEM((512, 128), F32)],
        6 * 10**8,
        (z, signal, taps, before, jnp.asarray(MATRICES, BF16), jnp.asarray(TWIDDLES, F32)),
        mib=16,
    )


def per_device(tokens_in, pre_gain, w_in, w_out, long_filter, w_unembed, target_ids, score_mask):
    ctx, tp = lax.axis_index("ctx"), lax.axis_index("tp")
    core, z = ctx % 2, ctx // 32
    z_at = z.reshape(1).astype(jnp.int32)

    core_at = core.reshape(1).astype(jnp.int32)
    w_in = w_in.transpose(1, 0, 2)
    keep = lax.dynamic_slice_in_dim(w_in, core * 128, 128, 2)
    rows = w_out.reshape(4, 8, 4, 128).transpose(0, 2, 1, 3).reshape(128, 128)
    first = call(
        first_kernel,
        shape((512, 128), BF16),
        [SCALARS] + whole(3),
        [],
        10**5,
        (core_at, keep, lax.ppermute(w_in, "ctx", PERM_CORE), rows),
    )
    near = call(copies_kernel, shape((4, 384, 128), BF16), whole(1), [], 10**5, (first,))
    beside = lax.ppermute(tokens_in, "ctx", PERM_CORE)
    near = lax.all_to_all(near, "ctx", 0, 0, axis_index_groups=GROUPS_X, tiled=True)
    far = lax.ppermute(first, "ctx", PERM_Z)

    along = far[:384]
    along = jnp.stack([along] + [lax.ppermute(along, "ctx", PERM_Y[k]) for k in (1, 2, 3)])
    near, along, far, taps = lax.optimization_barrier((near, along, far, long_filter))

    near = call(
        spread_kernel,
        shape((4, 1600, 128), BF16),
        [SCALARS] + whole(3),
        [pltpu.SemaphoreType.DMA((4, 3))],
        10**5,
        (z_at, near.reshape(1536, 128), first, far),
        out_specs=IN_HBM,
    )
    near = lax.all_to_all(near, "ctx", 0, 0, axis_index_groups=GROUPS_Y, tiled=True)
    far = along
    fars = [far] + [lax.ppermute(far, "ctx", PERM_X[k]) for k in (1, 2, 3)]
    taps_got = lax.ppermute(taps, "ctx", PERM_CORE)

    at = jnp.stack([(ctx // 8) % 4, (ctx // 2) % 4, core, z]).astype(jnp.int32)
    gained, scale, sums, terms, pieces = call(
        near_kernel,
        (
            shape((2, 256, 4096), BF16),
            shape((2, 256, 128), F32),
            shape((2, 256, 384), F32),
            shape((8, 32, 128), BF16),
            shape((16, 32, 128), BF16),
        ),
        [SCALARS, IN_HBM, IN_HBM] + whole(1) + [IN_HBM, IN_HBM] + whole(2),
        [
            pltpu.VMEM((2, 256, 4096), BF16),
            pltpu.VMEM((2, 256, 256), BF16),
            pltpu.SemaphoreType.DMA((3, 4)),
            pltpu.VMEM((40, 2048, 256), BF16),
        ],
        8 * 10**8,
        (at, tokens_in, beside, pre_gain.reshape(1, 4096), taps, taps_got, near, w_unembed),
        mib=56,
    )
    signal, gate = call(
        proj_kernel,
        (shape((16, 64, 128), BF16), shape((2, 2, 128, 128), BF16)),
        [SCALARS] + whole(4) + [IN_HBM] * 4,
        [pltpu.VMEM((4, 4, 384, 128), BF16), pltpu.SemaphoreType.DMA((4,))],
        8 * 10**8,
        (at, gained, scale, sums, pieces, *fars),
    )
    got = lax.all_to_all(signal, "ctx", 0, 0, axis_index_groups=GROUPS_CORE, tiled=True)
    before = lax.ppermute(got, "ctx", PERM_Z_UP)
    terms, _ = lax.optimization_barrier((terms, got))
    terms = lax.all_to_all(terms, "tp", 0, 0, tiled=True)
    gate_keep = lax.dynamic_index_in_dim(gate, core, 0, False)
    gate_got = lax.ppermute(lax.dynamic_index_in_dim(gate, 1 - core, 0, False), "ctx", PERM_CORE)

    conv = convolve(z_at, *spectra(got), before)
    conv = call(pack_kernel, shape((32, 48, 128), BF16), whole(2), [], 10**5, (conv, terms))
    conv = lax.all_to_all(conv, "ctx", 0, 0, axis_index_groups=GROUPS_PLANE, tiled=True)

    width = w_unembed.shape[0]
    base = mm(lax.dynamic_slice_in_dim(tokens_in, tp * width, width, 1), w_unembed)
    logits = call(
        mix_kernel,
        shape((256, 512), BF16),
        [SCALARS] + whole(4),
        [],
        10**8,
        (core_at, conv, gate_keep, gate_got, base),
    )
    logits = lax.all_to_all(logits.reshape(4, 64, 512), "tp", 0, 0, axis_index_groups=GROUPS_TP, tiled=True)
    logits = jnp.sum(logits.astype(F32), axis=0).astype(BF16)
    far = lax.ppermute(logits, "tp", [(i, i ^ 4) for i in range(8)])
    logits = logits.astype(F32) + far.astype(F32)

    row_top = jnp.max(logits, axis=1, keepdims=True)
    log_total = row_top[:, 0] + jnp.log(jnp.sum(jnp.exp(logits - row_top), axis=1))
    ids = lax.dynamic_slice_in_dim(target_ids, (tp % 4) * 64, 64, 0)
    mask = lax.dynamic_slice_in_dim(score_mask, (tp % 4) * 64, 64, 0)
    vocab_index = lax.broadcasted_iota(jnp.int32, (64, 512), 1)
    picked = jnp.sum(jnp.where(vocab_index == ids[:, None], logits, 0.0), axis=1)
    scores = (picked - log_total) * mask.astype(F32)
    scores = jnp.broadcast_to(scores[None, None, :], (4, 1, 64))
    scores = lax.all_to_all(scores, "tp", 0, 0, axis_index_groups=GROUPS_TP, tiled=True)
    return call(last_kernel, shape((1, 256), F32), whole(1), [], 10**3, (scores,)).reshape(256)


def solution(mesh):
    return jax.shard_map(
        per_device,
        mesh=mesh,
        in_specs=(
            P("ctx", None),
            P(),
            P("ctx", None, "tp"),
            P("ctx", "tp"),
            P("ctx", "tp"),
            P("tp", None),
            P("ctx"),
            P("ctx"),
        ),
        out_specs=P("ctx"),
        check_vma=False,
    )
```
